256 devices in a mesh: pool: 2 (over y_hi), band: 8 (over x, core), fft: 16 (over z, y_lo).
Axes of the slice: x: 4, y: 4 (y_hi: 2, y_lo: 2; y = y_hi * 2 + y_lo), z: 8, core: 2. Of those that a mesh axis runs over, the one named last changes fastest.
Arguments:
- coefficients: float32 [2, 32, 2, 221184], P('pool', 'band', None, 'fft'), may hold values from -6 to 6
- occupation: float32 [2, 32], P('pool', 'band'), may hold values from 0.1 to 2
- kpoint_weight: int32 [2], replicated, may hold values from 1 to 8
- stick_cell: int32 [2304], P('fft'), may hold values from 0 to 9215, as said below
- species: int32 [128], replicated, may hold values from 0 to 2
- positions: float32 [3, 128], replicated, may hold values from 0 to 1
- amplitude: float32 [3], replicated, may hold values from 30 to 300
- core_width: float32 [3], replicated, may hold values from 0.3 to 1
Outputs:
- forces: float32 [3, 128], replicated
The draws below stay inside these ranges and needn't reach their ends.
Inputs may be any that keep to these rules, and one draw needn't show every extreme that they name: `stick_cell`: the entries are distinct cells. Every cell with 16 m_x^2 + 16 m_y^2 <= 96^2 is among them, the others lie outside that disk; each block of 144 entries (one index of fft) holds the disk's cells to within one of an equal share.
All inputs are finite; a program needn't handle non-finite values.
Results may differ from the reference program's by a relative error of at most 0.0003.
Values sent between devices are 32-bit elements; how exact they have to be, the bound alone decides.
No kernel may reach another device: no remote copies, remote signals or barrier semaphores. Data moves between devices by JAX's collectives and lax.ppermute only.
A program may use at most 128 MiB of HBM per device.

```python
import math
import jax
import jax.numpy as jnp
from jax import lax

NX = 96
NY = 96
NZ = 192
ZSPAN = 96
STICKS = 2304
STICKS_DEV = 144
SPECIES = 3
ATOMS = 128
KPTS = 2
BANDS = 32
NGRID = 1769472
N_FFT = 16


def draw_stick_cell(key, part):
    key = jax.random.fold_in(key, 7)
    cells = jnp.arange(NX * NY, dtype=jnp.int32)
    freq_x = (cells // NY + NX // 2) % NX - NX // 2
    freq_y = (cells % NY + NY // 2) % NY - NY // 2
    outside = (16 * (freq_x * freq_x + freq_y * freq_y) > NX * NX).astype(jnp.int32)
    ranking = jax.random.permutation(key, NX * NY).astype(jnp.int32)
    order = jnp.argsort(outside * (NX * NY) + ranking, stable=True)
    chosen = cells[order][:STICKS]
    return chosen.reshape(STICKS_DEV, N_FFT).T.reshape(-1).astype(jnp.int32)


def plant(values, stream_key, least, high):
    spot = [jax.random.randint(jax.random.fold_in(stream_key, axis), (), 0, length) for axis, length in enumerate(values.shape)]
    main_axis = values.shape.index(max(values.shape))
    next_to = spot[:main_axis] + [(spot[main_axis] + 1) % values.shape[main_axis]] + spot[main_axis + 1:]
    return values.at[tuple(spot)].set(least).at[tuple(next_to)].set(high)


def shard_levels(own_key, extent, cuts, low, top_value):
    factor_of, own = 1.0, jax.random.fold_in(own_key, 6)
    for axis_at, blocks in cuts:
        steps = jnp.exp(jax.random.uniform(jax.random.fold_in(own, axis_at), (blocks,), jnp.float32, low / len(cuts), top_value / len(cuts)))
        factor_of = factor_of * jnp.repeat(steps, extent[axis_at] // blocks).reshape([-1 if axis == axis_at else 1 for axis in range(len(extent))])
    return factor_of


def bell_draw(own_key, dims, deviation, reach, cuts=(), kind=jnp.bfloat16):
    loudness = shard_levels(own_key, dims, cuts, -0.22, 0.18) if cuts else 1.0
    values = jax.random.normal(own_key, dims, jnp.float32) * deviation * loudness
    return jnp.minimum(jnp.maximum(values, -reach), reach).astype(kind)


def setup_inputs(seed: int = 0) -> dict:
    seeds = jax.random.split(jax.random.key(seed), 9)
    coefficients = bell_draw(seeds[0], (KPTS, BANDS, 2, STICKS * ZSPAN), 0.7, 6.0, ((0, 2), (1, 8), (3, 16)), jnp.float32)
    occupation = jnp.clip(0.1 + 1.9 * jax.random.uniform(seeds[1], (KPTS, BANDS), jnp.float32) ** shard_levels(seeds[1], (KPTS, BANDS), ((0, 2), (1, 8)), -0.2, 0.2), 0.1, 2.0)
    kpoint_weight = jax.random.randint(seeds[2], (KPTS,), 1, 9).astype(jnp.int32)
    stick_cell = draw_stick_cell(jax.random.fold_in(seeds[8], 71), 0)
    species = plant(jax.random.randint(seeds[4], (ATOMS,), 0, SPECIES), jax.random.fold_in(seeds[4], 1), 0, SPECIES - 1).astype(jnp.int32)
    positions = jnp.clip(jax.random.uniform(seeds[5], (3, ATOMS), jnp.float32, 0.0, 1.0), 0.0, 1.0)
    amplitude = jnp.clip(jnp.exp(jax.random.uniform(seeds[6], (SPECIES,), jnp.float32, math.log(30.0), math.log(300.0))), 30.0, 300.0)
    core_width = jnp.clip(jnp.exp(jax.random.uniform(seeds[7], (SPECIES,), jnp.float32, math.log(0.3), math.log(1.0))), 0.3, 1.0)
    return {"coefficients": coefficients, "occupation": occupation, "kpoint_weight": kpoint_weight, "stick_cell": stick_cell, "species": species, "positions": positions, "amplitude": amplitude, "core_width": core_width}


screen = 0.25

def signed_freq(offsets, length):
    return (offsets + length // 2) % length - length // 2

def sphere_mask(cells):
    freq_x = signed_freq(cells // NY, NX)
    freq_y = signed_freq(cells % NY, NY)
    freq_z = jnp.arange(ZSPAN, dtype=jnp.int32) - NZ // 4
    level = 16 * (freq_x * freq_x + freq_y * freq_y)[:, None] + 4 * (freq_z * freq_z)[None, :]
    return (level <= NX * NX).astype(jnp.float32)

def force_block(real_part, imag_part, z_start, x_start, y_start, species, positions, amplitude, core_width):
    rows_z, rows_x, rows_y = real_part.shape
    two_pi = 2.0 * math.pi
    freq_z = signed_freq(z_start + jnp.arange(rows_z, dtype=jnp.int32), NZ).astype(jnp.float32)
    freq_x = signed_freq(x_start + jnp.arange(rows_x, dtype=jnp.int32), NX).astype(jnp.float32)
    freq_y = signed_freq(y_start + jnp.arange(rows_y, dtype=jnp.int32), NY).astype(jnp.float32)
    vec_z = jnp.broadcast_to((two_pi / NZ * freq_z)[:, None, None], real_part.shape)
    vec_x = jnp.broadcast_to((two_pi / NX * freq_x)[None, :, None], real_part.shape)
    vec_y = jnp.broadcast_to((two_pi / NY * freq_y)[None, None, :], real_part.shape)
    squared = vec_x * vec_x + vec_y * vec_y + vec_z * vec_z
    components = jnp.stack([vec_x, vec_y, vec_z])
    angle_z = two_pi * freq_z[:, None] * positions[2][None, :]
    cos_z = jnp.cos(angle_z)
    sin_z = jnp.sin(angle_z)
    angle_xy = two_pi * (freq_x[:, None, None] * positions[0][None, None, :] + freq_y[None, :, None] * positions[1][None, None, :])
    angle_xy = angle_xy.reshape(rows_x * rows_y, -1)
    cos_xy = jnp.cos(angle_xy)
    sin_xy = jnp.sin(angle_xy)
    kind_ids = jnp.arange(amplitude.shape[0], dtype=jnp.int32)
    selector = (species[None, :] == kind_ids[:, None]).astype(jnp.float32)
    result = jnp.zeros((3, positions.shape[1]), jnp.float32)
    highest = lax.Precision.HIGHEST
    for kind_index in range(amplitude.shape[0]):
        potential = -amplitude[kind_index] * jnp.exp(-0.5 * squared * core_width[kind_index] * core_width[kind_index]) / (squared + screen)
        weighted = components * potential[None]
        field_re = (weighted * real_part[None]).reshape(3, rows_z, rows_x * rows_y)
        field_im = (weighted * imag_part[None]).reshape(3, rows_z, rows_x * rows_y)
        sum_re = jnp.einsum('czq,za->cqa', field_re, cos_z, precision=highest) - jnp.einsum('czq,za->cqa', field_im, sin_z, precision=highest)
        sum_im = jnp.einsum('czq,za->cqa', field_re, sin_z, precision=highest) + jnp.einsum('czq,za->cqa', field_im, cos_z, precision=highest)
        partial_force = jnp.einsum('cqa,qa->ca', sum_re, sin_xy, precision=highest) + jnp.einsum('cqa,qa->ca', sum_im, cos_xy, precision=highest)
        result = result + selector[kind_index][None, :] * partial_force
    return result

def reference(coefficients, occupation, kpoint_weight, stick_cell, species, positions, amplitude, core_width):
    weights = kpoint_weight.astype(jnp.float32) / jnp.sum(kpoint_weight).astype(jnp.float32)
    factors = (weights[:, None] * occupation).reshape(-1) / BANDS
    flattened = coefficients.reshape(KPTS * BANDS, 2, STICKS, ZSPAN)
    inside = sphere_mask(stick_cell)
    z_cells = (jnp.arange(ZSPAN, dtype=jnp.int32) - NZ // 4) % NZ
    normaliser = 4.0 * math.sqrt(NGRID)

    def make_box(values):
        columns = jnp.zeros((STICKS, NZ), jnp.float32).at[:, z_cells].set(values * inside)
        return jnp.zeros((NX * NY, NZ), jnp.float32).at[stick_cell].set(columns).reshape(NX, NY, NZ)

    def add_band(total, band_item):
        values, factor = band_item
        wavefunction = jnp.fft.ifftn(make_box(values[0]) + 1j * make_box(values[1])) * normaliser
        return (total + factor * (wavefunction.real * wavefunction.real + wavefunction.imag * wavefunction.imag), None)
    density, _ = lax.scan(add_band, jnp.zeros((NX, NY, NZ), jnp.float32), (flattened, factors))
    spectrum = jnp.transpose(jnp.fft.fftn(density) / NGRID, (2, 0, 1))
    return force_block(spectrum.real, spectrum.imag, 0, 0, 0, species, positions, amplitude, core_width)
```

```python
import math

import jax
import jax.numpy as jnp
import numpy as np
from jax import lax
from jax.sharding import PartitionSpec as P

NX = 96
NY = 96
NZ = 192
ZSPAN = 96
NGRID = 1769472
HALF = 24
SIDE = 49
LANES = 128
PLANES = 12
HIGH = lax.Precision.HIGH
HIGHEST = lax.Precision.HIGHEST
screen = 0.25


def signed_freq(offsets, length):
    return (offsets + length // 2) % length - length // 2


def trig(rows, columns, length):
    angles = 2.0 * np.pi / length * (np.outer(rows, columns) % length)
    return np.cos(angles).astype(np.float32), np.sin(angles).astype(np.float32)


def z_table():
    cosine, sine = trig(np.arange(NZ), np.arange(ZSPAN) - NZ // 4, NZ)
    real_rows = np.stack([cosine, -sine], 1)
    imag_rows = np.stack([sine, cosine], 1)
    table = np.stack([real_rows, imag_rows], 1)
    return table.reshape(16, PLANES, 2, 2, ZSPAN)


def box_sum(values):
    spread = jnp.broadcast_to(values[None], (16,) + values.shape)
    total = jnp.sum(lax.all_to_all(spread, ("pool", "band"), 0, 0, tiled=True), axis=0)
    spread = jnp.broadcast_to(total[None], (16,) + values.shape)
    return jnp.sum(lax.all_to_all(spread, "fft", 0, 0, tiled=True), axis=0)


def shards(
    coefficients, occupation, kpoint_weight, stick_cell, species, positions, amplitude, core_width
):
    sticks = stick_cell.shape[0]
    shaped = coefficients[0].reshape(4, 2, sticks, ZSPAN)
    freq_x = signed_freq(stick_cell // NY, NX)
    freq_y = signed_freq(stick_cell % NY, NY)
    freq_z = jnp.arange(ZSPAN, dtype=jnp.int32) - NZ // 4
    disk = 16 * (freq_x * freq_x + freq_y * freq_y)
    level = disk[:, None] + 4 * (freq_z * freq_z)[None, :]
    masked = jnp.where(level <= NX * NX, shaped, 0.0)
    chosen = disk <= NX * NX
    before = jnp.arange(sticks)[:, None] < jnp.arange(sticks)[None, :]
    rank = jnp.sum(jnp.where(before & chosen[:, None], 1, 0), axis=0)
    lane = jnp.arange(LANES, dtype=jnp.int32)
    pick = (chosen[:, None] & (rank[:, None] == lane[None, :])).astype(jnp.float32)
    place = ((freq_x + HALF) * SIDE + freq_y + HALF + 1).astype(jnp.float32)
    ids = jnp.sum(pick * place[:, None], axis=0) - 1.0
    packed = jnp.einsum("bcst,sj->bctj", masked, pick, precision=HIGH)
    planes = jnp.einsum("dpoct,bctj->dobpj", z_table(), packed, precision=HIGH)
    planes = planes.reshape(16, 96, LANES)
    payload = jnp.concatenate([planes, jnp.broadcast_to(ids[None, None], (16, 8, LANES))], 1)
    received = lax.all_to_all(payload, "fft", split_axis=0, concat_axis=0, tiled=True)
    place = received[:, 96, :].astype(jnp.int32)
    spots = (place[:, :, None] == jnp.arange(SIDE * SIDE)[None, None, :]).astype(jnp.float32)
    grid = jnp.einsum("srj,sjc->rc", received[:, :96], spots, precision=HIGH)
    grid = grid.reshape(2, 48, SIDE, SIDE)
    cosine, sine = trig(np.arange(96), np.arange(SIDE) - HALF, 96)
    even = jnp.einsum("rgxm,ym->rgxy", grid, cosine, precision=HIGH)
    odd = jnp.einsum("rgxm,ym->rgxy", grid, sine, precision=HIGH)
    real_part, imag_part = even[0] - odd[1], even[1] + odd[0]
    wave_re = jnp.einsum("gmy,xm->gxy", real_part, cosine, precision=HIGH) - jnp.einsum(
        "gmy,xm->gxy", imag_part, sine, precision=HIGH
    )
    wave_im = jnp.einsum("gmy,xm->gxy", real_part, sine, precision=HIGH) + jnp.einsum(
        "gmy,xm->gxy", imag_part, cosine, precision=HIGH
    )
    pool_weight = lax.dynamic_index_in_dim(
        kpoint_weight, lax.axis_index("pool"), keepdims=False
    ).astype(jnp.float32) / jnp.sum(kpoint_weight).astype(jnp.float32)
    factors = pool_weight * occupation[0] * (16.0 / NGRID / 32.0 / NGRID)
    squares = (wave_re * wave_re + wave_im * wave_im).reshape(4, PLANES, 96, 96)
    density = jnp.sum(factors[:, None, None, None] * squares, axis=0)

    wide_cos, wide_sin = trig(np.arange(SIDE), np.arange(96), 96)
    both = np.concatenate([wide_cos, wide_sin])
    forward = jnp.einsum("pxy,hy->pxh", density, both, precision=HIGH)
    forward = jnp.einsum("pxh,gx->pgh", forward, both, precision=HIGH)
    start = lax.axis_index("fft") * PLANES
    steps = (jnp.arange(ZSPAN)[:, None] * (start + jnp.arange(PLANES))[None, :]) % NZ
    angles = 2.0 * math.pi / NZ * steps.astype(jnp.float32)
    spectrum = jnp.einsum(
        "tkp,pgh->tkgh", jnp.stack([jnp.cos(angles), jnp.sin(angles)]), forward, precision=HIGH
    )
    gx = (2.0 * np.pi / 96 * np.arange(SIDE)).astype(np.float32)
    gz = (2.0 * np.pi / NZ * np.arange(ZSPAN)).astype(np.float32)
    gx2 = np.tile(gx * gx, 2)
    squared = gx2[None, :, None] + gx2[None, None, :] + (gz * gz)[:, None, None]
    weighted = spectrum * (1.0 / (squared + screen)).astype(np.float32)[None]
    kinds = species[None, :] == jnp.arange(3, dtype=jnp.int32)[:, None]
    width = jnp.sum(jnp.where(kinds, core_width[:, None], 0.0), axis=0)
    strength = jnp.sum(jnp.where(kinds, amplitude[:, None], 0.0), axis=0)
    fold = np.full(SIDE, 2.0, np.float32)
    fold[0] = fold[48] = 1.0
    fold_z = np.full(ZSPAN, 2.0, np.float32)
    fold_z[0] = 1.0

    def tables(where, waves, counts):
        turns = jnp.arange(waves.shape[0], dtype=jnp.float32)[:, None] * where[None, :]
        phase = 2.0 * math.pi * (turns - jnp.round(turns))
        scale = counts[:, None] * jnp.exp(-0.5 * (waves * waves)[:, None] * (width * width)[None])
        cosine, sine = scale * jnp.cos(phase), scale * jnp.sin(phase)
        slope = waves[:, None]
        return jnp.stack([cosine, sine]), jnp.stack([slope * sine, -slope * cosine])

    x_cos, x_sin = tables(positions[0], gx, fold)
    y_cos, y_sin = tables(positions[1], gx, fold)
    z_cos, z_sin = tables(positions[2], gz, fold_z)
    plain = jnp.einsum("tkgh,tka->gha", weighted, z_cos, precision=HIGH)
    sloped = jnp.einsum("tkgh,tka->gha", weighted, z_sin, precision=HIGH)
    x_cos, x_sin = x_cos.reshape(98, 1, -1), x_sin.reshape(98, 1, -1)
    y_cos, y_sin = y_cos.reshape(98, -1), y_sin.reshape(98, -1)
    force_x = jnp.sum(jnp.sum(plain * x_sin, axis=0) * y_cos, axis=0)
    force_y = jnp.sum(jnp.sum(plain * x_cos, axis=0) * y_sin, axis=0)
    force_z = jnp.sum(jnp.sum(sloped * x_cos, axis=0) * y_cos, axis=0)
    partial_force = -strength[None] * jnp.stack([force_x, force_y, force_z])
    return box_sum(partial_force)


def solution(mesh):
    placed = (P("pool", "band", None, "fft"), P("pool", "band"), P(), P("fft"), P(), P(), P(), P())
    return jax.shard_map(shards, mesh=mesh, in_specs=placed, out_specs=P(), check_vma=False)
```

```python
import math

import jax
import jax.numpy as jnp
import numpy as np
from jax import lax
from jax.experimental import pallas as pl
from jax.experimental.pallas import tpu as pltpu
from jax.sharding import PartitionSpec as P

NX = 96
NY = 96
NZ = 192
ZSPAN = 96
NGRID = 1769472
HALF = 24
SIDE = 49
LANES = 128
PLANES = 12
SLOTS = 25
SIDE_ROWS = SLOTS * 16
HIGH = lax.Precision.HIGH
screen = 0.25
VMEM = pl.BlockSpec(memory_space=pltpu.VMEM)
SMEM = pl.BlockSpec(memory_space=pltpu.SMEM)


def signed_freq(offsets, length):
    return (offsets + length // 2) % length - length // 2


def trig(rows, columns, length):
    angles = 2.0 * np.pi / length * (np.outer(rows, columns) % length)
    return np.cos(angles).astype(np.float32), np.sin(angles).astype(np.float32)


def halves(values):
    high = values.astype(jnp.bfloat16)
    return high, (values - high.astype(jnp.float32)).astype(jnp.bfloat16)


def table_halves(values):
    high = lax.reduce_precision(values, 8, 7)
    return high.astype(jnp.bfloat16), (values - high).astype(jnp.bfloat16)


def np_halves(values):
    high = values.astype(jnp.bfloat16)
    return high, (values - high.astype(np.float32)).astype(jnp.bfloat16)


def mm(left, right):
    return jnp.dot(left, right, preferred_element_type=jnp.float32)


def z_table():
    cosine, sine = trig(np.arange(NZ), np.arange(ZSPAN) - NZ // 4, NZ)
    real_rows = np.stack([cosine, -sine], 1)
    imag_rows = np.stack([sine, cosine], 1)
    table = np.stack([real_rows, imag_rows], 1)
    return table.reshape(16, PLANES, 2, 2, ZSPAN)


def inverse_y_tables():
    cosine, sine = trig(np.arange(SIDE) - HALF, np.arange(96), 96)
    both = np.zeros((SIDE, 256), np.float32)
    both[:, :96], both[:, 128:224] = cosine, sine
    high, low = np_halves(both)
    first = np.zeros((2, 256, 256), high.dtype)
    second = np.zeros((2, 128, 256), high.dtype)
    for half in range(2):
        for part in range(2):
            first[half, 128 * part + 64 * half : 128 * part + 64 * half + SIDE] = high
        second[half, 64 * half : 64 * half + SIDE] = low
    return first, second


def inverse_x_table():
    cosine, sine = trig(np.arange(96), np.arange(SIDE) - HALF, 96)
    both = np.zeros((192, 64), np.float32)
    both[:96, :SIDE], both[96:, :SIDE] = cosine, sine
    high, low = np_halves(both)
    return np.concatenate([high, high, low], 1)


def forward_y_tables():
    cosine, sine = trig(np.arange(96), np.arange(SIDE), 96)
    both = np.zeros((128, 128), np.float32)
    both[:96, :SIDE], both[:96, 64 : 64 + SIDE] = cosine, sine
    high, low = np_halves(both)
    return np.concatenate([high, high], 0), low


def forward_x_tables():
    cosine, sine = trig(np.arange(50), np.arange(96), 96)
    cosine[SIDE:], sine[SIDE:] = 0.0, 0.0
    result = []
    for core in range(2):
        both = np.zeros((128, 96), np.float32)
        for index, rows in enumerate((core, 1 - core)):
            both[64 * index : 64 * index + SLOTS] = cosine[rows::2]
            both[64 * index + 32 : 64 * index + 32 + SLOTS] = sine[rows::2]
        high, low = np_halves(both)
        result.append(np.concatenate([high, high, low], 1))
    return np.stack(result)


def density_kernel(
    factors, recv, inv_y1, inv_y2, inv_x, fwd_y1, fwd_y2, fwd_x, own, other, parts, ids, held_re, held_im
):
    for source in range(16):
        high, low = halves(recv[source, :96, :])
        parts[:96, source * LANES : (source + 1) * LANES] = high
        parts[96:, source * LANES : (source + 1) * LANES] = low
        ids[:, source * LANES : (source + 1) * LANES] = recv[source, 96:104, :].astype(jnp.int32)
    blank = jnp.zeros((48, 128), jnp.float32)
    for row in range(52, 64):
        held_re[pl.ds(row, 48, stride=64), :] = blank
        held_im[pl.ds(row, 48, stride=64), :] = blank

    def place(tile, _):
        cells = lax.broadcasted_iota(jnp.int32, (256, 256), 0) + tile * 256
        total = jnp.zeros((192, 256), jnp.float32)
        for block in range(8):
            span = slice(block * 256, block * 256 + 256)
            spots = (cells == ids[0:1, span]).astype(jnp.float32).astype(jnp.bfloat16)
            total = total + lax.dot_general(
                parts[:, span], spots, (((1,), (1,)), ((), ())), preferred_element_type=jnp.float32
            )
        grid = total[:96] + total[96:]
        high, low = halves(grid)
        for column in range(4):
            pair = slice((column // 2) * 128, (column // 2) * 128 + 128)
            both = jnp.concatenate([high[:, pair], low[:, pair]], 1)
            out = mm(both, inv_y1[column % 2]) + mm(high[:, pair], inv_y2[column % 2])
            rows = pl.ds(tile * 4 + column, 48, stride=64)
            held_re[rows, :] = out[:48, :128] - out[48:, 128:]
            held_im[rows, :] = out[48:, :128] + out[:48, 128:]
        return 0

    lax.fori_loop(0, 13, place, 0)
    clear = jnp.zeros((2 * SLOTS, 128), jnp.float32)
    for row in range(PLANES, 16):
        own[pl.ds(row, 2 * SLOTS, stride=16), :] = clear
        other[pl.ds(row, 2 * SLOTS, stride=16), :] = clear

    def plane_step(plane, _):
        density = jnp.zeros((96, 128), jnp.float32)
        for band in range(4):
            start = pl.multiple_of((band * PLANES + plane) * 64, 64)
            rows = pl.ds(start, 64)
            high, low = halves(jnp.concatenate([held_re[rows, :], held_im[rows, :]], 1))
            out = mm(inv_x[...], jnp.concatenate([high, low, high], 0))
            wave_re = out[:96, :128] - out[96:, 128:]
            wave_im = out[96:, :128] + out[:96, 128:]
            density = density + factors[band] * (wave_re * wave_re + wave_im * wave_im)
        high, low = halves(density)
        rows = mm(jnp.concatenate([high, low], 1), fwd_y1[...]) + mm(high, fwd_y2[...])
        high, low = halves(rows)
        out = mm(fwd_x[...], jnp.concatenate([high, low, high], 0))
        first, second = pl.ds(plane, SLOTS, stride=16), pl.ds(plane + SIDE_ROWS, SLOTS, stride=16)
        own[first, :] = out[0:SLOTS]
        own[second, :] = out[32 : 32 + SLOTS]
        other[first, :] = out[64 : 64 + SLOTS]
        other[second, :] = out[96 : 96 + SLOTS]
        return 0

    lax.fori_loop(0, PLANES, plane_step, 0)


def force_kernel(gx2, own, arrived, base, wave_z, atom_z, x_all, y_cos, y_sin, strength, out, acc, turn):
    acc[...] = jnp.zeros_like(acc)
    turn[...] = x_all[...]

    def step(slot, _):
        start = pl.multiple_of(slot * 16, 16)
        first, second = pl.ds(start, 16), pl.ds(start + SIDE_ROWS, 16)
        pair = [own[first, :] + arrived[first, :], own[second, :] + arrived[second, :]]
        high, low = halves(jnp.concatenate(pair, 1))
        raw = mm(wave_z[...], jnp.concatenate([high, low, high], 0))
        weight = 1.0 / (base[...] + gx2[slot])
        weight = jnp.concatenate([weight, weight], 1)
        weight = jnp.concatenate([weight, weight], 0)
        high, low = halves(raw * weight)
        both = mm(atom_z[...], jnp.concatenate([high, low, high], 0))
        table = turn[...]
        xc_c, xc_s = table[:, 0:1], table[:, 32:33]
        xs_c, xs_s = table[:, 64:65], table[:, 96:97]
        plain_c, plain_s = both[:128, :128], both[:128, 128:]
        acc[0] += xs_c * plain_c + xs_s * plain_s
        acc[1] += xc_c * plain_c + xc_s * plain_s
        acc[2] += xc_c * both[128:, :128] + xc_s * both[128:, 128:]
        turn[...] = pltpu.roll(table, 127, 1)
        return 0

    lax.fori_loop(0, SLOTS, step, 0)
    parts = [acc[0] * y_cos[...], acc[1] * y_sin[...], acc[2] * y_cos[...]]
    rows = [-strength[...] * jnp.sum(part.T, axis=0, keepdims=True) for part in parts]
    block = jnp.concatenate(rows + [jnp.zeros((5, 128), jnp.float32)], 0)
    for index in range(16):
        out[index] = block


def shards(
    coefficients, occupation, kpoint_weight, stick_cell, species, positions, amplitude, core_width
):
    sticks = stick_cell.shape[0]
    shaped = coefficients[0].reshape(4, 2, sticks, ZSPAN)
    freq_x = signed_freq(stick_cell // NY, NX)
    freq_y = signed_freq(stick_cell % NY, NY)
    freq_z = jnp.arange(ZSPAN, dtype=jnp.int32) - NZ // 4
    disk = 16 * (freq_x * freq_x + freq_y * freq_y)
    level = disk[:, None] + 4 * (freq_z * freq_z)[None, :]
    masked = jnp.where(level <= NX * NX, shaped, 0.0)
    chosen = disk <= NX * NX
    before = jnp.arange(sticks)[:, None] < jnp.arange(sticks)[None, :]
    rank = jnp.sum(jnp.where(before & chosen[:, None], 1, 0), axis=0)
    lane = jnp.arange(LANES, dtype=jnp.int32)
    pick = (chosen[:, None] & (rank[:, None] == lane[None, :])).astype(jnp.float32)
    place = ((freq_x + HALF) * 64 + freq_y + HALF + 1).astype(jnp.float32)
    ids = jnp.sum(pick * place[:, None], axis=0) - 1.0
    packed = jnp.einsum("bcst,sj->bctj", masked, pick, precision=HIGH)
    planes = jnp.einsum("dpoct,bctj->dobpj", z_table(), packed, precision=HIGH)
    planes = planes.reshape(16, 96, LANES)
    payload = jnp.concatenate([planes, jnp.broadcast_to(ids[None, None], (16, 8, LANES))], 1)
    received = lax.all_to_all(payload, "fft", split_axis=0, concat_axis=0, tiled=True)

    core = lax.axis_index("band") % 2
    pool_weight = lax.dynamic_index_in_dim(
        kpoint_weight, lax.axis_index("pool"), keepdims=False
    ).astype(jnp.float32) / jnp.sum(kpoint_weight).astype(jnp.float32)
    factors = pool_weight * occupation[0] * (16.0 / NGRID / 32.0 / NGRID)
    inv_y1, inv_y2 = inverse_y_tables()
    fwd_y1, fwd_y2 = forward_y_tables()
    fwd_x = lax.dynamic_index_in_dim(jnp.asarray(forward_x_tables()), core, keepdims=False)
    halves_shape = jax.ShapeDtypeStruct((2 * SIDE_ROWS, 128), jnp.float32)
    own, other = pl.pallas_call(
        density_kernel,
        out_shape=(halves_shape, halves_shape),
        in_specs=[SMEM] + [VMEM] * 7,
        out_specs=(VMEM, VMEM),
        scratch_shapes=[
            pltpu.VMEM((192, 2048), jnp.bfloat16),
            pltpu.VMEM((8, 2048), jnp.int32),
            pltpu.VMEM((48 * 64, 128), jnp.float32),
            pltpu.VMEM((48 * 64, 128), jnp.float32),
        ],
        compiler_params=pltpu.CompilerParams(vmem_limit_bytes=40 * 1024 * 1024),
        name="density",
    )(factors, received, inv_y1, inv_y2, inverse_x_table(), fwd_y1, fwd_y2, fwd_x)
    swap = [(index, index ^ 1) for index in range(8)]
    arrived = lax.ppermute(other, "band", swap)

    start = lax.axis_index("fft") * PLANES
    steps = (jnp.arange(ZSPAN)[:, None] * (start + jnp.arange(PLANES))[None, :]) % NZ
    angles = 2.0 * math.pi / NZ * steps.astype(jnp.float32)
    turned = jnp.pad(jnp.concatenate([jnp.cos(angles), jnp.sin(angles)], 0), ((0, 0), (0, 4)))
    high, low = table_halves(turned)
    wave_z = jnp.concatenate([high, high, low], 1)
    kinds = species[None, :] == jnp.arange(3, dtype=jnp.int32)[:, None]
    width = jnp.sum(jnp.where(kinds, core_width[:, None], 0.0), axis=0)
    strength = jnp.sum(jnp.where(kinds, amplitude[:, None], 0.0), axis=0)

    def tables(where, order, unit, counts):
        waves = unit * order
        turns = where[:, None] * order[None, :]
        phase = 2.0 * math.pi * (turns - jnp.round(turns))
        scale = counts[None, :] * jnp.exp(-0.5 * (width * width)[:, None] * (waves * waves)[None])
        cosine, sine = scale * jnp.cos(phase), scale * jnp.sin(phase)
        slope = waves[None, :]
        return cosine, sine, slope * sine, -slope * cosine

    hx = 2.0 * jnp.arange(32, dtype=jnp.float32) + core.astype(jnp.float32)
    unit = 2.0 * math.pi / 96
    count_x = jnp.where(hx > 48.0, 0.0, jnp.where((hx == 0.0) | (hx == 48.0), 1.0, 2.0))
    x_all = jnp.concatenate(tables(positions[0], hx, unit, count_x), 1)
    hy = jnp.arange(64, dtype=jnp.float32)
    count_y = jnp.where(hy > 48.0, 0.0, jnp.where((hy == 0.0) | (hy == 48.0), 1.0, 2.0))
    y_parts = tables(positions[1], hy, unit, count_y)
    y_cos = jnp.concatenate(y_parts[:2], 1)
    y_sin = jnp.concatenate(y_parts[2:], 1)
    hz = jnp.arange(ZSPAN, dtype=jnp.float32)
    z_parts = tables(positions[2], hz, 2.0 * math.pi / NZ, jnp.where(hz == 0.0, 1.0, 2.0))
    z_rows = jnp.concatenate(
        [jnp.concatenate(z_parts[:2], 1), jnp.concatenate(z_parts[2:], 1)], 0
    )
    high, low = table_halves(z_rows)
    atom_z = jnp.concatenate([high, high, low], 1)
    gy = np.tile(2.0 * np.pi / 96 * np.arange(64), 2)
    gz = 2.0 * np.pi / NZ * np.arange(ZSPAN)
    base = (gy[None, :] ** 2 + gz[:, None] ** 2 + screen).astype(np.float32)
    gx2 = (unit * hx) * (unit * hx)
    spread = pl.pallas_call(
        force_kernel,
        out_shape=jax.ShapeDtypeStruct((16, 8, LANES), jnp.float32),
        in_specs=[SMEM] + [VMEM] * 9,
        out_specs=VMEM,
        scratch_shapes=[
            pltpu.VMEM((3, 128, 128), jnp.float32),
            pltpu.VMEM((128, 128), jnp.float32),
        ],
        compiler_params=pltpu.CompilerParams(vmem_limit_bytes=40 * 1024 * 1024),
        name="force",
    )(gx2, own, arrived, base, wave_z, atom_z, x_all, y_cos, y_sin, strength[None])
    total = jnp.sum(lax.all_to_all(spread, ("pool", "band"), 0, 0, tiled=True), axis=0)
    spread = jnp.broadcast_to(total[None], (16, 8, LANES))
    total = jnp.sum(lax.all_to_all(spread, "fft", 0, 0, tiled=True), axis=0)
    return total[:3]


def solution(mesh):
    placed = (P("pool", "band", None, "fft"), P("pool", "band"), P(), P("fft"), P(), P(), P(), P())
    return jax.shard_map(shards, mesh=mesh, in_specs=placed, out_specs=P(), check_vma=False)
```

```python
import math

import jax
import jax.numpy as jnp
import numpy as np
from jax import lax
from jax.experimental import pallas as pl
from jax.experimental.pallas import tpu as pltpu
from jax.sharding import PartitionSpec as P

NX = 96
NY = 96
NZ = 192
ZSPAN = 96
NGRID = 1769472
HALF = 24
SIDE = 49
LANES = 128
PLANES = 12
SLOTS = 25
SIDE_ROWS = SLOTS * 16
STICK_LIMIT = 113
SPARE_ROW = SIDE * 64
HIGH = lax.Precision.HIGH
screen = 0.25
VMEM = pl.BlockSpec(memory_space=pltpu.VMEM)
SMEM = pl.BlockSpec(memory_space=pltpu.SMEM)


def signed_freq(offsets, length):
    return (offsets + length // 2) % length - length // 2


def trig(rows, columns, length):
    angles = 2.0 * np.pi / length * (np.outer(rows, columns) % length)
    return np.cos(angles).astype(np.float32), np.sin(angles).astype(np.float32)


def halves(values):
    high = values.astype(jnp.bfloat16)
    return high, (values - high.astype(jnp.float32)).astype(jnp.bfloat16)


def table_halves(values):
    high = lax.reduce_precision(values, 8, 7)
    return high.astype(jnp.bfloat16), (values - high).astype(jnp.bfloat16)


def np_halves(values):
    high = values.astype(jnp.bfloat16)
    return high, (values - high.astype(np.float32)).astype(jnp.bfloat16)


def mm(left, right):
    return jnp.dot(left, right, preferred_element_type=jnp.float32)


def z_table():
    cosine, sine = trig(np.arange(NZ), np.arange(ZSPAN) - NZ // 4, NZ)
    real_rows = np.stack([cosine, -sine], 1)
    imag_rows = np.stack([sine, cosine], 1)
    table = np.stack([real_rows, imag_rows], 1)
    return table.reshape(16, PLANES, 2, 2, ZSPAN)


def inverse_y_tables():
    cosine, sine = trig(np.arange(SIDE) - HALF, np.arange(96), 96)
    both = np.zeros((SIDE, 256), np.float32)
    both[:, :96], both[:, 128:224] = cosine, sine
    high, low = np_halves(both)
    table = np.zeros((2, 256, 256), high.dtype)
    for half in range(2):
        for part in range(2):
            table[half, 64 * part : 64 * part + SIDE] = high
        table[half, 128 + 64 * half : 128 + 64 * half + SIDE] = low
    return table


def inverse_x_table():
    cosine, sine = trig(np.arange(96), np.arange(SIDE) - HALF, 96)
    both = np.zeros((192, 64), np.float32)
    both[:96, :SIDE], both[96:, :SIDE] = cosine, sine
    high, low = np_halves(both)
    return np.concatenate([high, high, low], 1)


def forward_y_tables():
    cosine, sine = trig(np.arange(96), np.arange(SIDE), 96)
    both = np.zeros((128, 128), np.float32)
    both[:96, :SIDE], both[:96, 64 : 64 + SIDE] = cosine, sine
    high, low = np_halves(both)
    return np.concatenate([high, high], 0), low


def forward_x_tables():
    cosine, sine = trig(np.arange(50), np.arange(96), 96)
    cosine[SIDE:], sine[SIDE:] = 0.0, 0.0
    result = []
    for core in range(2):
        both = np.zeros((128, 96), np.float32)
        for index, rows in enumerate((core, 1 - core)):
            both[64 * index : 64 * index + SLOTS] = cosine[rows::2]
            both[64 * index + 32 : 64 * index + 32 + SLOTS] = sine[rows::2]
        high, low = np_halves(both)
        result.append(np.concatenate([high, high, low], 1))
    return np.stack(result)


def density_kernel(
    factors,
    recv,
    inv_y,
    inv_x,
    fwd_y1,
    fwd_y2,
    fwd_x,
    own,
    other,
    columns,
    grid,
    held_re,
    held_im,
    density,
    ids_vector,
    ids,
    arrival,
):
    for source in range(16):
        ids_vector[source : source + 1, :] = recv[source, 96:97, :].astype(jnp.int32)
    to_scalars = pltpu.make_async_copy(ids_vector, ids, arrival)
    to_scalars.start()
    pad = jnp.zeros((32, LANES), jnp.float32)
    for source in range(16):
        columns[source] = jnp.concatenate([recv[source, :96, :], pad], 0).T
    blank = jnp.zeros((48, 128), jnp.float32)
    for row in range(52, 64):
        held_re[pl.ds(row, 48, stride=64), :] = blank
        held_im[pl.ds(row, 48, stride=64), :] = blank
    grid[...] = jnp.zeros_like(grid)
    to_scalars.wait()

    def put(source, _):
        for stick in range(STICK_LIMIT):
            grid[pl.ds(ids[source, stick], 1), :] = columns[source, stick : stick + 1, :]
        return 0

    lax.fori_loop(0, 16, put, 0)
    lower = lax.broadcasted_iota(jnp.int32, (96, 128), 1) < 64

    def place(tile, _):
        for pair in range(2):
            start = pl.multiple_of(tile * 256 + pair * 128, 128)
            rows = grid[pl.ds(start, 128), :].T[:96]
            high = rows.astype(jnp.bfloat16).astype(jnp.float32)
            low = pltpu.roll(rows - high, 64, 1)
            for half in range(2):
                mixed = jnp.where(lower, low, high) if half else jnp.where(lower, high, low)
                both = jnp.concatenate([mixed, high], 1).astype(jnp.bfloat16)
                out = mm(both, inv_y[half])
                rows_to = pl.ds(tile * 4 + pair * 2 + half, 48, stride=64)
                held_re[rows_to, :] = out[:48, :128] - out[48:, 128:]
                held_im[rows_to, :] = out[48:, :128] + out[:48, 128:]
        return 0

    lax.fori_loop(0, 13, place, 0)
    clear = jnp.zeros((2 * SLOTS, 128), jnp.float32)
    for row in range(PLANES, 16):
        own[pl.ds(row, 2 * SLOTS, stride=16), :] = clear
        other[pl.ds(row, 2 * SLOTS, stride=16), :] = clear

    def waves(plane, _):
        total = jnp.zeros((96, 128), jnp.float32)
        for band in range(4):
            start = pl.multiple_of((band * PLANES + plane) * 64, 64)
            rows = pl.ds(start, 64)
            high, low = halves(jnp.concatenate([held_re[rows, :], held_im[rows, :]], 1))
            out = mm(inv_x[...], jnp.concatenate([high, low, high], 0))
            wave_re = out[:96, :128] - out[96:, 128:]
            wave_im = out[96:, :128] + out[:96, 128:]
            total = total + factors[band] * (wave_re * wave_re + wave_im * wave_im)
        density[pl.ds(pl.multiple_of(plane * 96, 96), 96), :] = total
        return 0

    lax.fori_loop(0, PLANES, waves, 0, unroll=2)

    def forward(group, _):
        start = pl.multiple_of(group * 384, 384)
        high, low = halves(density[pl.ds(start, 384), :])
        rows = mm(jnp.concatenate([high, low], 1), fwd_y1[...]) + mm(high, fwd_y2[...])
        high, low = halves(rows)
        for pair in range(2):
            first, second = slice(pair * 192, pair * 192 + 96), slice(pair * 192 + 96, pair * 192 + 192)
            wide_high = jnp.concatenate([high[first], high[second]], 1)
            wide_low = jnp.concatenate([low[first], low[second]], 1)
            out = mm(fwd_x[...], jnp.concatenate([wide_high, wide_low, wide_high], 0))
            for member in range(2):
                plane = group * 4 + pair * 2 + member
                lanes = slice(member * 128, member * 128 + 128)
                cosine = pl.ds(plane, SLOTS, stride=16)
                sine = pl.ds(plane + SIDE_ROWS, SLOTS, stride=16)
                own[cosine, :] = out[0:SLOTS, lanes]
                own[sine, :] = out[32 : 32 + SLOTS, lanes]
                other[cosine, :] = out[64 : 64 + SLOTS, lanes]
                other[sine, :] = out[96 : 96 + SLOTS, lanes]
        return 0

    lax.fori_loop(0, 3, forward, 0)


def force_kernel(gx2, own, arrived, base, wave_z, atom_z, x_all, y_cos, y_sin, strength, out, acc, turn):
    acc[...] = jnp.zeros_like(acc)
    turn[...] = x_all[...]

    def step(slot, _):
        start = pl.multiple_of(slot * 16, 16)
        first, second = pl.ds(start, 16), pl.ds(start + SIDE_ROWS, 16)
        pair = [own[first, :] + arrived[first, :], own[second, :] + arrived[second, :]]
        high, low = halves(jnp.concatenate(pair, 1))
        raw = mm(wave_z[...], jnp.concatenate([high, low, high], 0))
        weight = 1.0 / (base[...] + gx2[slot])
        weight = jnp.concatenate([weight, weight], 1)
        weight = jnp.concatenate([weight, weight], 0)
        high, low = halves(raw * weight)
        both = mm(atom_z[...], jnp.concatenate([high, low, high], 0))
        table = turn[...]
        xc_c, xc_s = table[:, 0:1], table[:, 32:33]
        xs_c, xs_s = table[:, 64:65], table[:, 96:97]
        plain_c, plain_s = both[:128, :128], both[:128, 128:]
        acc[0] += xs_c * plain_c + xs_s * plain_s
        acc[1] += xc_c * plain_c + xc_s * plain_s
        acc[2] += xc_c * both[128:, :128] + xc_s * both[128:, 128:]
        turn[...] = pltpu.roll(table, 127, 1)
        return 0

    lax.fori_loop(0, SLOTS, step, 0, unroll=5)
    parts = [acc[0] * y_cos[...], acc[1] * y_sin[...], acc[2] * y_cos[...]]
    rows = [-strength[...] * jnp.sum(part.T, axis=0, keepdims=True) for part in parts]
    block = jnp.concatenate(rows + [jnp.zeros((5, 128), jnp.float32)], 0)
    for index in range(16):
        out[index] = block


def shards(
    coefficients, occupation, kpoint_weight, stick_cell, species, positions, amplitude, core_width
):
    sticks = stick_cell.shape[0]
    shaped = coefficients[0].reshape(4, 2, sticks, ZSPAN)
    freq_x = signed_freq(stick_cell // NY, NX)
    freq_y = signed_freq(stick_cell % NY, NY)
    freq_z = jnp.arange(ZSPAN, dtype=jnp.int32) - NZ // 4
    disk = 16 * (freq_x * freq_x + freq_y * freq_y)
    level = disk[:, None] + 4 * (freq_z * freq_z)[None, :]
    masked = jnp.where(level <= NX * NX, shaped, 0.0)
    chosen = disk <= NX * NX
    before = jnp.arange(sticks)[:, None] < jnp.arange(sticks)[None, :]
    rank = jnp.sum(jnp.where(before & chosen[:, None], 1, 0), axis=0)
    lane = jnp.arange(LANES, dtype=jnp.int32)
    pick = (chosen[:, None] & (rank[:, None] == lane[None, :])).astype(jnp.float32)
    place = ((freq_x + HALF) * 64 + freq_y + HALF - SPARE_ROW).astype(jnp.float32)
    ids = jnp.sum(pick * place[:, None], axis=0) + float(SPARE_ROW)
    packed = jnp.einsum("bcst,sj->bctj", masked, pick, precision=HIGH)
    planes = jnp.einsum("dpoct,bctj->dobpj", z_table(), packed, precision=HIGH)
    planes = planes.reshape(16, 96, LANES)
    payload = jnp.concatenate([planes, jnp.broadcast_to(ids[None, None], (16, 8, LANES))], 1)
    received = lax.all_to_all(payload, "fft", split_axis=0, concat_axis=0, tiled=True)

    core = lax.axis_index("band") % 2
    pool_weight = lax.dynamic_index_in_dim(
        kpoint_weight, lax.axis_index("pool"), keepdims=False
    ).astype(jnp.float32) / jnp.sum(kpoint_weight).astype(jnp.float32)
    factors = pool_weight * occupation[0] * (16.0 / NGRID / 32.0 / NGRID)
    fwd_y1, fwd_y2 = forward_y_tables()
    fwd_x = lax.dynamic_index_in_dim(jnp.asarray(forward_x_tables()), core, keepdims=False)
    halves_shape = jax.ShapeDtypeStruct((2 * SIDE_ROWS, 128), jnp.float32)
    own, other = pl.pallas_call(
        density_kernel,
        out_shape=(halves_shape, halves_shape),
        in_specs=[SMEM] + [VMEM] * 6,
        out_specs=(VMEM, VMEM),
        scratch_shapes=[
            pltpu.VMEM((16, LANES, LANES), jnp.float32),
            pltpu.VMEM((52 * 64, LANES), jnp.float32),
            pltpu.VMEM((48 * 64, LANES), jnp.float32),
            pltpu.VMEM((48 * 64, LANES), jnp.float32),
            pltpu.VMEM((PLANES * 96, LANES), jnp.float32),
            pltpu.VMEM((16, LANES), jnp.int32),
            pltpu.SMEM((16, LANES), jnp.int32),
            pltpu.SemaphoreType.DMA,
        ],
        compiler_params=pltpu.CompilerParams(vmem_limit_bytes=40 * 1024 * 1024),
        name="density",
    )(factors, received, inverse_y_tables(), inverse_x_table(), fwd_y1, fwd_y2, fwd_x)
    swap = [(index, index ^ 1) for index in range(8)]
    arrived = lax.ppermute(other, "band", swap)

    start = lax.axis_index("fft") * PLANES
    steps = (jnp.arange(ZSPAN)[:, None] * (start + jnp.arange(PLANES))[None, :]) % NZ
    angles = 2.0 * math.pi / NZ * steps.astype(jnp.float32)
    turned = jnp.pad(jnp.concatenate([jnp.cos(angles), jnp.sin(angles)], 0), ((0, 0), (0, 4)))
    high, low = table_halves(turned)
    wave_z = jnp.concatenate([high, high, low], 1)
    kinds = species[None, :] == jnp.arange(3, dtype=jnp.int32)[:, None]
    width = jnp.sum(jnp.where(kinds, core_width[:, None], 0.0), axis=0)
    strength = jnp.sum(jnp.where(kinds, amplitude[:, None], 0.0), axis=0)

    def tables(where, order, unit, counts):
        waves = unit * order
        turns = where[:, None] * order[None, :]
        phase = 2.0 * math.pi * (turns - jnp.round(turns))
        scale = counts[None, :] * jnp.exp(-0.5 * (width * width)[:, None] * (waves * waves)[None])
        cosine, sine = scale * jnp.cos(phase), scale * jnp.sin(phase)
        slope = waves[None, :]
        return cosine, sine, slope * sine, -slope * cosine

    hx = 2.0 * jnp.arange(32, dtype=jnp.float32) + core.astype(jnp.float32)
    unit = 2.0 * math.pi / 96
    count_x = jnp.where(hx > 48.0, 0.0, jnp.where((hx == 0.0) | (hx == 48.0), 1.0, 2.0))
    x_all = jnp.concatenate(tables(positions[0], hx, unit, count_x), 1)
    hy = jnp.arange(64, dtype=jnp.float32)
    count_y = jnp.where(hy > 48.0, 0.0, jnp.where((hy == 0.0) | (hy == 48.0), 1.0, 2.0))
    y_parts = tables(positions[1], hy, unit, count_y)
    y_cos = jnp.concatenate(y_parts[:2], 1)
    y_sin = jnp.concatenate(y_parts[2:], 1)
    hz = jnp.arange(ZSPAN, dtype=jnp.float32)
    z_parts = tables(positions[2], hz, 2.0 * math.pi / NZ, jnp.where(hz == 0.0, 1.0, 2.0))
    z_rows = jnp.concatenate(
        [jnp.concatenate(z_parts[:2], 1), jnp.concatenate(z_parts[2:], 1)], 0
    )
    high, low = table_halves(z_rows)
    atom_z = jnp.concatenate([high, high, low], 1)
    gy = np.tile(2.0 * np.pi / 96 * np.arange(64), 2)
    gz = 2.0 * np.pi / NZ * np.arange(ZSPAN)
    base = (gy[None, :] ** 2 + gz[:, None] ** 2 + screen).astype(np.float32)
    gx2 = (unit * hx) * (unit * hx)
    spread = pl.pallas_call(
        force_kernel,
        out_shape=jax.ShapeDtypeStruct((16, 8, LANES), jnp.float32),
        in_specs=[SMEM] + [VMEM] * 9,
        out_specs=VMEM,
        scratch_shapes=[
            pltpu.VMEM((3, 128, 128), jnp.float32),
            pltpu.VMEM((128, 128), jnp.float32),
        ],
        compiler_params=pltpu.CompilerParams(vmem_limit_bytes=40 * 1024 * 1024),
        name="force",
    )(gx2, own, arrived, base, wave_z, atom_z, x_all, y_cos, y_sin, strength[None])
    total = jnp.sum(lax.all_to_all(spread, ("pool", "band"), 0, 0, tiled=True), axis=0)
    spread = jnp.broadcast_to(total[None], (16, 8, LANES))
    total = jnp.sum(lax.all_to_all(spread, "fft", 0, 0, tiled=True), axis=0)
    return total[:3]


def solution(mesh):
    placed = (P("pool", "band", None, "fft"), P("pool", "band"), P(), P("fft"), P(), P(), P(), P())
    return jax.shard_map(shards, mesh=mesh, in_specs=placed, out_specs=P(), check_vma=False)
```

```python
import math

import jax
import jax.numpy as jnp
import numpy as np
from jax import lax
from jax.experimental import pallas as pl
from jax.experimental.pallas import tpu as pltpu
from jax.sharding import PartitionSpec as P

NX = 96
NY = 96
NZ = 192
ZSPAN = 96
NGRID = 1769472
HALF = 24
SIDE = 49
LANES = 128
PLANES = 12
SLOTS = 25
SIDE_ROWS = SLOTS * 16
STICK_LIMIT = 113
SPARE = 15
ROWS = 88
NEAR = 80
HELD = 72
GROUPS = 36
SPARE_ROW = SIDE * 64
HIGH = lax.Precision.HIGH
screen = 0.25
AXES = ("pool", "band", "fft")
VMEM = pl.BlockSpec(memory_space=pltpu.VMEM)
SMEM = pl.BlockSpec(memory_space=pltpu.SMEM)


def signed_freq(offsets, length):
    return (offsets + length // 2) % length - length // 2


def trig(rows, columns, length):
    angles = 2.0 * np.pi / length * (np.outer(rows, columns) % length)
    return np.cos(angles).astype(np.float32), np.sin(angles).astype(np.float32)


def reduce_groups():
    ranks = np.arange(256).reshape(2, 4, 2, 8, 2)
    across = ranks.transpose(3, 2, 0, 4, 1).reshape(16, 16)
    along = ranks.transpose(0, 4, 1, 3, 2).reshape(16, 16)
    return across.tolist(), along.tolist()


def halves(values):
    high = values.astype(jnp.bfloat16)
    return high, (values - high.astype(jnp.float32)).astype(jnp.bfloat16)


def table_halves(values):
    high = lax.reduce_precision(values, 8, 7)
    return high.astype(jnp.bfloat16), (values - high).astype(jnp.bfloat16)


def np_halves(values):
    high = values.astype(jnp.bfloat16)
    return high, (values - high.astype(np.float32)).astype(jnp.bfloat16)


def mm(left, right):
    return jnp.dot(left, right, preferred_element_type=jnp.float32)


def z_table():
    both = np.zeros((2, NZ, LANES), np.float32)
    both[:, :, :ZSPAN] = trig(np.arange(NZ), np.arange(ZSPAN) - NZ // 4, NZ)
    return np.concatenate(np_halves(both.reshape(2 * NZ, LANES)), 1)


def inverse_y_tables():
    cosine, sine = trig(np.arange(SIDE) - HALF, np.arange(96), 96)
    both = np.zeros((SIDE, 256), np.float32)
    both[:, :96], both[:, 128:224] = cosine, sine
    high, low = np_halves(both)
    table = np.zeros((2, 256, 256), high.dtype)
    for half in range(2):
        for part in range(2):
            table[half, 64 * part : 64 * part + SIDE] = high
        table[half, 128 + 64 * half : 128 + 64 * half + SIDE] = low
    return table


def inverse_x_table():
    cosine, sine = trig(np.arange(96), np.arange(SIDE) - HALF, 96)
    both = np.zeros((192, 64), np.float32)
    both[:96, :SIDE], both[96:, :SIDE] = cosine, sine
    high, low = np_halves(both)
    return np.concatenate([high, high, low], 1)


def forward_y_tables():
    cosine, sine = trig(np.arange(96), np.arange(SIDE), 96)
    both = np.zeros((128, 128), np.float32)
    both[:96, :SIDE], both[:96, 64 : 64 + SIDE] = cosine, sine
    high, low = np_halves(both)
    return np.concatenate([high, high], 0), low


def forward_x_tables():
    cosine, sine = trig(np.arange(50), np.arange(96), 96)
    cosine[SIDE:], sine[SIDE:] = 0.0, 0.0
    result = []
    for core in range(2):
        both = np.zeros((128, 96), np.float32)
        for index, rows in enumerate((core, 1 - core)):
            both[64 * index : 64 * index + SLOTS] = cosine[rows::2]
            both[64 * index + 32 : 64 * index + 32 + SLOTS] = sine[rows::2]
        high, low = np_halves(both)
        result.append(np.concatenate([high, high, low], 1))
    return np.stack(result)


def mm_t(left, right):
    return lax.dot_general(
        left, right, (((1,), (1,)), ((), ())), preferred_element_type=jnp.float32
    )


def pieces(held, dest, tile):
    found = []
    for row in range(tile * 8, tile * 8 + 8, 4):
        start = (row // 48) * 192 + dest * PLANES + row % 12
        found.append(held[(row % 48) // 12, start : start + 4, :])
    return jnp.concatenate(found, 0)


def send_kernel(coefs, mask, pick, ids, table, out, held, rows):
    for chunk in range(3 * GROUPS):
        piece = coefs[:, :, chunk * LANES : (chunk + 1) * LANES]
        for band in range(4):
            for part in range(2):
                start = (band * 2 + part) * 40 + chunk // 3
                rows[chunk % 3, start : start + 1, :] = piece[band, part : part + 1]
    high_table = table[:, :LANES]
    wide_table = jnp.concatenate([high_table, high_table], 1)
    low_table = table[:, LANES:]
    low_lane = lax.broadcasted_iota(jnp.int32, (40, LANES), 1)
    filler = jnp.zeros((96, 256), jnp.bfloat16)
    for band in range(4):
        highs, lows = [], []
        for part in range(2):
            span = slice((band * 2 + part) * 40, (band * 2 + part) * 40 + 40)
            first, second, third = rows[0, span, :], rows[1, span, :], rows[2, span, :]
            quarters = [
                first,
                jnp.where(low_lane < 32, pltpu.roll(first, 32, 1), pltpu.roll(second, 32, 1)),
                jnp.where(low_lane < 64, pltpu.roll(second, 64, 1), pltpu.roll(third, 64, 1)),
                pltpu.roll(third, 96, 1),
            ]
            values = jnp.concatenate(quarters, 0)
            values = jnp.where(mask[...] > 0.0, values, 0.0)
            both = jnp.concatenate(halves(values), 1)
            chosen = mm(pick[...], jnp.concatenate([both, filler], 0))
            highs.append(chosen[:, :128].astype(jnp.bfloat16))
            lows.append(chosen[:, 128:].astype(jnp.bfloat16))
        high = jnp.concatenate(highs, 0)
        spread = jnp.concatenate([high, jnp.concatenate(lows, 0)], 1)
        waves = mm_t(wide_table, spread) + mm_t(low_table, high)
        cosine, sine = waves[:192], waves[192:]
        held[band, :192] = cosine[:, :128] - sine[:, 128:]
        held[band, 192:] = sine[:, :128] + cosine[:, 128:]
    lane = lax.broadcasted_iota(jnp.int32, (8, LANES), 1)
    row = lax.broadcasted_iota(jnp.int32, (8, LANES), 0)
    marks = jnp.zeros((8, LANES), jnp.float32)
    spots = jnp.broadcast_to(ids[...], (8, LANES))
    for index in range(8):
        marks = jnp.where(row == index, pltpu.roll(spots, STICK_LIMIT - SPARE * index, 1), marks)
    for dest in range(16):
        tail = pieces(held, dest, 11)
        for tile in range(11):
            main = pieces(held, dest, tile)
            if tile < 8:
                extra = pltpu.roll(tail, STICK_LIMIT - SPARE * tile, 1)
            else:
                extra = marks
            out[dest, tile * 8 : tile * 8 + 8, :] = jnp.where(lane < STICK_LIMIT, main, extra)


def density_kernel(
    factors,
    recv,
    inv_y,
    inv_x,
    fwd_y1,
    fwd_y2,
    fwd_x,
    own,
    other,
    columns,
    grid,
    held_re,
    held_im,
    density,
    ids_vector,
    ids,
    arrival,
):
    lane = lax.broadcasted_iota(jnp.int32, (16, LANES), 1)
    marks = jnp.zeros((16, LANES), jnp.float32)
    for index in range(8):
        rolled = pltpu.roll(recv[pl.ds(64 + index, 16, stride=ROWS), :], 15 + SPARE * index, 1)
        marks = jnp.where(lane // SPARE == index, rolled, marks)
    ids_vector[...] = marks.astype(jnp.int32)
    to_scalars = pltpu.make_async_copy(ids_vector, ids, arrival)
    to_scalars.start()
    lane = lane[:8]
    pad = jnp.zeros((32, LANES), jnp.float32)
    for source in range(16):
        first = source * ROWS
        tail = jnp.zeros((8, LANES), jnp.float32)
        for tile in range(8):
            piece = recv[first + tile * 8 : first + tile * 8 + 8, :]
            tail = jnp.where(lane // SPARE == tile, pltpu.roll(piece, 15 + SPARE * tile, 1), tail)
        columns[source] = jnp.concatenate([recv[first : first + ROWS, :], tail, pad], 0).T
    blank = jnp.zeros((48, 128), jnp.float32)
    for row in range(50, 64):
        held_re[pl.ds(row, 48, stride=HELD), :] = blank
        held_im[pl.ds(row, 48, stride=HELD), :] = blank
    grid[...] = jnp.zeros_like(grid)
    to_scalars.wait()

    def put(source, _):
        for stick in range(STICK_LIMIT):
            grid[pl.ds(ids[source, stick], 1), :] = columns[source, stick : stick + 1, :]
        return 0

    lax.fori_loop(0, 16, put, 0)
    lower = lax.broadcasted_iota(jnp.int32, (96, 128), 1) < 64

    def place(pair, _):
        rows = grid[pl.ds(pl.multiple_of(pair * 128, 128), 128), :].T[:96]
        high = rows.astype(jnp.bfloat16).astype(jnp.float32)
        low = pltpu.roll(rows - high, 64, 1)
        for half in range(2):
            mixed = jnp.where(lower, low, high) if half else jnp.where(lower, high, low)
            both = jnp.concatenate([mixed, high], 1).astype(jnp.bfloat16)
            out = mm(both, inv_y[half])
            rows_to = pl.ds(pair * 2 + half, 48, stride=HELD)
            held_re[rows_to, :] = out[:48, :128] - out[48:, 128:]
            held_im[rows_to, :] = out[48:, :128] + out[:48, 128:]
        return 0

    lax.fori_loop(0, 25, place, 0, unroll=25)
    clear = jnp.zeros((2 * SLOTS, 128), jnp.float32)
    for row in range(PLANES, 16):
        own[pl.ds(row, 2 * SLOTS, stride=16), :] = clear
        other[pl.ds(row, 2 * SLOTS, stride=16), :] = clear

    def waves(plane, _):
        total = jnp.zeros((96, 128), jnp.float32)
        for band in range(4):
            start = pl.multiple_of((band * PLANES + plane) * HELD, HELD)
            rows = pl.ds(start, 64)
            high, low = halves(jnp.concatenate([held_re[rows, :], held_im[rows, :]], 1))
            out = mm(inv_x[...], jnp.concatenate([high, low, high], 0))
            wave_re = out[:96, :128] - out[96:, 128:]
            wave_im = out[96:, :128] + out[:96, 128:]
            total = total + factors[band] * (wave_re * wave_re + wave_im * wave_im)
        density[pl.ds(pl.multiple_of(plane * 96, 96), 96), :] = total
        return 0

    lax.fori_loop(0, PLANES, waves, 0, unroll=4)

    def forward(group, _):
        start = pl.multiple_of(group * 384, 384)
        high, low = halves(density[pl.ds(start, 384), :])
        rows = mm(jnp.concatenate([high, low], 1), fwd_y1[...]) + mm(high, fwd_y2[...])
        high, low = halves(rows)
        for pair in range(2):
            first, second = slice(pair * 192, pair * 192 + 96), slice(pair * 192 + 96, pair * 192 + 192)
            wide_high = jnp.concatenate([high[first], high[second]], 1)
            wide_low = jnp.concatenate([low[first], low[second]], 1)
            out = mm(fwd_x[...], jnp.concatenate([wide_high, wide_low, wide_high], 0))
            for member in range(2):
                plane = group * 4 + pair * 2 + member
                lanes = slice(member * 128, member * 128 + 128)
                cosine = pl.ds(plane, SLOTS, stride=16)
                sine = pl.ds(plane + SIDE_ROWS, SLOTS, stride=16)
                own[cosine, :] = out[0:SLOTS, lanes]
                own[sine, :] = out[32 : 32 + SLOTS, lanes]
                other[cosine, :] = out[64 : 64 + SLOTS, lanes]
                other[sine, :] = out[96 : 96 + SLOTS, lanes]
        return 0

    lax.fori_loop(0, 3, forward, 0, unroll=3)


def force_kernel(
    gx2, own, arrived, base, wave_z, atom_z, near_z, x_all, y_cos, y_sin, strength, out, acc, turn
):
    acc[...] = jnp.zeros_like(acc)
    turn[...] = x_all[...]

    def step(slot, reach, phases):
        start = pl.multiple_of(slot * 16, 16)
        first, second = pl.ds(start, 16), pl.ds(start + SIDE_ROWS, 16)
        pair = [own[first, :] + arrived[first, :], own[second, :] + arrived[second, :]]
        high, low = halves(jnp.concatenate(pair, 1))
        waves = wave_z[...]
        if reach < ZSPAN:
            waves = jnp.concatenate([waves[:reach], waves[ZSPAN : ZSPAN + reach]], 0)
        raw = mm(waves, jnp.concatenate([high, low, high], 0))
        weight = 1.0 / (base[:reach] + gx2[slot])
        weight = jnp.concatenate([weight, weight], 1)
        weight = jnp.concatenate([weight, weight], 0)
        high, low = halves(raw * weight)
        both = mm(phases[...], jnp.concatenate([high, low, high], 0))
        table = turn[...]
        xc_c, xc_s = table[:, 0:1], table[:, 32:33]
        xs_c, xs_s = table[:, 64:65], table[:, 96:97]
        plain_c, plain_s = both[:128, :128], both[:128, 128:]
        acc[0] += xs_c * plain_c + xs_s * plain_s
        acc[1] += xc_c * plain_c + xc_s * plain_s
        acc[2] += xc_c * both[128:, :128] + xc_s * both[128:, 128:]
        turn[...] = pltpu.roll(table, 127, 1)
        return 0

    lax.fori_loop(0, 14, lambda slot, _: step(slot, ZSPAN, atom_z), 0, unroll=7)
    lax.fori_loop(14, SLOTS, lambda slot, _: step(slot, NEAR, near_z), 0, unroll=11)
    parts = [acc[0] * y_cos[...], acc[1] * y_sin[...], acc[2] * y_cos[...]]
    rows = [-strength[...] * jnp.sum(part.T, axis=0, keepdims=True) for part in parts]
    block = jnp.concatenate(rows, 0)
    for index in range(16):
        out[index] = block


def shards(
    coefficients, occupation, kpoint_weight, stick_cell, species, positions, amplitude, core_width
):
    cells = jnp.pad(stick_cell.reshape(GROUPS, 4).T, ((0, 0), (0, 4)), constant_values=48 * NY)
    cells = cells.reshape(160)
    freq_x = signed_freq(cells // NY, NX)
    freq_y = signed_freq(cells % NY, NY)
    freq_z = jnp.arange(LANES, dtype=jnp.int32) - NZ // 4
    disk = 16 * (freq_x * freq_x + freq_y * freq_y)
    level = disk[:, None] + 4 * (freq_z * freq_z)[None, :]
    mask = ((level <= NX * NX) & (freq_z < NZ // 4)[None, :]).astype(jnp.float32)
    chosen = disk <= NX * NX
    before = jnp.arange(160)[:, None] < jnp.arange(160)[None, :]
    rank = jnp.sum(jnp.where(before & chosen[:, None], 1, 0), axis=0)
    lane = jnp.arange(LANES, dtype=jnp.int32)
    pick = chosen[None, :] & (rank[None, :] == lane[:, None])
    place = (freq_x + HALF) * 64 + freq_y + HALF
    ids = jnp.sum(jnp.where(pick, place[None, :] - SPARE_ROW, 0), axis=1) + SPARE_ROW
    pick = jnp.pad(pick.astype(jnp.bfloat16), ((0, 0), (0, 96)))
    payload = pl.pallas_call(
        send_kernel,
        out_shape=jax.ShapeDtypeStruct((16, ROWS, LANES), jnp.float32),
        in_specs=[VMEM] * 5,
        out_specs=VMEM,
        scratch_shapes=[
            pltpu.VMEM((4, 384, LANES), jnp.float32),
            pltpu.VMEM((3, 320, LANES), jnp.float32),
        ],
        compiler_params=pltpu.CompilerParams(vmem_limit_bytes=40 * 1024 * 1024),
        name="sticks",
    )(coefficients[0], mask, pick, ids.astype(jnp.float32)[None], z_table())
    received = lax.all_to_all(payload, "fft", split_axis=0, concat_axis=0, tiled=True)
    received = received.reshape(16 * ROWS, LANES)

    core = lax.axis_index("band") % 2
    pool_weight = lax.dynamic_index_in_dim(
        kpoint_weight, lax.axis_index("pool"), keepdims=False
    ).astype(jnp.float32) / jnp.sum(kpoint_weight).astype(jnp.float32)
    factors = pool_weight * occupation[0] * (16.0 / NGRID / 32.0 / NGRID)
    fwd_y1, fwd_y2 = forward_y_tables()
    fwd_x = lax.dynamic_index_in_dim(jnp.asarray(forward_x_tables()), core, keepdims=False)
    halves_shape = jax.ShapeDtypeStruct((2 * SIDE_ROWS, 128), jnp.float32)
    own, other = pl.pallas_call(
        density_kernel,
        out_shape=(halves_shape, halves_shape),
        in_specs=[SMEM] + [VMEM] * 6,
        out_specs=(VMEM, VMEM),
        scratch_shapes=[
            pltpu.VMEM((16, LANES, LANES), jnp.float32),
            pltpu.VMEM((50 * 64, LANES), jnp.float32),
            pltpu.VMEM((48 * HELD, LANES), jnp.float32),
            pltpu.VMEM((48 * HELD, LANES), jnp.float32),
            pltpu.VMEM((PLANES * 96, LANES), jnp.float32),
            pltpu.VMEM((16, LANES), jnp.int32),
            pltpu.SMEM((16, LANES), jnp.int32),
            pltpu.SemaphoreType.DMA,
        ],
        compiler_params=pltpu.CompilerParams(vmem_limit_bytes=40 * 1024 * 1024),
        name="density",
    )(factors, received, inverse_y_tables(), inverse_x_table(), fwd_y1, fwd_y2, fwd_x)
    swap = [(index, index ^ 1) for index in range(8)]
    arrived = lax.ppermute(other, "band", swap)

    start = lax.axis_index("fft") * PLANES
    steps = (jnp.arange(ZSPAN)[:, None] * (start + jnp.arange(PLANES))[None, :]) % NZ
    angles = 2.0 * math.pi / NZ * steps.astype(jnp.float32)
    turned = jnp.pad(jnp.concatenate([jnp.cos(angles), jnp.sin(angles)], 0), ((0, 0), (0, 4)))
    high, low = table_halves(turned)
    wave_z = jnp.concatenate([high, high, low], 1)
    kinds = species[None, :] == jnp.arange(3, dtype=jnp.int32)[:, None]
    width = jnp.sum(jnp.where(kinds, core_width[:, None], 0.0), axis=0)
    strength = jnp.sum(jnp.where(kinds, amplitude[:, None], 0.0), axis=0)

    def tables(where, order, unit, counts):
        waves = unit * order
        turns = where[:, None] * order[None, :]
        phase = 2.0 * math.pi * (turns - jnp.round(turns))
        scale = counts[None, :] * jnp.exp(-0.5 * (width * width)[:, None] * (waves * waves)[None])
        cosine, sine = scale * jnp.cos(phase), scale * jnp.sin(phase)
        slope = waves[None, :]
        return cosine, sine, slope * sine, -slope * cosine

    hx = 2.0 * jnp.arange(32, dtype=jnp.float32) + core.astype(jnp.float32)
    unit = 2.0 * math.pi / 96
    count_x = jnp.where(hx > 48.0, 0.0, jnp.where((hx == 0.0) | (hx == 48.0), 1.0, 2.0))
    x_all = jnp.concatenate(tables(positions[0], hx, unit, count_x), 1)
    hy = jnp.arange(64, dtype=jnp.float32)
    count_y = jnp.where(hy > 48.0, 0.0, jnp.where((hy == 0.0) | (hy == 48.0), 1.0, 2.0))
    y_parts = tables(positions[1], hy, unit, count_y)
    y_cos = jnp.concatenate(y_parts[:2], 1)
    y_sin = jnp.concatenate(y_parts[2:], 1)
    hz = jnp.arange(ZSPAN, dtype=jnp.float32)
    z_parts = tables(positions[2], hz, 2.0 * math.pi / NZ, jnp.where(hz == 0.0, 1.0, 2.0))

    def atom_table(reach):
        plain = jnp.concatenate([part[:, :reach] for part in z_parts[:2]], 1)
        sloped = jnp.concatenate([part[:, :reach] for part in z_parts[2:]], 1)
        high, low = table_halves(jnp.concatenate([plain, sloped], 0))
        return jnp.concatenate([high, high, low], 1)

    gy = np.tile(2.0 * np.pi / 96 * np.arange(64), 2)
    gz = 2.0 * np.pi / NZ * np.arange(ZSPAN)
    base = (gy[None, :] ** 2 + gz[:, None] ** 2 + screen).astype(np.float32)
    gx2 = (unit * hx) * (unit * hx)
    spread = pl.pallas_call(
        force_kernel,
        out_shape=jax.ShapeDtypeStruct((16, 3, LANES), jnp.float32),
        in_specs=[SMEM] + [VMEM] * 10,
        out_specs=VMEM,
        scratch_shapes=[
            pltpu.VMEM((3, 128, 128), jnp.float32),
            pltpu.VMEM((128, 128), jnp.float32),
        ],
        compiler_params=pltpu.CompilerParams(vmem_limit_bytes=40 * 1024 * 1024),
        name="force",
    )(
        gx2,
        own,
        arrived,
        base,
        wave_z,
        atom_table(ZSPAN),
        atom_table(NEAR),
        x_all,
        y_cos,
        y_sin,
        strength[None],
    )
    across, along = reduce_groups()
    total = jnp.sum(lax.all_to_all(spread, AXES, 0, 0, axis_index_groups=across, tiled=True), axis=0)
    spread = jnp.broadcast_to(total[None], (16, 3, LANES))
    return jnp.sum(lax.all_to_all(spread, AXES, 0, 0, axis_index_groups=along, tiled=True), axis=0)


def solution(mesh):
    placed = (P("pool", "band", None, "fft"), P("pool", "band"), P(), P("fft"), P(), P(), P(), P())
    return jax.shard_map(shards, mesh=mesh, in_specs=placed, out_specs=P(), check_vma=False)
```

```python
import math

import jax
import jax.numpy as jnp
import numpy as np
from jax import lax
from jax.experimental import pallas as pl
from jax.experimental.pallas import tpu as pltpu
from jax.sharding import PartitionSpec as P

NX = 96
NY = 96
NZ = 192
ZSPAN = 96
NGRID = 1769472
HALF = 24
SIDE = 49
LANES = 128
PLANES = 12
SLOTS = 25
SIDE_ROWS = SLOTS * 16
STICK_LIMIT = 113
SPARE = 15
ROWS = 88
NEAR = 80
HELD = 72
GROUPS = 36
SPARE_ROW = SIDE * 64
HIGH = lax.Precision.HIGH
screen = 0.25
AXES = ("pool", "band", "fft")
VMEM = pl.BlockSpec(memory_space=pltpu.VMEM)
SMEM = pl.BlockSpec(memory_space=pltpu.SMEM)


def trig(rows, columns, length):
    angles = 2.0 * np.pi / length * (np.outer(rows, columns) % length)
    return np.cos(angles).astype(np.float32), np.sin(angles).astype(np.float32)


def exchange_groups():
    ranks = np.arange(256).reshape(16, 8, 2)
    return ranks.transpose(0, 2, 1).reshape(16, 16).tolist()


def reduce_groups():
    ranks = np.arange(256).reshape(2, 4, 2, 8, 2)
    across = ranks.transpose(3, 2, 0, 4, 1).reshape(16, 16)
    along = ranks.transpose(0, 4, 1, 3, 2).reshape(16, 16)
    return across.tolist(), along.tolist()


def halves(values):
    high = values.astype(jnp.bfloat16)
    return high, (values - high.astype(jnp.float32)).astype(jnp.bfloat16)


def table_halves(values):
    high = lax.reduce_precision(values, 8, 7)
    return high.astype(jnp.bfloat16), (values - high).astype(jnp.bfloat16)


def np_halves(values):
    high = values.astype(jnp.bfloat16)
    return high, (values - high.astype(np.float32)).astype(jnp.bfloat16)


def mm(left, right):
    return jnp.dot(left, right, preferred_element_type=jnp.float32)


def z_table():
    both = np.zeros((2, NZ, LANES), np.float32)
    both[:, :, :ZSPAN] = trig(np.arange(NZ), np.arange(ZSPAN) - NZ // 4, NZ)
    return np.concatenate(np_halves(both.reshape(2 * NZ, LANES)), 1)


def inverse_y_tables():
    cosine, sine = trig(np.arange(SIDE) - HALF, np.arange(96), 96)
    both = np.zeros((SIDE, 256), np.float32)
    both[:, :96], both[:, 128:224] = cosine, sine
    high, low = np_halves(both)
    table = np.zeros((2, 256, 256), high.dtype)
    for half in range(2):
        for part in range(2):
            table[half, 64 * part : 64 * part + SIDE] = high
        table[half, 128 + 64 * half : 128 + 64 * half + SIDE] = low
    return table


def inverse_x_table():
    cosine, sine = trig(np.arange(96), np.arange(SIDE) - HALF, 96)
    both = np.zeros((192, 64), np.float32)
    both[:96, :SIDE], both[96:, :SIDE] = cosine, sine
    high, low = np_halves(both)
    return np.concatenate([high, high, low], 1)


def forward_y_tables():
    cosine, sine = trig(np.arange(96), np.arange(SIDE), 96)
    both = np.zeros((128, 128), np.float32)
    both[:96, :SIDE], both[:96, 64 : 64 + SIDE] = cosine, sine
    high, low = np_halves(both)
    return np.concatenate([high, high], 0), low


def forward_x_tables():
    cosine, sine = trig(np.arange(50), np.arange(96), 96)
    cosine[SIDE:], sine[SIDE:] = 0.0, 0.0
    result = []
    for core in range(2):
        both = np.zeros((128, 96), np.float32)
        for index, rows in enumerate((core, 1 - core)):
            both[64 * index : 64 * index + SLOTS] = cosine[rows::2]
            both[64 * index + 32 : 64 * index + 32 + SLOTS] = sine[rows::2]
        high, low = np_halves(both)
        result.append(np.concatenate([high, high, low], 1))
    return np.stack(result)


def mm_t(left, right):
    return lax.dot_general(
        left, right, (((1,), (1,)), ((), ())), preferred_element_type=jnp.float32
    )


def small(flags):
    return flags.astype(jnp.float32).astype(jnp.bfloat16)


def pieces(held, dest, tile):
    found = []
    for row in range(tile * 8, tile * 8 + 8, 4):
        start = (row // 48) * 192 + dest * PLANES + row % 12
        found.append(held[(row % 48) // 12, start : start + 4, :])
    return jnp.concatenate(found, 0)


def send_kernel(cells, coefs, z_waves, out, raw, table, held, natural, rows, loads):
    copies = [
        pltpu.make_async_copy(coefs.at[0, band], raw.at[band], loads.at[band]) for band in range(4)
    ]
    copies.append(pltpu.make_async_copy(z_waves, table, loads.at[4]))
    for copy in copies:
        copy.start()
    stick = jnp.concatenate([cells[...], jnp.full((1, 112), 48 * NY, jnp.int32)], 1)
    stick = jnp.broadcast_to(stick, (8, 256))
    column = stick // NY
    freq_x = jnp.where(column < 48, column, column - NX)
    freq_y = stick - column * NY
    freq_y = jnp.where(freq_y < 48, freq_y, freq_y - NY)
    reach = freq_x * freq_x + freq_y * freq_y
    chosen = reach <= HALF * HALF
    earlier = lax.broadcasted_iota(jnp.int32, (256, 256), 0)
    earlier = earlier < lax.broadcasted_iota(jnp.int32, (256, 256), 1)
    rank = mm(chosen.astype(jnp.float32).astype(jnp.bfloat16), small(earlier))
    order = lax.broadcasted_iota(jnp.int32, (LANES, 256), 0).astype(jnp.float32)
    pick = small((rank[0:1] == order) & chosen[0:1])
    line = lax.broadcasted_iota(jnp.int32, (8, 256), 0)
    facts = jnp.where(line == 0, (freq_x + HALF) * 64, jnp.where(line == 1, freq_y + HALF, 1))
    facts = mm_t(facts.astype(jnp.float32).astype(jnp.bfloat16), pick)
    ids = facts[0:1] + facts[1:2] + SPARE_ROW * (1.0 - facts[2:3])
    coarse = reach // 16 * 16
    spread = [jnp.broadcast_to(part[0:1], (LANES, 256)) for part in (coarse, reach - coarse)]
    level = sum(mm_t(pick, part.astype(jnp.float32).astype(jnp.bfloat16)) for part in spread)
    slot = lax.broadcasted_iota(jnp.int32, (LANES, LANES), 1)
    freq_z = (slot - NZ // 4).astype(jnp.float32)
    inside = (16.0 * level + 4.0 * freq_z * freq_z <= NX * NX) & (slot < ZSPAN)
    inside = jnp.concatenate([inside, inside], 1)
    for copy in copies:
        copy.wait()
    high_table = table[:, :LANES]
    wide_table = jnp.concatenate([high_table, high_table], 1)
    low_table = table[:, LANES:]
    lane = lax.broadcasted_iota(jnp.int32, (40, LANES), 1)
    filler = jnp.zeros((112, 256), jnp.bfloat16)
    for band in range(4):
        highs, lows = [], []
        for chunk in range(3 * GROUPS):
            piece = raw[band, :, chunk * LANES : (chunk + 1) * LANES]
            for part in range(2):
                start = part * 40 + chunk // 3
                rows[band, chunk % 3, start : start + 1, :] = piece[part : part + 1]
        for part in range(2):
            span = slice(part * 40, part * 40 + 40)
            first, second, third = rows[band, 0, span, :], rows[band, 1, span, :], rows[band, 2, span, :]
            quarters = [
                first,
                jnp.where(lane < 32, pltpu.roll(first, 32, 1), pltpu.roll(second, 32, 1)),
                jnp.where(lane < 64, pltpu.roll(second, 64, 1), pltpu.roll(third, 64, 1)),
                pltpu.roll(third, 96, 1),
            ]
            for index in range(4):
                natural[band, pl.ds(part * 144 + index, GROUPS, stride=4), :] = quarters[index][:GROUPS]
            values = natural[band, part * 144 : part * 144 + 144, :]
            both = jnp.concatenate(halves(values), 1)
            taken = mm(pick, jnp.concatenate([both, filler], 0))
            taken = jnp.where(inside, taken, 0.0).astype(jnp.bfloat16)
            highs.append(taken[:, :128])
            lows.append(taken[:, 128:])
        high = jnp.concatenate(highs, 0)
        spread = jnp.concatenate([high, jnp.concatenate(lows, 0)], 1)
        waves = mm_t(wide_table, spread) + mm_t(low_table, high)
        cosine, sine = waves[:192], waves[192:]
        held[band, :192] = cosine[:, :128] - sine[:, 128:]
        held[band, 192:] = sine[:, :128] + cosine[:, 128:]
    lane = lax.broadcasted_iota(jnp.int32, (8, LANES), 1)
    row = lax.broadcasted_iota(jnp.int32, (8, LANES), 0)
    marks = jnp.zeros((8, LANES), jnp.float32)
    spots = jnp.broadcast_to(ids, (8, LANES))
    for index in range(8):
        marks = jnp.where(row == index, pltpu.roll(spots, STICK_LIMIT - SPARE * index, 1), marks)
    for dest in range(16):
        tail = pieces(held, dest, 11)
        for tile in range(11):
            main = pieces(held, dest, tile)
            if tile < 8:
                extra = pltpu.roll(tail, STICK_LIMIT - SPARE * tile, 1)
            else:
                extra = marks
            out[dest, tile * 8 : tile * 8 + 8, :] = jnp.where(lane < STICK_LIMIT, main, extra)


def density_kernel(
    factors,
    recv,
    inv_y,
    inv_x,
    fwd_y1,
    fwd_y2,
    fwd_x,
    own,
    other,
    columns,
    grid,
    held_re,
    held_im,
    density,
    ids_vector,
    ids,
    arrival,
):
    lane = lax.broadcasted_iota(jnp.int32, (16, LANES), 1)
    marks = jnp.zeros((16, LANES), jnp.float32)
    for index in range(8):
        rolled = pltpu.roll(recv[pl.ds(64 + index, 16, stride=ROWS), :], 15 + SPARE * index, 1)
        marks = jnp.where(lane // SPARE == index, rolled, marks)
    ids_vector[...] = marks.astype(jnp.int32)
    to_scalars = pltpu.make_async_copy(ids_vector, ids, arrival)
    to_scalars.start()
    lane = lane[:8]
    pad = jnp.zeros((32, LANES), jnp.float32)
    for source in range(16):
        first = source * ROWS
        tail = jnp.zeros((8, LANES), jnp.float32)
        for tile in range(8):
            piece = recv[first + tile * 8 : first + tile * 8 + 8, :]
            tail = jnp.where(lane // SPARE == tile, pltpu.roll(piece, 15 + SPARE * tile, 1), tail)
        columns[source] = jnp.concatenate([recv[first : first + ROWS, :], tail, pad], 0).T
    blank = jnp.zeros((48, 128), jnp.float32)
    for row in range(50, 64):
        held_re[pl.ds(row, 48, stride=HELD), :] = blank
        held_im[pl.ds(row, 48, stride=HELD), :] = blank
    grid[...] = jnp.zeros_like(grid)
    to_scalars.wait()

    def put(source, _):
        for stick in range(STICK_LIMIT):
            grid[pl.ds(ids[source, stick], 1), :] = columns[source, stick : stick + 1, :]
        return 0

    lax.fori_loop(0, 16, put, 0)
    lower = lax.broadcasted_iota(jnp.int32, (96, 128), 1) < 64

    def place(pair, _):
        rows = grid[pl.ds(pl.multiple_of(pair * 128, 128), 128), :].T[:96]
        high = rows.astype(jnp.bfloat16).astype(jnp.float32)
        low = pltpu.roll(rows - high, 64, 1)
        for half in range(2):
            mixed = jnp.where(lower, low, high) if half else jnp.where(lower, high, low)
            both = jnp.concatenate([mixed, high], 1).astype(jnp.bfloat16)
            out = mm(both, inv_y[half])
            rows_to = pl.ds(pair * 2 + half, 48, stride=HELD)
            held_re[rows_to, :] = out[:48, :128] - out[48:, 128:]
            held_im[rows_to, :] = out[48:, :128] + out[:48, 128:]
        return 0

    lax.fori_loop(0, 25, place, 0, unroll=25)
    clear = jnp.zeros((2 * SLOTS, 128), jnp.float32)
    for row in range(PLANES, 16):
        own[pl.ds(row, 2 * SLOTS, stride=16), :] = clear
        other[pl.ds(row, 2 * SLOTS, stride=16), :] = clear

    def waves(plane, _):
        total = jnp.zeros((96, 128), jnp.float32)
        for band in range(4):
            start = pl.multiple_of((band * PLANES + plane) * HELD, HELD)
            rows = pl.ds(start, 64)
            high, low = halves(jnp.concatenate([held_re[rows, :], held_im[rows, :]], 1))
            out = mm(inv_x[...], jnp.concatenate([high, low, high], 0))
            wave_re = out[:96, :128] - out[96:, 128:]
            wave_im = out[96:, :128] + out[:96, 128:]
            total = total + factors[band] * (wave_re * wave_re + wave_im * wave_im)
        density[pl.ds(pl.multiple_of(plane * 96, 96), 96), :] = total
        return 0

    lax.fori_loop(0, PLANES, waves, 0, unroll=4)

    def forward(group, _):
        start = pl.multiple_of(group * 384, 384)
        high, low = halves(density[pl.ds(start, 384), :])
        rows = mm(jnp.concatenate([high, low], 1), fwd_y1[...]) + mm(high, fwd_y2[...])
        high, low = halves(rows)
        for pair in range(2):
            first, second = slice(pair * 192, pair * 192 + 96), slice(pair * 192 + 96, pair * 192 + 192)
            wide_high = jnp.concatenate([high[first], high[second]], 1)
            wide_low = jnp.concatenate([low[first], low[second]], 1)
            out = mm(fwd_x[...], jnp.concatenate([wide_high, wide_low, wide_high], 0))
            for member in range(2):
                plane = group * 4 + pair * 2 + member
                lanes = slice(member * 128, member * 128 + 128)
                cosine = pl.ds(plane, SLOTS, stride=16)
                sine = pl.ds(plane + SIDE_ROWS, SLOTS, stride=16)
                own[cosine, :] = out[0:SLOTS, lanes]
                own[sine, :] = out[32 : 32 + SLOTS, lanes]
                other[cosine, :] = out[64 : 64 + SLOTS, lanes]
                other[sine, :] = out[96 : 96 + SLOTS, lanes]
        return 0

    lax.fori_loop(0, 3, forward, 0, unroll=3)


def force_kernel(
    gx2, own, arrived, base, wave_z, atom_z, near_z, x_all, y_cos, y_sin, strength, out, acc, turn
):
    acc[...] = jnp.zeros_like(acc)
    turn[...] = x_all[...]

    def step(slot, reach, phases):
        start = pl.multiple_of(slot * 16, 16)
        first, second = pl.ds(start, 16), pl.ds(start + SIDE_ROWS, 16)
        pair = [own[first, :] + arrived[first, :], own[second, :] + arrived[second, :]]
        high, low = halves(jnp.concatenate(pair, 1))
        waves = wave_z[...]
        if reach < ZSPAN:
            waves = jnp.concatenate([waves[:reach], waves[ZSPAN : ZSPAN + reach]], 0)
        raw = mm(waves, jnp.concatenate([high, low, high], 0))
        weight = 1.0 / (base[:reach] + gx2[slot])
        weight = jnp.concatenate([weight, weight], 1)
        weight = jnp.concatenate([weight, weight], 0)
        high, low = halves(raw * weight)
        both = mm(phases[...], jnp.concatenate([high, low, high], 0))
        table = turn[...]
        xc_c, xc_s = table[:, 0:1], table[:, 32:33]
        xs_c, xs_s = table[:, 64:65], table[:, 96:97]
        plain_c, plain_s = both[:128, :128], both[:128, 128:]
        acc[0] += xs_c * plain_c + xs_s * plain_s
        acc[1] += xc_c * plain_c + xc_s * plain_s
        acc[2] += xc_c * both[128:, :128] + xc_s * both[128:, 128:]
        turn[...] = pltpu.roll(table, 127, 1)
        return 0

    lax.fori_loop(0, 14, lambda slot, _: step(slot, ZSPAN, atom_z), 0, unroll=7)
    lax.fori_loop(14, SLOTS, lambda slot, _: step(slot, NEAR, near_z), 0, unroll=11)
    parts = [acc[0] * y_cos[...], acc[1] * y_sin[...], acc[2] * y_cos[...]]
    rows = [-strength[...] * jnp.sum(part.T, axis=0, keepdims=True) for part in parts]
    block = jnp.concatenate(rows, 0)
    for index in range(16):
        out[index] = block


def shards(
    coefficients, occupation, kpoint_weight, stick_cell, species, positions, amplitude, core_width
):
    payload = pl.pallas_call(
        send_kernel,
        out_shape=jax.ShapeDtypeStruct((16, ROWS, LANES), jnp.float32),
        in_specs=[VMEM, pl.BlockSpec(memory_space=pltpu.HBM), pl.BlockSpec(memory_space=pltpu.HBM)],
        out_specs=VMEM,
        scratch_shapes=[
            pltpu.VMEM((4, 2, 13824), jnp.float32),
            pltpu.VMEM((384, 256), jnp.bfloat16),
            pltpu.VMEM((4, 384, LANES), jnp.float32),
            pltpu.VMEM((4, 288, LANES), jnp.float32),
            pltpu.VMEM((4, 3, 80, LANES), jnp.float32),
            pltpu.SemaphoreType.DMA((5,)),
        ],
        compiler_params=pltpu.CompilerParams(vmem_limit_bytes=60 * 1024 * 1024),
        name="sticks",
    )(stick_cell[None], coefficients, z_table())
    received = lax.all_to_all(payload, AXES, 0, 0, axis_index_groups=exchange_groups(), tiled=True)
    received = received.reshape(16 * ROWS, LANES)

    core = lax.axis_index("band") % 2
    pool_weight = lax.dynamic_index_in_dim(
        kpoint_weight, lax.axis_index("pool"), keepdims=False
    ).astype(jnp.float32) / jnp.sum(kpoint_weight).astype(jnp.float32)
    factors = pool_weight * occupation[0] * (16.0 / NGRID / 32.0 / NGRID)
    fwd_y1, fwd_y2 = forward_y_tables()
    fwd_x = lax.dynamic_index_in_dim(jnp.asarray(forward_x_tables()), core, keepdims=False)
    halves_shape = jax.ShapeDtypeStruct((2 * SIDE_ROWS, 128), jnp.float32)
    own, other = pl.pallas_call(
        density_kernel,
        out_shape=(halves_shape, halves_shape),
        in_specs=[SMEM] + [VMEM] * 6,
        out_specs=(VMEM, VMEM),
        scratch_shapes=[
            pltpu.VMEM((16, LANES, LANES), jnp.float32),
            pltpu.VMEM((50 * 64, LANES), jnp.float32),
            pltpu.VMEM((48 * HELD, LANES), jnp.float32),
            pltpu.VMEM((48 * HELD, LANES), jnp.float32),
            pltpu.VMEM((PLANES * 96, LANES), jnp.float32),
            pltpu.VMEM((16, LANES), jnp.int32),
            pltpu.SMEM((16, LANES), jnp.int32),
            pltpu.SemaphoreType.DMA,
        ],
        compiler_params=pltpu.CompilerParams(vmem_limit_bytes=40 * 1024 * 1024),
        name="density",
    )(factors, received, inverse_y_tables(), inverse_x_table(), fwd_y1, fwd_y2, fwd_x)
    swap = [(index, index ^ 1) for index in range(8)]
    arrived = lax.ppermute(other, "band", swap)

    rank_z, rank_y = lax.axis_index("fft") // 2, lax.axis_index("fft") % 2
    start = (rank_y * 8 + rank_z) * PLANES
    steps = (jnp.arange(ZSPAN)[:, None] * (start + jnp.arange(PLANES))[None, :]) % NZ
    angles = 2.0 * math.pi / NZ * steps.astype(jnp.float32)
    turned = jnp.pad(jnp.concatenate([jnp.cos(angles), jnp.sin(angles)], 0), ((0, 0), (0, 4)))
    high, low = table_halves(turned)
    wave_z = jnp.concatenate([high, high, low], 1)
    kinds = species[None, :] == jnp.arange(3, dtype=jnp.int32)[:, None]
    width = jnp.sum(jnp.where(kinds, core_width[:, None], 0.0), axis=0)
    strength = jnp.sum(jnp.where(kinds, amplitude[:, None], 0.0), axis=0)

    def tables(where, order, unit, counts):
        waves = unit * order
        turns = where[:, None] * order[None, :]
        phase = 2.0 * math.pi * (turns - jnp.round(turns))
        scale = counts[None, :] * jnp.exp(-0.5 * (width * width)[:, None] * (waves * waves)[None])
        cosine, sine = scale * jnp.cos(phase), scale * jnp.sin(phase)
        slope = waves[None, :]
        return cosine, sine, slope * sine, -slope * cosine

    hx = 2.0 * jnp.arange(32, dtype=jnp.float32) + core.astype(jnp.float32)
    unit = 2.0 * math.pi / 96
    count_x = jnp.where(hx > 48.0, 0.0, jnp.where((hx == 0.0) | (hx == 48.0), 1.0, 2.0))
    x_all = jnp.concatenate(tables(positions[0], hx, unit, count_x), 1)
    hy = jnp.arange(64, dtype=jnp.float32)
    count_y = jnp.where(hy > 48.0, 0.0, jnp.where((hy == 0.0) | (hy == 48.0), 1.0, 2.0))
    y_parts = tables(positions[1], hy, unit, count_y)
    y_cos = jnp.concatenate(y_parts[:2], 1)
    y_sin = jnp.concatenate(y_parts[2:], 1)
    hz = jnp.arange(ZSPAN, dtype=jnp.float32)
    z_parts = tables(positions[2], hz, 2.0 * math.pi / NZ, jnp.where(hz == 0.0, 1.0, 2.0))

    def atom_table(reach):
        plain = jnp.concatenate([part[:, :reach] for part in z_parts[:2]], 1)
        sloped = jnp.concatenate([part[:, :reach] for part in z_parts[2:]], 1)
        high, low = table_halves(jnp.concatenate([plain, sloped], 0))
        return jnp.concatenate([high, high, low], 1)

    gy = np.tile(2.0 * np.pi / 96 * np.arange(64), 2)
    gz = 2.0 * np.pi / NZ * np.arange(ZSPAN)
    base = (gy[None, :] ** 2 + gz[:, None] ** 2 + screen).astype(np.float32)
    gx2 = (unit * hx) * (unit * hx)
    spread = pl.pallas_call(
        force_kernel,
        out_shape=jax.ShapeDtypeStruct((16, 3, LANES), jnp.float32),
        in_specs=[SMEM] + [VMEM] * 10,
        out_specs=VMEM,
        scratch_shapes=[
            pltpu.VMEM((3, 128, 128), jnp.float32),
            pltpu.VMEM((128, 128), jnp.float32),
        ],
        compiler_params=pltpu.CompilerParams(vmem_limit_bytes=40 * 1024 * 1024),
        name="force",
    )(
        gx2,
        own,
        arrived,
        base,
        wave_z,
        atom_table(ZSPAN),
        atom_table(NEAR),
        x_all,
        y_cos,
        y_sin,
        strength[None],
    )
    across, along = reduce_groups()
    total = jnp.sum(lax.all_to_all(spread, AXES, 0, 0, axis_index_groups=across, tiled=True), axis=0)
    spread = jnp.broadcast_to(total[None], (16, 3, LANES))
    return jnp.sum(lax.all_to_all(spread, AXES, 0, 0, axis_index_groups=along, tiled=True), axis=0)


def solution(mesh):
    placed = (P("pool", "band", None, "fft"), P("pool", "band"), P(), P("fft"), P(), P(), P(), P())
    return jax.shard_map(shards, mesh=mesh, in_specs=placed, out_specs=P(), check_vma=False)
```

```python
import math

import jax
import jax.numpy as jnp
import numpy as np
from jax import lax
from jax.experimental import pallas as pl
from jax.experimental.pallas import tpu as pltpu
from jax.sharding import PartitionSpec as P

NX = 96
NY = 96
NZ = 192
ZSPAN = 96
NGRID = 1769472
HALF = 24
SIDE = 49
LANES = 128
PLANES = 12
SLOTS = 25
SIDE_ROWS = SLOTS * 16
STICK_LIMIT = 113
SPARE = 15
ROWS = 88
NEAR = 80
HELD = 72
FOLD = 56
GROUPS = 36
SPARE_ROW = SIDE * 64
HIGH = lax.Precision.HIGH
screen = 0.25
AXES = ("pool", "band", "fft")
VMEM = pl.BlockSpec(memory_space=pltpu.VMEM)
HBM = pl.BlockSpec(memory_space=pltpu.HBM)
SMEM = pl.BlockSpec(memory_space=pltpu.SMEM)


def trig(rows, columns, length):
    angles = 2.0 * np.pi / length * (np.outer(rows, columns) % length)
    return np.cos(angles).astype(np.float32), np.sin(angles).astype(np.float32)


def exchange_groups():
    ranks = np.arange(256).reshape(16, 8, 2)
    return ranks.transpose(0, 2, 1).reshape(16, 16).tolist()


def reduce_groups():
    ranks = np.arange(256).reshape(2, 4, 2, 8, 2)
    across = ranks.transpose(3, 2, 0, 4, 1).reshape(16, 16)
    along = ranks.transpose(0, 4, 1, 3, 2).reshape(16, 16)
    return across.tolist(), along.tolist()


def halves(values):
    high = values.astype(jnp.bfloat16)
    return high, (values - high.astype(jnp.float32)).astype(jnp.bfloat16)


def table_halves(values):
    high = lax.reduce_precision(values, 8, 7)
    return high.astype(jnp.bfloat16), (values - high).astype(jnp.bfloat16)


def np_halves(values):
    high = values.astype(jnp.bfloat16)
    return high, (values - high.astype(np.float32)).astype(jnp.bfloat16)


def mm(left, right):
    return jnp.dot(left, right, preferred_element_type=jnp.float32)


def z_table():
    both = np.zeros((2, NZ, LANES), np.float32)
    both[:, :, :ZSPAN] = trig(np.arange(NZ), np.arange(ZSPAN) - NZ // 4, NZ)
    return np.concatenate(np_halves(both.reshape(2 * NZ, LANES)), 1)


def inverse_y_tables():
    cosine, sine = trig(np.arange(SIDE) - HALF, np.arange(96), 96)
    both = np.zeros((SIDE, 256), np.float32)
    both[:, :96], both[:, 128:224] = cosine, sine
    high, low = np_halves(both)
    table = np.zeros((2, 256, 256), high.dtype)
    for half in range(2):
        for part in range(2):
            table[half, 64 * part : 64 * part + SIDE] = high
        table[half, 128 + 64 * half : 128 + 64 * half + SIDE] = low
    return table


def inverse_x_table():
    cosine, sine = trig(np.arange(SIDE), np.arange(SIDE) - HALF, 96)
    both = np.zeros((2 * FOLD, 64), np.float32)
    both[:SIDE, :SIDE], both[FOLD : FOLD + SIDE, :SIDE] = cosine, sine
    high, low = np_halves(both)
    return np.concatenate([high, high, low], 1)


def forward_y_tables():
    cosine, sine = trig(np.arange(96), np.arange(SIDE), 96)
    both = np.zeros((128, 128), np.float32)
    both[:96, :SIDE], both[:96, 64 : 64 + SIDE] = cosine, sine
    high, low = np_halves(both)
    return np.concatenate([high, high], 0), low


def forward_x_tables():
    cosine, sine = trig(np.arange(50), np.arange(SIDE), 96)
    cosine[SIDE:], sine[SIDE:] = 0.0, 0.0
    cosine[:, 0], cosine[:, 48] = cosine[:, 0] / 2, cosine[:, 48] / 2
    result = []
    for core in range(2):
        both = np.zeros((128, 2 * FOLD), np.float32)
        for index, rows in enumerate((core, 1 - core)):
            both[64 * index : 64 * index + SLOTS, :SIDE] = cosine[rows::2]
            both[64 * index + 32 : 64 * index + 32 + SLOTS, FOLD : FOLD + SIDE] = sine[rows::2]
        high, low = np_halves(both)
        result.append(np.concatenate([high, high, low], 1))
    return np.stack(result)


def mm_t(left, right):
    return lax.dot_general(
        left, right, (((1,), (1,)), ((), ())), preferred_element_type=jnp.float32
    )


def small(flags):
    return flags.astype(jnp.float32).astype(jnp.bfloat16)


def pieces(held, dest, tile):
    found = []
    for row in range(tile * 8, tile * 8 + 8, 4):
        start = (row // 48) * 192 + dest * PLANES + row % 12
        found.append(held[(row % 48) // 12, start : start + 4, :])
    return jnp.concatenate(found, 0)


def send_kernel(
    cells, coefs, z_waves, out, place, raw, table, held, natural, rows, packed, loads, stores
):
    copies = [
        pltpu.make_async_copy(coefs.at[0, band], raw.at[band], loads.at[band]) for band in range(4)
    ]
    copies.append(pltpu.make_async_copy(z_waves, table, loads.at[4]))
    where = pltpu.make_async_copy(cells, place, loads.at[5])
    where.start()
    for copy in copies:
        copy.start()
    where.wait()
    for copy in copies:
        copy.wait()
    stick = jnp.concatenate([place[...], jnp.full((1, 112), 48 * NY, jnp.int32)], 1)
    stick = jnp.broadcast_to(stick, (8, 256))
    column = stick // NY
    freq_x = jnp.where(column < 48, column, column - NX)
    freq_y = stick - column * NY
    freq_y = jnp.where(freq_y < 48, freq_y, freq_y - NY)
    reach = freq_x * freq_x + freq_y * freq_y
    chosen = reach <= HALF * HALF
    earlier = lax.broadcasted_iota(jnp.int32, (256, 256), 0)
    earlier = earlier < lax.broadcasted_iota(jnp.int32, (256, 256), 1)
    rank = mm(chosen.astype(jnp.float32).astype(jnp.bfloat16), small(earlier))
    order = lax.broadcasted_iota(jnp.int32, (LANES, 256), 0).astype(jnp.float32)
    pick = small((rank[0:1] == order) & chosen[0:1])
    line = lax.broadcasted_iota(jnp.int32, (8, 256), 0)
    facts = jnp.where(line == 0, (freq_x + HALF) * 64, jnp.where(line == 1, freq_y + HALF, 1))
    facts = mm_t(facts.astype(jnp.float32).astype(jnp.bfloat16), pick)
    ids = facts[0:1] + facts[1:2] + SPARE_ROW * (1.0 - facts[2:3])
    coarse = reach // 16 * 16
    spread = [jnp.broadcast_to(part[0:1], (LANES, 256)) for part in (coarse, reach - coarse)]
    level = sum(mm_t(pick, part.astype(jnp.float32).astype(jnp.bfloat16)) for part in spread)
    slot = lax.broadcasted_iota(jnp.int32, (LANES, LANES), 1)
    freq_z = (slot - NZ // 4).astype(jnp.float32)
    inside = (16.0 * level + 4.0 * freq_z * freq_z <= NX * NX) & (slot < ZSPAN)
    inside = jnp.concatenate([inside, inside], 1)
    high_table = table[:, :LANES]
    wide_table = jnp.concatenate([high_table, high_table], 1)
    low_table = table[:, LANES:]
    lane = lax.broadcasted_iota(jnp.int32, (40, LANES), 1)
    filler = jnp.zeros((112, 256), jnp.bfloat16)
    for band in range(4):
        highs, lows = [], []
        for chunk in range(3 * GROUPS):
            piece = raw[band, :, chunk * LANES : (chunk + 1) * LANES]
            for part in range(2):
                start = part * 40 + chunk // 3
                rows[band, chunk % 3, start : start + 1, :] = piece[part : part + 1]
        for part in range(2):
            span = slice(part * 40, part * 40 + 40)
            first, second, third = rows[band, 0, span, :], rows[band, 1, span, :], rows[band, 2, span, :]
            quarters = [
                first,
                jnp.where(lane < 32, pltpu.roll(first, 32, 1), pltpu.roll(second, 32, 1)),
                jnp.where(lane < 64, pltpu.roll(second, 64, 1), pltpu.roll(third, 64, 1)),
                pltpu.roll(third, 96, 1),
            ]
            for index in range(4):
                natural[band, pl.ds(part * 144 + index, GROUPS, stride=4), :] = quarters[index][:GROUPS]
            values = natural[band, part * 144 : part * 144 + 144, :]
            both = jnp.concatenate(halves(values), 1)
            taken = mm(pick, jnp.concatenate([both, filler], 0))
            taken = jnp.where(inside, taken, 0.0).astype(jnp.bfloat16)
            highs.append(taken[:, :128])
            lows.append(taken[:, 128:])
        high = jnp.concatenate(highs, 0)
        spread = jnp.concatenate([high, jnp.concatenate(lows, 0)], 1)
        waves = mm_t(wide_table, spread) + mm_t(low_table, high)
        cosine, sine = waves[:192], waves[192:]
        held[band, :192] = cosine[:, :128] - sine[:, 128:]
        held[band, 192:] = sine[:, :128] + cosine[:, 128:]
    lane = lax.broadcasted_iota(jnp.int32, (8, LANES), 1)
    row = lax.broadcasted_iota(jnp.int32, (8, LANES), 0)
    marks = jnp.zeros((8, LANES), jnp.float32)
    spots = jnp.broadcast_to(ids, (8, LANES))
    for index in range(8):
        marks = jnp.where(row == index, pltpu.roll(spots, STICK_LIMIT - SPARE * index, 1), marks)
    sent = []
    for dest in range(16):
        tail = pieces(held, dest, 11)
        for tile in range(11):
            main = pieces(held, dest, tile)
            if tile < 8:
                extra = pltpu.roll(tail, STICK_LIMIT - SPARE * tile, 1)
            else:
                extra = marks
            packed[dest, tile * 8 : tile * 8 + 8, :] = jnp.where(lane < STICK_LIMIT, main, extra)
        copy = pltpu.make_async_copy(packed.at[dest], out.at[dest], stores.at[dest])
        copy.start()
        sent.append(copy)
    for copy in sent:
        copy.wait()


def density_kernel(
    factors,
    recv,
    inv_y,
    inv_x,
    fwd_y1,
    fwd_y2,
    fwd_x,
    own,
    other,
    columns,
    grid,
    held_re,
    held_im,
    density,
    ids_vector,
    ids,
    arrival,
):
    lane = lax.broadcasted_iota(jnp.int32, (16, LANES), 1)
    marks = jnp.zeros((16, LANES), jnp.float32)
    for index in range(8):
        rolled = pltpu.roll(recv[pl.ds(64 + index, 16, stride=ROWS), :], 15 + SPARE * index, 1)
        marks = jnp.where(lane // SPARE == index, rolled, marks)
    ids_vector[...] = marks.astype(jnp.int32)
    to_scalars = pltpu.make_async_copy(ids_vector, ids, arrival)
    to_scalars.start()
    lane = lane[:8]
    pad = jnp.zeros((32, LANES), jnp.float32)
    for source in range(16):
        first = source * ROWS
        tail = jnp.zeros((8, LANES), jnp.float32)
        for tile in range(8):
            piece = recv[first + tile * 8 : first + tile * 8 + 8, :]
            tail = jnp.where(lane // SPARE == tile, pltpu.roll(piece, 15 + SPARE * tile, 1), tail)
        columns[source] = jnp.concatenate([recv[first : first + ROWS, :], tail, pad], 0).T
    blank = jnp.zeros((48, 128), jnp.float32)
    for row in range(50, 64):
        held_re[pl.ds(row, 48, stride=HELD), :] = blank
        held_im[pl.ds(row, 48, stride=HELD), :] = blank
    grid[...] = jnp.zeros_like(grid)
    to_scalars.wait()

    def put(source, _):
        for stick in range(STICK_LIMIT):
            grid[pl.ds(ids[source, stick], 1), :] = columns[source, stick : stick + 1, :]
        return 0

    lax.fori_loop(0, 16, put, 0, unroll=16)
    lower = lax.broadcasted_iota(jnp.int32, (96, 128), 1) < 64

    def place(pair, _):
        rows = grid[pl.ds(pl.multiple_of(pair * 128, 128), 128), :].T[:96]
        high = rows.astype(jnp.bfloat16).astype(jnp.float32)
        low = pltpu.roll(rows - high, 64, 1)
        for half in range(2):
            mixed = jnp.where(lower, low, high) if half else jnp.where(lower, high, low)
            both = jnp.concatenate([mixed, high], 1).astype(jnp.bfloat16)
            out = mm(both, inv_y[half])
            rows_to = pl.ds(pair * 2 + half, 48, stride=HELD)
            held_re[rows_to, :] = out[:48, :128] - out[48:, 128:]
            held_im[rows_to, :] = out[48:, :128] + out[:48, 128:]
        return 0

    lax.fori_loop(0, 25, place, 0, unroll=25)
    clear = jnp.zeros((2 * SLOTS, 128), jnp.float32)
    for row in range(PLANES, 16):
        own[pl.ds(row, 2 * SLOTS, stride=16), :] = clear
        other[pl.ds(row, 2 * SLOTS, stride=16), :] = clear

    def waves(plane, _):
        even = jnp.zeros((FOLD, 128), jnp.float32)
        odd = jnp.zeros((FOLD, 128), jnp.float32)
        for band in range(4):
            start = pl.multiple_of((band * PLANES + plane) * HELD, HELD)
            rows = pl.ds(start, 64)
            high, low = halves(jnp.concatenate([held_re[rows, :], held_im[rows, :]], 1))
            out = mm(inv_x[...], jnp.concatenate([high, low, high], 0))
            cos_re, cos_im = out[:FOLD, :128], out[:FOLD, 128:]
            sin_re, sin_im = out[FOLD:, :128], out[FOLD:, 128:]
            sums = cos_re * cos_re + cos_im * cos_im + (sin_re * sin_re + sin_im * sin_im)
            even = even + (2.0 * factors[band]) * sums
            odd = odd + (4.0 * factors[band]) * (cos_im * sin_re - cos_re * sin_im)
        start = pl.multiple_of(plane * 2 * FOLD, 2 * FOLD)
        density[pl.ds(start, 2 * FOLD), :] = jnp.concatenate([even, odd], 0)
        return 0

    lax.fori_loop(0, PLANES, waves, 0, unroll=12)

    def forward(group, _):
        start = pl.multiple_of(group * 8 * FOLD, 8 * FOLD)
        high, low = halves(density[pl.ds(start, 8 * FOLD), :])
        rows = mm(jnp.concatenate([high, low], 1), fwd_y1[...]) + mm(high, fwd_y2[...])
        high, low = halves(rows)
        for pair in range(2):
            middle = (4 * pair + 2) * FOLD
            first, second = slice(middle - 2 * FOLD, middle), slice(middle, middle + 2 * FOLD)
            wide_high = jnp.concatenate([high[first], high[second]], 1)
            wide_low = jnp.concatenate([low[first], low[second]], 1)
            out = mm(fwd_x[...], jnp.concatenate([wide_high, wide_low, wide_high], 0))
            for member in range(2):
                plane = group * 4 + pair * 2 + member
                lanes = slice(member * 128, member * 128 + 128)
                cosine = pl.ds(plane, SLOTS, stride=16)
                sine = pl.ds(plane + SIDE_ROWS, SLOTS, stride=16)
                own[cosine, :] = out[0:SLOTS, lanes]
                own[sine, :] = out[32 : 32 + SLOTS, lanes]
                other[cosine, :] = out[64 : 64 + SLOTS, lanes]
                other[sine, :] = out[96 : 96 + SLOTS, lanes]
        return 0

    lax.fori_loop(0, 3, forward, 0, unroll=3)


def force_kernel(
    gx2, own, arrived, base, wave_z, atom_z, near_z, x_all, y_cos, y_sin, strength, out, acc, turn
):
    acc[...] = jnp.zeros_like(acc)
    turn[...] = x_all[...]

    def step(slot, reach, phases):
        start = pl.multiple_of(slot * 16, 16)
        first, second = pl.ds(start, 16), pl.ds(start + SIDE_ROWS, 16)
        pair = [own[first, :] + arrived[first, :], own[second, :] + arrived[second, :]]
        high, low = halves(jnp.concatenate(pair, 1))
        waves = wave_z[...]
        if reach < ZSPAN:
            waves = jnp.concatenate([waves[:reach], waves[ZSPAN : ZSPAN + reach]], 0)
        raw = mm(waves, jnp.concatenate([high, low, high], 0))
        weight = 1.0 / (base[:reach] + gx2[slot])
        weight = jnp.concatenate([weight, weight], 1)
        weight = jnp.concatenate([weight, weight], 0)
        high, low = halves(raw * weight)
        both = mm(phases[...], jnp.concatenate([high, low, high], 0))
        table = turn[...]
        xc_c, xc_s = table[:, 0:1], table[:, 32:33]
        xs_c, xs_s = table[:, 64:65], table[:, 96:97]
        plain_c, plain_s = both[:128, :128], both[:128, 128:]
        acc[0] += xs_c * plain_c + xs_s * plain_s
        acc[1] += xc_c * plain_c + xc_s * plain_s
        acc[2] += xc_c * both[128:, :128] + xc_s * both[128:, 128:]
        turn[...] = pltpu.roll(table, 127, 1)
        return 0

    lax.fori_loop(0, 14, lambda slot, _: step(slot, ZSPAN, atom_z), 0, unroll=14)
    lax.fori_loop(14, SLOTS, lambda slot, _: step(slot, NEAR, near_z), 0, unroll=11)
    parts = [acc[0] * y_cos[...], acc[1] * y_sin[...], acc[2] * y_cos[...]]
    rows = [-strength[...] * jnp.sum(part.T, axis=0, keepdims=True) for part in parts]
    block = jnp.concatenate(rows, 0)
    for index in range(16):
        out[index] = block


def shards(
    coefficients, occupation, kpoint_weight, stick_cell, species, positions, amplitude, core_width
):
    payload = pl.pallas_call(
        send_kernel,
        out_shape=jax.ShapeDtypeStruct((16, ROWS, LANES), jnp.float32),
        in_specs=[HBM] * 3,
        out_specs=HBM,
        scratch_shapes=[
            pltpu.VMEM((1, 144), jnp.int32),
            pltpu.VMEM((4, 2, 13824), jnp.float32),
            pltpu.VMEM((384, 256), jnp.bfloat16),
            pltpu.VMEM((4, 384, LANES), jnp.float32),
            pltpu.VMEM((4, 288, LANES), jnp.float32),
            pltpu.VMEM((4, 3, 80, LANES), jnp.float32),
            pltpu.VMEM((16, ROWS, LANES), jnp.float32),
            pltpu.SemaphoreType.DMA((6,)),
            pltpu.SemaphoreType.DMA((16,)),
        ],
        compiler_params=pltpu.CompilerParams(vmem_limit_bytes=60 * 1024 * 1024),
        name="sticks",
    )(stick_cell[None], coefficients, z_table())
    received = lax.all_to_all(payload, AXES, 0, 0, axis_index_groups=exchange_groups(), tiled=True)
    received = received.reshape(16 * ROWS, LANES)

    core = lax.axis_index("band") % 2
    pool_weight = lax.dynamic_index_in_dim(
        kpoint_weight, lax.axis_index("pool"), keepdims=False
    ).astype(jnp.float32) / jnp.sum(kpoint_weight).astype(jnp.float32)
    factors = pool_weight * occupation[0] * (16.0 / NGRID / 32.0 / NGRID)
    fwd_y1, fwd_y2 = forward_y_tables()
    fwd_x = lax.dynamic_index_in_dim(jnp.asarray(forward_x_tables()), core, keepdims=False)
    halves_shape = jax.ShapeDtypeStruct((2 * SIDE_ROWS, 128), jnp.float32)
    own, other = pl.pallas_call(
        density_kernel,
        out_shape=(halves_shape, halves_shape),
        in_specs=[SMEM] + [VMEM] * 6,
        out_specs=(VMEM, VMEM),
        scratch_shapes=[
            pltpu.VMEM((16, LANES, LANES), jnp.float32),
            pltpu.VMEM((50 * 64, LANES), jnp.float32),
            pltpu.VMEM((48 * HELD, LANES), jnp.float32),
            pltpu.VMEM((48 * HELD, LANES), jnp.float32),
            pltpu.VMEM((PLANES * 2 * FOLD, LANES), jnp.float32),
            pltpu.VMEM((16, LANES), jnp.int32),
            pltpu.SMEM((16, LANES), jnp.int32),
            pltpu.SemaphoreType.DMA,
        ],
        compiler_params=pltpu.CompilerParams(vmem_limit_bytes=40 * 1024 * 1024),
        name="density",
    )(factors, received, inverse_y_tables(), inverse_x_table(), fwd_y1, fwd_y2, fwd_x)
    swap = [(index, index ^ 1) for index in range(8)]
    arrived = lax.ppermute(other, "band", swap)

    rank_z, rank_y = lax.axis_index("fft") // 2, lax.axis_index("fft") % 2
    start = (rank_y * 8 + rank_z) * PLANES
    steps = (jnp.arange(ZSPAN)[:, None] * (start + jnp.arange(PLANES))[None, :]) % NZ
    angles = 2.0 * math.pi / NZ * steps.astype(jnp.float32)
    turned = jnp.pad(jnp.concatenate([jnp.cos(angles), jnp.sin(angles)], 0), ((0, 0), (0, 4)))
    high, low = table_halves(turned)
    wave_z = jnp.concatenate([high, high, low], 1)
    kinds = species[None, :] == jnp.arange(3, dtype=jnp.int32)[:, None]
    width = jnp.sum(jnp.where(kinds, core_width[:, None], 0.0), axis=0)
    strength = jnp.sum(jnp.where(kinds, amplitude[:, None], 0.0), axis=0)

    def tables(where, order, unit, counts):
        waves = unit * order
        turns = where[:, None] * order[None, :]
        phase = 2.0 * math.pi * (turns - jnp.round(turns))
        scale = counts[None, :] * jnp.exp(-0.5 * (width * width)[:, None] * (waves * waves)[None])
        cosine, sine = scale * jnp.cos(phase), scale * jnp.sin(phase)
        slope = waves[None, :]
        return cosine, sine, slope * sine, -slope * cosine

    hx = 2.0 * jnp.arange(32, dtype=jnp.float32) + core.astype(jnp.float32)
    unit = 2.0 * math.pi / 96
    count_x = jnp.where(hx > 48.0, 0.0, jnp.where((hx == 0.0) | (hx == 48.0), 1.0, 2.0))
    x_all = jnp.concatenate(tables(positions[0], hx, unit, count_x), 1)
    hy = jnp.arange(64, dtype=jnp.float32)
    count_y = jnp.where(hy > 48.0, 0.0, jnp.where((hy == 0.0) | (hy == 48.0), 1.0, 2.0))
    y_parts = tables(positions[1], hy, unit, count_y)
    y_cos = jnp.concatenate(y_parts[:2], 1)
    y_sin = jnp.concatenate(y_parts[2:], 1)
    hz = jnp.arange(ZSPAN, dtype=jnp.float32)
    z_parts = tables(positions[2], hz, 2.0 * math.pi / NZ, jnp.where(hz == 0.0, 1.0, 2.0))

    def atom_table(reach):
        plain = jnp.concatenate([part[:, :reach] for part in z_parts[:2]], 1)
        sloped = jnp.concatenate([part[:, :reach] for part in z_parts[2:]], 1)
        high, low = table_halves(jnp.concatenate([plain, sloped], 0))
        return jnp.concatenate([high, high, low], 1)

    gy = np.tile(2.0 * np.pi / 96 * np.arange(64), 2)
    gz = 2.0 * np.pi / NZ * np.arange(ZSPAN)
    base = (gy[None, :] ** 2 + gz[:, None] ** 2 + screen).astype(np.float32)
    gx2 = (unit * hx) * (unit * hx)
    spread = pl.pallas_call(
        force_kernel,
        out_shape=jax.ShapeDtypeStruct((16, 3, LANES), jnp.float32),
        in_specs=[SMEM] + [VMEM] * 10,
        out_specs=VMEM,
        scratch_shapes=[
            pltpu.VMEM((3, 128, 128), jnp.float32),
            pltpu.VMEM((128, 128), jnp.float32),
        ],
        compiler_params=pltpu.CompilerParams(vmem_limit_bytes=40 * 1024 * 1024),
        name="force",
    )(
        gx2,
        own,
        arrived,
        base,
        wave_z,
        atom_table(ZSPAN),
        atom_table(NEAR),
        x_all,
        y_cos,
        y_sin,
        strength[None],
    )
    across, along = reduce_groups()
    total = jnp.sum(lax.all_to_all(spread, AXES, 0, 0, axis_index_groups=across, tiled=True), axis=0)
    spread = jnp.broadcast_to(total[None], (16, 3, LANES))
    return jnp.sum(lax.all_to_all(spread, AXES, 0, 0, axis_index_groups=along, tiled=True), axis=0)


def solution(mesh):
    placed = (P("pool", "band", None, "fft"), P("pool", "band"), P(), P("fft"), P(), P(), P(), P())
    return jax.shard_map(shards, mesh=mesh, in_specs=placed, out_specs=P(), check_vma=False)
```

```python
import math

import jax
import jax.numpy as jnp
import numpy as np
from jax import lax
from jax.experimental import pallas as pl
from jax.experimental.pallas import tpu as pltpu
from jax.sharding import PartitionSpec as P

NX = 96
NY = 96
NZ = 192
ZSPAN = 96
NGRID = 1769472
HALF = 24
SIDE = 49
LANES = 128
PLANES = 12
SLOTS = 25
SIDE_ROWS = SLOTS * 16
STICK_LIMIT = 113
SPARE = 15
ROWS = 88
NEAR = 80
HELD = 72
FOLD = 56
GROUPS = 36
SPARE_ROW = SIDE * 64
HIGH = lax.Precision.HIGH
screen = 0.25
AXES = ("pool", "band", "fft")
VMEM = pl.BlockSpec(memory_space=pltpu.VMEM)
HBM = pl.BlockSpec(memory_space=pltpu.HBM)
SMEM = pl.BlockSpec(memory_space=pltpu.SMEM)


def trig(rows, columns, length):
    angles = 2.0 * np.pi / length * (np.outer(rows, columns) % length)
    return np.cos(angles).astype(np.float32), np.sin(angles).astype(np.float32)


def exchange_groups():
    ranks = np.arange(256).reshape(16, 8, 2)
    return ranks.transpose(0, 2, 1).reshape(16, 16).tolist()


def reduce_groups():
    ranks = np.arange(256).reshape(2, 4, 2, 8, 2)
    across = ranks.transpose(3, 2, 0, 4, 1).reshape(16, 16)
    along = ranks.transpose(0, 4, 1, 3, 2).reshape(16, 16)
    return across.tolist(), along.tolist()


def halves(values):
    high = values.astype(jnp.bfloat16)
    return high, (values - high.astype(jnp.float32)).astype(jnp.bfloat16)


def table_halves(values):
    high = lax.reduce_precision(values, 8, 7)
    return high.astype(jnp.bfloat16), (values - high).astype(jnp.bfloat16)


def np_halves(values):
    high = values.astype(jnp.bfloat16)
    return high, (values - high.astype(np.float32)).astype(jnp.bfloat16)


def mm(left, right):
    return jnp.dot(left, right, preferred_element_type=jnp.float32)


def z_table():
    both = np.zeros((2, NZ, LANES), np.float32)
    both[:, :, :ZSPAN] = trig(np.arange(NZ), np.arange(ZSPAN) - NZ // 4, NZ)
    return np.concatenate(np_halves(both.reshape(2 * NZ, LANES)), 1)


def inverse_y_tables():
    cosine, sine = trig(np.arange(SIDE) - HALF, np.arange(96), 96)
    both = np.zeros((SIDE, 256), np.float32)
    both[:, :96], both[:, 128:224] = cosine, sine
    high, low = np_halves(both)
    table = np.zeros((2, 256, 256), high.dtype)
    for half in range(2):
        for part in range(2):
            table[half, 64 * part : 64 * part + SIDE] = high
        table[half, 128 + 64 * half : 128 + 64 * half + SIDE] = low
    return table


def inverse_x_table():
    cosine, sine = trig(np.arange(SIDE), np.arange(SIDE) - HALF, 96)
    both = np.zeros((2 * FOLD, 64), np.float32)
    both[:SIDE, :SIDE], both[FOLD : FOLD + SIDE, :SIDE] = cosine, sine
    high, low = np_halves(both)
    return np.concatenate([high, high, low], 1)


def forward_y_tables():
    cosine, sine = trig(np.arange(96), np.arange(SIDE), 96)
    both = np.zeros((128, 128), np.float32)
    both[:96, :SIDE], both[:96, 64 : 64 + SIDE] = cosine, sine
    high, low = np_halves(both)
    return np.concatenate([high, high], 0), low


def forward_x_tables():
    cosine, sine = trig(np.arange(50), np.arange(SIDE), 96)
    cosine[SIDE:], sine[SIDE:] = 0.0, 0.0
    cosine[:, 0], cosine[:, 48] = cosine[:, 0] / 2, cosine[:, 48] / 2
    result = []
    for core in range(2):
        both = np.zeros((128, 2 * FOLD), np.float32)
        for index, rows in enumerate((core, 1 - core)):
            both[64 * index : 64 * index + SLOTS, :SIDE] = cosine[rows::2]
            both[64 * index + 32 : 64 * index + 32 + SLOTS, FOLD : FOLD + SIDE] = sine[rows::2]
        high, low = np_halves(both)
        result.append(np.concatenate([high, high, low], 1))
    return np.stack(result)


def mm_t(left, right):
    return lax.dot_general(
        left, right, (((1,), (1,)), ((), ())), preferred_element_type=jnp.float32
    )


def small(flags):
    return flags.astype(jnp.float32).astype(jnp.bfloat16)


def pieces(held, dest, tile):
    found = []
    for row in range(tile * 8, tile * 8 + 8, 4):
        start = (row // 48) * 192 + dest * PLANES + row % 12
        found.append(held[(row % 48) // 12, start : start + 4, :])
    return jnp.concatenate(found, 0)


def send_kernel(
    cells, coefs, z_waves, out, place, raw, table, held, natural, rows, packed, loads, stores
):
    copies = [
        pltpu.make_async_copy(coefs.at[0, band], raw.at[band], loads.at[band]) for band in range(4)
    ]
    copies.append(pltpu.make_async_copy(z_waves, table, loads.at[4]))
    where = pltpu.make_async_copy(cells, place, loads.at[5])
    where.start()
    for copy in copies:
        copy.start()
    where.wait()
    for copy in copies:
        copy.wait()
    stick = jnp.concatenate([place[...], jnp.full((1, 112), 48 * NY, jnp.int32)], 1)
    stick = jnp.broadcast_to(stick, (8, 256))
    column = stick // NY
    freq_x = jnp.where(column < 48, column, column - NX)
    freq_y = stick - column * NY
    freq_y = jnp.where(freq_y < 48, freq_y, freq_y - NY)
    reach = freq_x * freq_x + freq_y * freq_y
    chosen = reach <= HALF * HALF
    earlier = lax.broadcasted_iota(jnp.int32, (256, 256), 0)
    earlier = earlier < lax.broadcasted_iota(jnp.int32, (256, 256), 1)
    rank = mm(chosen.astype(jnp.float32).astype(jnp.bfloat16), small(earlier))
    order = lax.broadcasted_iota(jnp.int32, (LANES, 256), 0).astype(jnp.float32)
    pick = small((rank[0:1] == order) & chosen[0:1])
    line = lax.broadcasted_iota(jnp.int32, (8, 256), 0)
    facts = jnp.where(line == 0, (freq_x + HALF) * 64, jnp.where(line == 1, freq_y + HALF, 1))
    facts = mm_t(facts.astype(jnp.float32).astype(jnp.bfloat16), pick)
    ids = facts[0:1] + facts[1:2] + SPARE_ROW * (1.0 - facts[2:3])
    coarse = reach // 16 * 16
    spread = [jnp.broadcast_to(part[0:1], (LANES, 256)) for part in (coarse, reach - coarse)]
    level = sum(mm_t(pick, part.astype(jnp.float32).astype(jnp.bfloat16)) for part in spread)
    slot = lax.broadcasted_iota(jnp.int32, (LANES, LANES), 1)
    freq_z = (slot - NZ // 4).astype(jnp.float32)
    inside = (16.0 * level + 4.0 * freq_z * freq_z <= NX * NX) & (slot < ZSPAN)
    inside = jnp.concatenate([inside, inside], 1)
    high_table = table[:, :LANES]
    wide_table = jnp.concatenate([high_table, high_table], 1)
    low_table = table[:, LANES:]
    lane = lax.broadcasted_iota(jnp.int32, (40, LANES), 1)
    filler = jnp.zeros((112, 256), jnp.bfloat16)
    for band in range(4):
        highs, lows = [], []
        for chunk in range(3 * GROUPS):
            piece = raw[band, :, chunk * LANES : (chunk + 1) * LANES]
            for part in range(2):
                start = part * 40 + chunk // 3
                rows[band, chunk % 3, start : start + 1, :] = piece[part : part + 1]
        for part in range(2):
            span = slice(part * 40, part * 40 + 40)
            first, second, third = rows[band, 0, span, :], rows[band, 1, span, :], rows[band, 2, span, :]
            quarters = [
                first,
                jnp.where(lane < 32, pltpu.roll(first, 32, 1), pltpu.roll(second, 32, 1)),
                jnp.where(lane < 64, pltpu.roll(second, 64, 1), pltpu.roll(third, 64, 1)),
                pltpu.roll(third, 96, 1),
            ]
            for index in range(4):
                natural[band, pl.ds(part * 144 + index, GROUPS, stride=4), :] = quarters[index][:GROUPS]
            values = natural[band, part * 144 : part * 144 + 144, :]
            both = jnp.concatenate(halves(values), 1)
            taken = mm(pick, jnp.concatenate([both, filler], 0))
            taken = jnp.where(inside, taken, 0.0).astype(jnp.bfloat16)
            highs.append(taken[:, :128])
            lows.append(taken[:, 128:])
        high = jnp.concatenate(highs, 0)
        spread = jnp.concatenate([high, jnp.concatenate(lows, 0)], 1)
        waves = mm_t(wide_table, spread) + mm_t(low_table, high)
        cosine, sine = waves[:192], waves[192:]
        held[band, :192] = cosine[:, :128] - sine[:, 128:]
        held[band, 192:] = sine[:, :128] + cosine[:, 128:]
    lane = lax.broadcasted_iota(jnp.int32, (8, LANES), 1)
    row = lax.broadcasted_iota(jnp.int32, (8, LANES), 0)
    marks = jnp.zeros((8, LANES), jnp.float32)
    spots = jnp.broadcast_to(ids, (8, LANES))
    for index in range(8):
        marks = jnp.where(row == index, pltpu.roll(spots, STICK_LIMIT - SPARE * index, 1), marks)
    sent = []
    for dest in range(16):
        tail = pieces(held, dest, 11)
        for tile in range(11):
            main = pieces(held, dest, tile)
            if tile < 8:
                extra = pltpu.roll(tail, STICK_LIMIT - SPARE * tile, 1)
            else:
                extra = marks
            packed[dest, tile * 8 : tile * 8 + 8, :] = jnp.where(lane < STICK_LIMIT, main, extra)
        copy = pltpu.make_async_copy(packed.at[dest], out.at[dest], stores.at[dest])
        copy.start()
        sent.append(copy)
    for copy in sent:
        copy.wait()


def density_kernel(
    factors,
    recv,
    inv_y,
    inv_x,
    fwd_y1,
    fwd_y2,
    fwd_x,
    own,
    other,
    columns,
    grid,
    held_re,
    held_im,
    density,
    ids_vector,
    ids,
    arrival,
):
    lane = lax.broadcasted_iota(jnp.int32, (16, LANES), 1)
    marks = jnp.zeros((16, LANES), jnp.float32)
    for index in range(8):
        rolled = pltpu.roll(recv[pl.ds(64 + index, 16, stride=ROWS), :], 15 + SPARE * index, 1)
        marks = jnp.where(lane // SPARE == index, rolled, marks)
    ids_vector[...] = marks.astype(jnp.int32)
    to_scalars = pltpu.make_async_copy(ids_vector, ids, arrival)
    to_scalars.start()
    lane = lane[:8]
    pad = jnp.zeros((32, LANES), jnp.float32)
    for source in range(16):
        first = source * ROWS
        tail = jnp.zeros((8, LANES), jnp.float32)
        for tile in range(8):
            piece = recv[first + tile * 8 : first + tile * 8 + 8, :]
            tail = jnp.where(lane // SPARE == tile, pltpu.roll(piece, 15 + SPARE * tile, 1), tail)
        columns[source] = jnp.concatenate([recv[first : first + ROWS, :], tail, pad], 0).T
    blank = jnp.zeros((48, 128), jnp.float32)
    for row in range(50, 64):
        held_re[pl.ds(row, 48, stride=HELD), :] = blank
        held_im[pl.ds(row, 48, stride=HELD), :] = blank
    grid[...] = jnp.zeros_like(grid)
    to_scalars.wait()

    def put(source, _):
        for stick in range(STICK_LIMIT):
            grid[pl.ds(ids[source, stick], 1), :] = columns[source, stick : stick + 1, :]
        return 0

    lax.fori_loop(0, 16, put, 0, unroll=16)
    lower = lax.broadcasted_iota(jnp.int32, (96, 128), 1) < 64

    def place(pair, _):
        rows = grid[pl.ds(pl.multiple_of(pair * 128, 128), 128), :].T[:96]
        high = rows.astype(jnp.bfloat16).astype(jnp.float32)
        low = pltpu.roll(rows - high, 64, 1)
        for half in range(2):
            mixed = jnp.where(lower, low, high) if half else jnp.where(lower, high, low)
            both = jnp.concatenate([mixed, high], 1).astype(jnp.bfloat16)
            out = mm(both, inv_y[half])
            rows_to = pl.ds(pair * 2 + half, 48, stride=HELD)
            held_re[rows_to, :] = out[:48, :128] - out[48:, 128:]
            held_im[rows_to, :] = out[48:, :128] + out[:48, 128:]
        return 0

    lax.fori_loop(0, 25, place, 0, unroll=25)
    clear = jnp.zeros((2 * SLOTS, 128), jnp.float32)
    for row in range(PLANES, 16):
        own[pl.ds(row, 2 * SLOTS, stride=16), :] = clear
        other[pl.ds(row, 2 * SLOTS, stride=16), :] = clear

    def waves(plane, _):
        even = jnp.zeros((FOLD, 128), jnp.float32)
        odd = jnp.zeros((FOLD, 128), jnp.float32)
        for band in range(4):
            start = pl.multiple_of((band * PLANES + plane) * HELD, HELD)
            rows = pl.ds(start, 64)
            high, low = halves(jnp.concatenate([held_re[rows, :], held_im[rows, :]], 1))
            out = mm(inv_x[...], jnp.concatenate([high, low, high], 0))
            cos_re, cos_im = out[:FOLD, :128], out[:FOLD, 128:]
            sin_re, sin_im = out[FOLD:, :128], out[FOLD:, 128:]
            sums = cos_re * cos_re + cos_im * cos_im + (sin_re * sin_re + sin_im * sin_im)
            even = even + (2.0 * factors[band]) * sums
            odd = odd + (4.0 * factors[band]) * (cos_im * sin_re - cos_re * sin_im)
        start = pl.multiple_of(plane * 2 * FOLD, 2 * FOLD)
        density[pl.ds(start, 2 * FOLD), :] = jnp.concatenate([even, odd], 0)
        return 0

    lax.fori_loop(0, PLANES, waves, 0, unroll=12)

    def forward(group, _):
        start = pl.multiple_of(group * 8 * FOLD, 8 * FOLD)
        high, low = halves(density[pl.ds(start, 8 * FOLD), :])
        rows = mm(jnp.concatenate([high, low], 1), fwd_y1[...]) + mm(high, fwd_y2[...])
        high, low = halves(rows)
        for pair in range(2):
            middle = (4 * pair + 2) * FOLD
            first, second = slice(middle - 2 * FOLD, middle), slice(middle, middle + 2 * FOLD)
            wide_high = jnp.concatenate([high[first], high[second]], 1)
            wide_low = jnp.concatenate([low[first], low[second]], 1)
            out = mm(fwd_x[...], jnp.concatenate([wide_high, wide_low, wide_high], 0))
            for member in range(2):
                plane = group * 4 + pair * 2 + member
                lanes = slice(member * 128, member * 128 + 128)
                cosine = pl.ds(plane, SLOTS, stride=16)
                sine = pl.ds(plane + SIDE_ROWS, SLOTS, stride=16)
                own[cosine, :] = out[0:SLOTS, lanes]
                own[sine, :] = out[32 : 32 + SLOTS, lanes]
                other[cosine, :] = out[64 : 64 + SLOTS, lanes]
                other[sine, :] = out[96 : 96 + SLOTS, lanes]
        return 0

    lax.fori_loop(0, 3, forward, 0, unroll=3)


def force_kernel(
    gx2, own, arrived, base, wave_z, atom_z, near_z, x_all, y_cos, y_sin, strength, out, acc, turn
):
    acc[...] = jnp.zeros_like(acc)
    turn[...] = x_all[...]

    def step(slot, reach, phases):
        start = pl.multiple_of(slot * 16, 16)
        first, second = pl.ds(start, 16), pl.ds(start + SIDE_ROWS, 16)
        pair = [own[first, :] + arrived[first, :], own[second, :] + arrived[second, :]]
        high, low = halves(jnp.concatenate(pair, 1))
        waves = wave_z[...]
        if reach < ZSPAN:
            waves = jnp.concatenate([waves[:reach], waves[ZSPAN : ZSPAN + reach]], 0)
        raw = mm(waves, jnp.concatenate([high, low, high], 0))
        weight = 1.0 / (base[:reach] + gx2[slot])
        weight = jnp.concatenate([weight, weight], 1)
        weight = jnp.concatenate([weight, weight], 0)
        high, low = halves(raw * weight)
        both = mm(phases[...], jnp.concatenate([high, low, high], 0))
        table = turn[...]
        xc_c, xc_s = table[:, 0:1], table[:, 32:33]
        xs_c, xs_s = table[:, 64:65], table[:, 96:97]
        plain_c, plain_s = both[:128, :128], both[:128, 128:]
        acc[0] += xs_c * plain_c + xs_s * plain_s
        acc[1] += xc_c * plain_c + xc_s * plain_s
        acc[2] += xc_c * both[128:, :128] + xc_s * both[128:, 128:]
        turn[...] = pltpu.roll(table, 127, 1)
        return 0

    lax.fori_loop(0, 14, lambda slot, _: step(slot, ZSPAN, atom_z), 0, unroll=14)
    lax.fori_loop(14, SLOTS, lambda slot, _: step(slot, NEAR, near_z), 0, unroll=11)
    parts = [acc[0] * y_cos[...], acc[1] * y_sin[...], acc[2] * y_cos[...]]
    rows = [-strength[...] * jnp.sum(part.T, axis=0, keepdims=True) for part in parts]
    block = jnp.concatenate(rows, 0)
    for index in range(16):
        out[index] = block


def shards(
    coefficients, occupation, kpoint_weight, stick_cell, species, positions, amplitude, core_width
):
    payload = pl.pallas_call(
        send_kernel,
        out_shape=jax.ShapeDtypeStruct((16, ROWS, LANES), jnp.float32),
        in_specs=[HBM] * 3,
        out_specs=HBM,
        scratch_shapes=[
            pltpu.VMEM((1, 144), jnp.int32),
            pltpu.VMEM((4, 2, 13824), jnp.float32),
            pltpu.VMEM((384, 256), jnp.bfloat16),
            pltpu.VMEM((4, 384, LANES), jnp.float32),
            pltpu.VMEM((4, 288, LANES), jnp.float32),
            pltpu.VMEM((4, 3, 80, LANES), jnp.float32),
            pltpu.VMEM((16, ROWS, LANES), jnp.float32),
            pltpu.SemaphoreType.DMA((6,)),
            pltpu.SemaphoreType.DMA((16,)),
        ],
        compiler_params=pltpu.CompilerParams(vmem_limit_bytes=60 * 1024 * 1024),
        name="sticks",
    )(stick_cell[None], coefficients, z_table())
    received = lax.all_to_all(payload, AXES, 0, 0, axis_index_groups=exchange_groups(), tiled=True)
    received = received.reshape(16 * ROWS, LANES)

    core = lax.axis_index("band") % 2
    pool_weight = lax.dynamic_index_in_dim(
        kpoint_weight, lax.axis_index("pool"), keepdims=False
    ).astype(jnp.float32) / jnp.sum(kpoint_weight).astype(jnp.float32)
    factors = pool_weight * occupation[0] * (16.0 / NGRID / 32.0 / NGRID)
    fwd_y1, fwd_y2 = forward_y_tables()
    fwd_x = lax.dynamic_index_in_dim(jnp.asarray(forward_x_tables()), core, keepdims=False)
    halves_shape = jax.ShapeDtypeStruct((2 * SIDE_ROWS, 128), jnp.float32)
    own, other = pl.pallas_call(
        density_kernel,
        out_shape=(halves_shape, halves_shape),
        in_specs=[SMEM] + [VMEM] * 6,
        out_specs=(VMEM, VMEM),
        scratch_shapes=[
            pltpu.VMEM((16, LANES, LANES), jnp.float32),
            pltpu.VMEM((50 * 64, LANES), jnp.float32),
            pltpu.VMEM((48 * HELD, LANES), jnp.float32),
            pltpu.VMEM((48 * HELD, LANES), jnp.float32),
            pltpu.VMEM((PLANES * 2 * FOLD, LANES), jnp.float32),
            pltpu.VMEM((16, LANES), jnp.int32),
            pltpu.SMEM((16, LANES), jnp.int32),
            pltpu.SemaphoreType.DMA,
        ],
        compiler_params=pltpu.CompilerParams(vmem_limit_bytes=40 * 1024 * 1024),
        name="density",
    )(factors, received, inverse_y_tables(), inverse_x_table(), fwd_y1, fwd_y2, fwd_x)
    swap = [(index, index ^ 1) for index in range(8)]
    arrived = lax.ppermute(other, "band", swap)

    rank_z, rank_y = lax.axis_index("fft") // 2, lax.axis_index("fft") % 2
    start = (rank_y * 8 + rank_z) * PLANES
    steps = (jnp.arange(ZSPAN)[:, None] * (start + jnp.arange(PLANES))[None, :]) % NZ
    angles = 2.0 * math.pi / NZ * steps.astype(jnp.float32)
    turned = jnp.pad(jnp.concatenate([jnp.cos(angles), jnp.sin(angles)], 0), ((0, 0), (0, 4)))
    high, low = table_halves(turned)
    wave_z = jnp.concatenate([high, high, low], 1)
    kinds = species[None, :] == jnp.arange(3, dtype=jnp.int32)[:, None]
    width = jnp.sum(jnp.where(kinds, core_width[:, None], 0.0), axis=0)
    strength = jnp.sum(jnp.where(kinds, amplitude[:, None], 0.0), axis=0)

    def tables(where, order, unit, counts):
        waves = unit * order
        turns = where[:, None] * order[None, :]
        phase = 2.0 * math.pi * (turns - jnp.round(turns))
        scale = counts[None, :] * jnp.exp(-0.5 * (width * width)[:, None] * (waves * waves)[None])
        cosine, sine = scale * jnp.cos(phase), scale * jnp.sin(phase)
        slope = waves[None, :]
        return cosine, sine, slope * sine, -slope * cosine

    hx = 2.0 * jnp.arange(32, dtype=jnp.float32) + core.astype(jnp.float32)
    unit = 2.0 * math.pi / 96
    count_x = jnp.where(hx > 48.0, 0.0, jnp.where((hx == 0.0) | (hx == 48.0), 1.0, 2.0))
    x_all = jnp.concatenate(tables(positions[0], hx, unit, count_x), 1)
    hy = jnp.arange(64, dtype=jnp.float32)
    count_y = jnp.where(hy > 48.0, 0.0, jnp.where((hy == 0.0) | (hy == 48.0), 1.0, 2.0))
    y_parts = tables(positions[1], hy, unit, count_y)
    y_cos = jnp.concatenate(y_parts[:2], 1)
    y_sin = jnp.concatenate(y_parts[2:], 1)
    hz = jnp.arange(ZSPAN, dtype=jnp.float32)
    z_parts = tables(positions[2], hz, 2.0 * math.pi / NZ, jnp.where(hz == 0.0, 1.0, 2.0))

    def atom_table(reach):
        plain = jnp.concatenate([part[:, :reach] for part in z_parts[:2]], 1)
        sloped = jnp.concatenate([part[:, :reach] for part in z_parts[2:]], 1)
        high, low = table_halves(jnp.concatenate([plain, sloped], 0))
        return jnp.concatenate([high, high, low], 1)

    gy = np.tile(2.0 * np.pi / 96 * np.arange(64), 2)
    gz = 2.0 * np.pi / NZ * np.arange(ZSPAN)
    base = (gy[None, :] ** 2 + gz[:, None] ** 2 + screen).astype(np.float32)
    gx2 = (unit * hx) * (unit * hx)
    spread = pl.pallas_call(
        force_kernel,
        out_shape=jax.ShapeDtypeStruct((16, 3, LANES), jnp.float32),
        in_specs=[SMEM] + [VMEM] * 10,
        out_specs=VMEM,
        scratch_shapes=[
            pltpu.VMEM((3, 128, 128), jnp.float32),
            pltpu.VMEM((128, 128), jnp.float32),
        ],
        compiler_params=pltpu.CompilerParams(vmem_limit_bytes=40 * 1024 * 1024),
        name="force",
    )(
        gx2,
        own,
        arrived,
        base,
        wave_z,
        atom_table(ZSPAN),
        atom_table(NEAR),
        x_all,
        y_cos,
        y_sin,
        strength[None],
    )
    along, across = reduce_groups()
    total = jnp.sum(lax.all_to_all(spread, AXES, 0, 0, axis_index_groups=across, tiled=True), axis=0)
    spread = jnp.broadcast_to(total[None], (16, 3, LANES))
    return jnp.sum(lax.all_to_all(spread, AXES, 0, 0, axis_index_groups=along, tiled=True), axis=0)


def solution(mesh):
    placed = (P("pool", "band", None, "fft"), P("pool", "band"), P(), P("fft"), P(), P(), P(), P())
    return jax.shard_map(shards, mesh=mesh, in_specs=placed, out_specs=P(), check_vma=False)
```

```python
import math

import jax
import jax.numpy as jnp
import numpy as np
from jax import lax
from jax.experimental import pallas as pl
from jax.experimental.pallas import tpu as pltpu
from jax.sharding import PartitionSpec as P

NX = 96
NY = 96
NZ = 192
ZSPAN = 96
NGRID = 1769472
HALF = 24
SIDE = 49
LANES = 128
PLANES = 12
SLOTS = 25
SIDE_ROWS = SLOTS * 16
STICK_LIMIT = 113
SPARE = 15
ROWS = 88
NEAR = 80
HELD = 72
FOLD = 56
GROUPS = 36
SPARE_ROW = SIDE * 64
HIGH = lax.Precision.HIGH
screen = 0.25
AXES = ("pool", "band", "fft")
VMEM = pl.BlockSpec(memory_space=pltpu.VMEM)
HBM = pl.BlockSpec(memory_space=pltpu.HBM)
SMEM = pl.BlockSpec(memory_space=pltpu.SMEM)


def trig(rows, columns, length):
    angles = 2.0 * np.pi / length * (np.outer(rows, columns) % length)
    return np.cos(angles).astype(np.float32), np.sin(angles).astype(np.float32)


def exchange_groups():
    ranks = np.arange(256).reshape(16, 8, 2)
    return ranks.transpose(0, 2, 1).reshape(16, 16).tolist()


def reduce_groups():
    ranks = np.arange(256).reshape(2, 4, 2, 8, 2)
    across = ranks.transpose(3, 2, 4, 0, 1).reshape(16, 16)
    along = ranks.transpose(0, 1, 4, 2, 3).reshape(16, 16)
    return across.tolist(), along.tolist()


def halves(values):
    high = values.astype(jnp.bfloat16)
    return high, (values - high.astype(jnp.float32)).astype(jnp.bfloat16)


def table_halves(values):
    high = lax.reduce_precision(values, 8, 7)
    return high.astype(jnp.bfloat16), (values - high).astype(jnp.bfloat16)


def np_halves(values):
    high = values.astype(jnp.bfloat16)
    return high, (values - high.astype(np.float32)).astype(jnp.bfloat16)


def mm(left, right):
    return jnp.dot(left, right, preferred_element_type=jnp.float32)


def z_table():
    both = np.zeros((2, NZ, LANES), np.float32)
    both[:, :, :ZSPAN] = trig(np.arange(NZ), np.arange(ZSPAN) - NZ // 4, NZ)
    return np.concatenate(np_halves(both.reshape(2 * NZ, LANES)), 1)


def inverse_y_tables():
    cosine, sine = trig(np.arange(SIDE) - HALF, np.arange(96), 96)
    both = np.zeros((SIDE, 256), np.float32)
    both[:, :96], both[:, 128:224] = cosine, sine
    high, low = np_halves(both)
    table = np.zeros((2, 256, 256), high.dtype)
    for half in range(2):
        for part in range(2):
            table[half, 64 * part : 64 * part + SIDE] = high
        table[half, 128 + 64 * half : 128 + 64 * half + SIDE] = low
    return table


def inverse_x_table():
    cosine, sine = trig(np.arange(SIDE), np.arange(SIDE) - HALF, 96)
    both = np.zeros((2 * FOLD, 64), np.float32)
    both[:SIDE, :SIDE], both[FOLD : FOLD + SIDE, :SIDE] = cosine, sine
    high, low = np_halves(both)
    return np.concatenate([high, high, low], 1)


def forward_y_tables():
    cosine, sine = trig(np.arange(96), np.arange(SIDE), 96)
    both = np.zeros((128, 128), np.float32)
    both[:96, :SIDE], both[:96, 64 : 64 + SIDE] = cosine, sine
    high, low = np_halves(both)
    return np.concatenate([high, high], 0), low


def forward_x_tables():
    cosine, sine = trig(np.arange(50), np.arange(SIDE), 96)
    cosine[SIDE:], sine[SIDE:] = 0.0, 0.0
    cosine[:, 0], cosine[:, 48] = cosine[:, 0] / 2, cosine[:, 48] / 2
    result = []
    for core in range(2):
        both = np.zeros((128, 2 * FOLD), np.float32)
        for index, rows in enumerate((core, 1 - core)):
            both[64 * index : 64 * index + SLOTS, :SIDE] = cosine[rows::2]
            both[64 * index + 32 : 64 * index + 32 + SLOTS, FOLD : FOLD + SIDE] = sine[rows::2]
        high, low = np_halves(both)
        result.append(np.concatenate([high, high, low], 1))
    return np.stack(result)


def mm_t(left, right):
    return lax.dot_general(
        left, right, (((1,), (1,)), ((), ())), preferred_element_type=jnp.float32
    )


def small(flags):
    return flags.astype(jnp.float32).astype(jnp.bfloat16)


def pieces(held, dest, tile):
    found = []
    for row in range(tile * 8, tile * 8 + 8, 4):
        start = (row // 48) * 192 + dest * PLANES + row % 12
        found.append(held[(row % 48) // 12, start : start + 4, :])
    return jnp.concatenate(found, 0)


def send_kernel(
    cells, coefs, z_waves, out, place, raw, table, held, natural, rows, packed, loads, stores
):
    copies = [
        pltpu.make_async_copy(coefs.at[0, band], raw.at[band], loads.at[band]) for band in range(4)
    ]
    copies.append(pltpu.make_async_copy(z_waves, table, loads.at[4]))
    where = pltpu.make_async_copy(cells, place, loads.at[5])
    where.start()
    for copy in copies:
        copy.start()
    where.wait()
    for copy in copies:
        copy.wait()
    stick = jnp.concatenate([place[...], jnp.full((1, 112), 48 * NY, jnp.int32)], 1)
    stick = jnp.broadcast_to(stick, (8, 256))
    column = stick // NY
    freq_x = jnp.where(column < 48, column, column - NX)
    freq_y = stick - column * NY
    freq_y = jnp.where(freq_y < 48, freq_y, freq_y - NY)
    reach = freq_x * freq_x + freq_y * freq_y
    chosen = reach <= HALF * HALF
    earlier = lax.broadcasted_iota(jnp.int32, (256, 256), 0)
    earlier = earlier < lax.broadcasted_iota(jnp.int32, (256, 256), 1)
    rank = mm(chosen.astype(jnp.float32).astype(jnp.bfloat16), small(earlier))
    order = lax.broadcasted_iota(jnp.int32, (LANES, 256), 0).astype(jnp.float32)
    pick = small((rank[0:1] == order) & chosen[0:1])
    line = lax.broadcasted_iota(jnp.int32, (8, 256), 0)
    facts = jnp.where(line == 0, (freq_x + HALF) * 64, jnp.where(line == 1, freq_y + HALF, 1))
    facts = mm_t(facts.astype(jnp.float32).astype(jnp.bfloat16), pick)
    ids = facts[0:1] + facts[1:2] + SPARE_ROW * (1.0 - facts[2:3])
    coarse = reach // 16 * 16
    spread = [jnp.broadcast_to(part[0:1], (LANES, 256)) for part in (coarse, reach - coarse)]
    level = sum(mm_t(pick, part.astype(jnp.float32).astype(jnp.bfloat16)) for part in spread)
    slot = lax.broadcasted_iota(jnp.int32, (LANES, LANES), 1)
    freq_z = (slot - NZ // 4).astype(jnp.float32)
    inside = (16.0 * level + 4.0 * freq_z * freq_z <= NX * NX) & (slot < ZSPAN)
    inside = jnp.concatenate([inside, inside], 1)
    high_table = table[:, :LANES]
    wide_table = jnp.concatenate([high_table, high_table], 1)
    low_table = table[:, LANES:]
    lane = lax.broadcasted_iota(jnp.int32, (40, LANES), 1)
    filler = jnp.zeros((112, 256), jnp.bfloat16)
    for band in range(4):
        highs, lows = [], []
        for chunk in range(3 * GROUPS):
            piece = raw[band, :, chunk * LANES : (chunk + 1) * LANES]
            for part in range(2):
                start = part * 40 + chunk // 3
                rows[band, chunk % 3, start : start + 1, :] = piece[part : part + 1]
        for part in range(2):
            span = slice(part * 40, part * 40 + 40)
            first, second, third = rows[band, 0, span, :], rows[band, 1, span, :], rows[band, 2, span, :]
            quarters = [
                first,
                jnp.where(lane < 32, pltpu.roll(first, 32, 1), pltpu.roll(second, 32, 1)),
                jnp.where(lane < 64, pltpu.roll(second, 64, 1), pltpu.roll(third, 64, 1)),
                pltpu.roll(third, 96, 1),
            ]
            for index in range(4):
                natural[band, pl.ds(part * 144 + index, GROUPS, stride=4), :] = quarters[index][:GROUPS]
            values = natural[band, part * 144 : part * 144 + 144, :]
            both = jnp.concatenate(halves(values), 1)
            taken = mm(pick, jnp.concatenate([both, filler], 0))
            taken = jnp.where(inside, taken, 0.0).astype(jnp.bfloat16)
            highs.append(taken[:, :128])
            lows.append(taken[:, 128:])
        high = jnp.concatenate(highs, 0)
        spread = jnp.concatenate([high, jnp.concatenate(lows, 0)], 1)
        waves = mm_t(wide_table, spread) + mm_t(low_table, high)
        cosine, sine = waves[:192], waves[192:]
        held[band, :192] = cosine[:, :128] - sine[:, 128:]
        held[band, 192:] = sine[:, :128] + cosine[:, 128:]
    lane = lax.broadcasted_iota(jnp.int32, (8, LANES), 1)
    row = lax.broadcasted_iota(jnp.int32, (8, LANES), 0)
    marks = jnp.zeros((8, LANES), jnp.float32)
    spots = jnp.broadcast_to(ids, (8, LANES))
    for index in range(8):
        marks = jnp.where(row == index, pltpu.roll(spots, STICK_LIMIT - SPARE * index, 1), marks)
    sent = []
    for dest in range(16):
        tail = pieces(held, dest, 11)
        for tile in range(11):
            main = pieces(held, dest, tile)
            if tile < 8:
                extra = pltpu.roll(tail, STICK_LIMIT - SPARE * tile, 1)
            else:
                extra = marks
            packed[dest, tile * 8 : tile * 8 + 8, :] = jnp.where(lane < STICK_LIMIT, main, extra)
        copy = pltpu.make_async_copy(packed.at[dest], out.at[dest], stores.at[dest])
        copy.start()
        sent.append(copy)
    for copy in sent:
        copy.wait()


def density_kernel(
    factors,
    recv,
    inv_y,
    inv_x,
    fwd_y1,
    fwd_y2,
    fwd_x,
    own,
    other,
    columns,
    grid,
    held_re,
    held_im,
    density,
    ids_vector,
    ids,
    arrival,
):
    lane = lax.broadcasted_iota(jnp.int32, (16, LANES), 1)
    marks = jnp.zeros((16, LANES), jnp.float32)
    for index in range(8):
        rolled = pltpu.roll(recv[pl.ds(64 + index, 16, stride=ROWS), :], 15 + SPARE * index, 1)
        marks = jnp.where(lane // SPARE == index, rolled, marks)
    ids_vector[...] = marks.astype(jnp.int32)
    to_scalars = pltpu.make_async_copy(ids_vector, ids, arrival)
    to_scalars.start()
    lane = lane[:8]
    pad = jnp.zeros((32, LANES), jnp.float32)
    for source in range(16):
        first = source * ROWS
        tail = jnp.zeros((8, LANES), jnp.float32)
        for tile in range(8):
            piece = recv[first + tile * 8 : first + tile * 8 + 8, :]
            tail = jnp.where(lane // SPARE == tile, pltpu.roll(piece, 15 + SPARE * tile, 1), tail)
        columns[source] = jnp.concatenate([recv[first : first + ROWS, :], tail, pad], 0).T
    blank = jnp.zeros((48, 128), jnp.float32)
    for row in range(50, 64):
        held_re[pl.ds(row, 48, stride=HELD), :] = blank
        held_im[pl.ds(row, 48, stride=HELD), :] = blank
    grid[...] = jnp.zeros_like(grid)
    to_scalars.wait()

    def put(source, _):
        for stick in range(STICK_LIMIT):
            grid[pl.ds(ids[source, stick], 1), :] = columns[source, stick : stick + 1, :]
        return 0

    lax.fori_loop(0, 16, put, 0, unroll=16)
    lower = lax.broadcasted_iota(jnp.int32, (96, 128), 1) < 64

    def place(pair, _):
        rows = grid[pl.ds(pl.multiple_of(pair * 128, 128), 128), :].T[:96]
        high = rows.astype(jnp.bfloat16).astype(jnp.float32)
        low = pltpu.roll(rows - high, 64, 1)
        for half in range(2):
            mixed = jnp.where(lower, low, high) if half else jnp.where(lower, high, low)
            both = jnp.concatenate([mixed, high], 1).astype(jnp.bfloat16)
            out = mm(both, inv_y[half])
            rows_to = pl.ds(pair * 2 + half, 48, stride=HELD)
            held_re[rows_to, :] = out[:48, :128] - out[48:, 128:]
            held_im[rows_to, :] = out[48:, :128] + out[:48, 128:]
        return 0

    lax.fori_loop(0, 25, place, 0, unroll=25)
    clear = jnp.zeros((2 * SLOTS, 128), jnp.float32)
    for row in range(PLANES, 16):
        own[pl.ds(row, 2 * SLOTS, stride=16), :] = clear
        other[pl.ds(row, 2 * SLOTS, stride=16), :] = clear

    def waves(plane, _):
        even = jnp.zeros((FOLD, 128), jnp.float32)
        odd = jnp.zeros((FOLD, 128), jnp.float32)
        for band in range(4):
            start = pl.multiple_of((band * PLANES + plane) * HELD, HELD)
            rows = pl.ds(start, 64)
            high, low = halves(jnp.concatenate([held_re[rows, :], held_im[rows, :]], 1))
            out = mm(inv_x[...], jnp.concatenate([high, low, high], 0))
            cos_re, cos_im = out[:FOLD, :128], out[:FOLD, 128:]
            sin_re, sin_im = out[FOLD:, :128], out[FOLD:, 128:]
            sums = cos_re * cos_re + cos_im * cos_im + (sin_re * sin_re + sin_im * sin_im)
            even = even + (2.0 * factors[band]) * sums
            odd = odd + (4.0 * factors[band]) * (cos_im * sin_re - cos_re * sin_im)
        start = pl.multiple_of(plane * 2 * FOLD, 2 * FOLD)
        density[pl.ds(start, 2 * FOLD), :] = jnp.concatenate([even, odd], 0)
        return 0

    lax.fori_loop(0, PLANES, waves, 0, unroll=12)

    def forward(group, _):
        start = pl.multiple_of(group * 8 * FOLD, 8 * FOLD)
        high, low = halves(density[pl.ds(start, 8 * FOLD), :])
        rows = mm(jnp.concatenate([high, low], 1), fwd_y1[...]) + mm(high, fwd_y2[...])
        high, low = halves(rows)
        for pair in range(2):
            middle = (4 * pair + 2) * FOLD
            first, second = slice(middle - 2 * FOLD, middle), slice(middle, middle + 2 * FOLD)
            wide_high = jnp.concatenate([high[first], high[second]], 1)
            wide_low = jnp.concatenate([low[first], low[second]], 1)
            out = mm(fwd_x[...], jnp.concatenate([wide_high, wide_low, wide_high], 0))
            for member in range(2):
                plane = group * 4 + pair * 2 + member
                lanes = slice(member * 128, member * 128 + 128)
                cosine = pl.ds(plane, SLOTS, stride=16)
                sine = pl.ds(plane + SIDE_ROWS, SLOTS, stride=16)
                own[cosine, :] = out[0:SLOTS, lanes]
                own[sine, :] = out[32 : 32 + SLOTS, lanes]
                other[cosine, :] = out[64 : 64 + SLOTS, lanes]
                other[sine, :] = out[96 : 96 + SLOTS, lanes]
        return 0

    lax.fori_loop(0, 3, forward, 0, unroll=3)


def force_kernel(
    gx2, own, arrived, base, wave_z, atom_z, near_z, x_all, y_cos, y_sin, strength, out, acc, turn
):
    acc[...] = jnp.zeros_like(acc)
    turn[...] = x_all[...]

    def step(slot, reach, phases):
        start = pl.multiple_of(slot * 16, 16)
        first, second = pl.ds(start, 16), pl.ds(start + SIDE_ROWS, 16)
        pair = [own[first, :] + arrived[first, :], own[second, :] + arrived[second, :]]
        high, low = halves(jnp.concatenate(pair, 1))
        waves = wave_z[...]
        if reach < ZSPAN:
            waves = jnp.concatenate([waves[:reach], waves[ZSPAN : ZSPAN + reach]], 0)
        raw = mm(waves, jnp.concatenate([high, low, high], 0))
        weight = 1.0 / (base[:reach] + gx2[slot])
        weight = jnp.concatenate([weight, weight], 1)
        weight = jnp.concatenate([weight, weight], 0)
        high, low = halves(raw * weight)
        both = mm(phases[...], jnp.concatenate([high, low, high], 0))
        table = turn[...]
        xc_c, xc_s = table[:, 0:1], table[:, 32:33]
        xs_c, xs_s = table[:, 64:65], table[:, 96:97]
        plain_c, plain_s = both[:128, :128], both[:128, 128:]
        acc[0] += xs_c * plain_c + xs_s * plain_s
        acc[1] += xc_c * plain_c + xc_s * plain_s
        acc[2] += xc_c * both[128:, :128] + xc_s * both[128:, 128:]
        turn[...] = pltpu.roll(table, 127, 1)
        return 0

    lax.fori_loop(0, 14, lambda slot, _: step(slot, ZSPAN, atom_z), 0, unroll=14)
    lax.fori_loop(14, SLOTS, lambda slot, _: step(slot, NEAR, near_z), 0, unroll=11)
    parts = [acc[0] * y_cos[...], acc[1] * y_sin[...], acc[2] * y_cos[...]]
    rows = [-strength[...] * jnp.sum(part.T, axis=0, keepdims=True) for part in parts]
    block = jnp.concatenate(rows, 0)
    for index in range(16):
        out[index] = block


def shards(
    coefficients, occupation, kpoint_weight, stick_cell, species, positions, amplitude, core_width
):
    payload = pl.pallas_call(
        send_kernel,
        out_shape=jax.ShapeDtypeStruct((16, ROWS, LANES), jnp.float32),
        in_specs=[HBM] * 3,
        out_specs=HBM,
        scratch_shapes=[
            pltpu.VMEM((1, 144), jnp.int32),
            pltpu.VMEM((4, 2, 13824), jnp.float32),
            pltpu.VMEM((384, 256), jnp.bfloat16),
            pltpu.VMEM((4, 384, LANES), jnp.float32),
            pltpu.VMEM((4, 288, LANES), jnp.float32),
            pltpu.VMEM((4, 3, 80, LANES), jnp.float32),
            pltpu.VMEM((16, ROWS, LANES), jnp.float32),
            pltpu.SemaphoreType.DMA((6,)),
            pltpu.SemaphoreType.DMA((16,)),
        ],
        compiler_params=pltpu.CompilerParams(vmem_limit_bytes=60 * 1024 * 1024),
        name="sticks",
    )(stick_cell[None], coefficients, z_table())
    received = lax.all_to_all(payload, AXES, 0, 0, axis_index_groups=exchange_groups(), tiled=True)
    received = received.reshape(16 * ROWS, LANES)

    core = lax.axis_index("band") % 2
    pool_weight = lax.dynamic_index_in_dim(
        kpoint_weight, lax.axis_index("pool"), keepdims=False
    ).astype(jnp.float32) / jnp.sum(kpoint_weight).astype(jnp.float32)
    factors = pool_weight * occupation[0] * (16.0 / NGRID / 32.0 / NGRID)
    fwd_y1, fwd_y2 = forward_y_tables()
    fwd_x = lax.dynamic_index_in_dim(jnp.asarray(forward_x_tables()), core, keepdims=False)
    halves_shape = jax.ShapeDtypeStruct((2 * SIDE_ROWS, 128), jnp.float32)
    own, other = pl.pallas_call(
        density_kernel,
        out_shape=(halves_shape, halves_shape),
        in_specs=[SMEM] + [VMEM] * 6,
        out_specs=(VMEM, VMEM),
        scratch_shapes=[
            pltpu.VMEM((16, LANES, LANES), jnp.float32),
            pltpu.VMEM((50 * 64, LANES), jnp.float32),
            pltpu.VMEM((48 * HELD, LANES), jnp.float32),
            pltpu.VMEM((48 * HELD, LANES), jnp.float32),
            pltpu.VMEM((PLANES * 2 * FOLD, LANES), jnp.float32),
            pltpu.VMEM((16, LANES), jnp.int32),
            pltpu.SMEM((16, LANES), jnp.int32),
            pltpu.SemaphoreType.DMA,
        ],
        compiler_params=pltpu.CompilerParams(vmem_limit_bytes=40 * 1024 * 1024),
        name="density",
    )(factors, received, inverse_y_tables(), inverse_x_table(), fwd_y1, fwd_y2, fwd_x)
    swap = [(index, index ^ 1) for index in range(8)]
    arrived = lax.ppermute(other, "band", swap)

    rank_z, rank_y = lax.axis_index("fft") // 2, lax.axis_index("fft") % 2
    start = (rank_y * 8 + rank_z) * PLANES
    steps = (jnp.arange(ZSPAN)[:, None] * (start + jnp.arange(PLANES))[None, :]) % NZ
    angles = 2.0 * math.pi / NZ * steps.astype(jnp.float32)
    turned = jnp.pad(jnp.concatenate([jnp.cos(angles), jnp.sin(angles)], 0), ((0, 0), (0, 4)))
    high, low = table_halves(turned)
    wave_z = jnp.concatenate([high, high, low], 1)
    kinds = species[None, :] == jnp.arange(3, dtype=jnp.int32)[:, None]
    width = jnp.sum(jnp.where(kinds, core_width[:, None], 0.0), axis=0)
    strength = jnp.sum(jnp.where(kinds, amplitude[:, None], 0.0), axis=0)

    def tables(where, order, unit, counts):
        waves = unit * order
        turns = where[:, None] * order[None, :]
        phase = 2.0 * math.pi * (turns - jnp.round(turns))
        scale = counts[None, :] * jnp.exp(-0.5 * (width * width)[:, None] * (waves * waves)[None])
        cosine, sine = scale * jnp.cos(phase), scale * jnp.sin(phase)
        slope = waves[None, :]
        return cosine, sine, slope * sine, -slope * cosine

    hx = 2.0 * jnp.arange(32, dtype=jnp.float32) + core.astype(jnp.float32)
    unit = 2.0 * math.pi / 96
    count_x = jnp.where(hx > 48.0, 0.0, jnp.where((hx == 0.0) | (hx == 48.0), 1.0, 2.0))
    x_all = jnp.concatenate(tables(positions[0], hx, unit, count_x), 1)
    hy = jnp.arange(64, dtype=jnp.float32)
    count_y = jnp.where(hy > 48.0, 0.0, jnp.where((hy == 0.0) | (hy == 48.0), 1.0, 2.0))
    y_parts = tables(positions[1], hy, unit, count_y)
    y_cos = jnp.concatenate(y_parts[:2], 1)
    y_sin = jnp.concatenate(y_parts[2:], 1)
    hz = jnp.arange(ZSPAN, dtype=jnp.float32)
    z_parts = tables(positions[2], hz, 2.0 * math.pi / NZ, jnp.where(hz == 0.0, 1.0, 2.0))

    def atom_table(reach):
        plain = jnp.concatenate([part[:, :reach] for part in z_parts[:2]], 1)
        sloped = jnp.concatenate([part[:, :reach] for part in z_parts[2:]], 1)
        high, low = table_halves(jnp.concatenate([plain, sloped], 0))
        return jnp.concatenate([high, high, low], 1)

    gy = np.tile(2.0 * np.pi / 96 * np.arange(64), 2)
    gz = 2.0 * np.pi / NZ * np.arange(ZSPAN)
    base = (gy[None, :] ** 2 + gz[:, None] ** 2 + screen).astype(np.float32)
    gx2 = (unit * hx) * (unit * hx)
    spread = pl.pallas_call(
        force_kernel,
        out_shape=jax.ShapeDtypeStruct((16, 3, LANES), jnp.float32),
        in_specs=[SMEM] + [VMEM] * 10,
        out_specs=VMEM,
        scratch_shapes=[
            pltpu.VMEM((3, 128, 128), jnp.float32),
            pltpu.VMEM((128, 128), jnp.float32),
        ],
        compiler_params=pltpu.CompilerParams(vmem_limit_bytes=40 * 1024 * 1024),
        name="force",
    )(
        gx2,
        own,
        arrived,
        base,
        wave_z,
        atom_table(ZSPAN),
        atom_table(NEAR),
        x_all,
        y_cos,
        y_sin,
        strength[None],
    )
    along, across = reduce_groups()
    total = jnp.sum(lax.all_to_all(spread, AXES, 0, 0, axis_index_groups=across, tiled=True), axis=0)
    spread = jnp.broadcast_to(total[None], (16, 3, LANES))
    return jnp.sum(lax.all_to_all(spread, AXES, 0, 0, axis_index_groups=along, tiled=True), axis=0)


def solution(mesh):
    placed = (P("pool", "band", None, "fft"), P("pool", "band"), P(), P("fft"), P(), P(), P(), P())
    return jax.shard_map(shards, mesh=mesh, in_specs=placed, out_specs=P(), check_vma=False)
```

```python
import math

import jax
import jax.numpy as jnp
import numpy as np
from jax import lax
from jax.experimental import pallas as pl
from jax.experimental.pallas import tpu as pltpu
from jax.sharding import PartitionSpec as P

NX = 96
NY = 96
NZ = 192
ZSPAN = 96
NGRID = 1769472
HALF = 24
SIDE = 49
LANES = 128
PLANES = 12
SLOTS = 25
SIDE_ROWS = SLOTS * 16
STICK_LIMIT = 113
SPARE = 15
ROWS = 88
NEAR = 80
LAST = 32
HELD = 72
FOLD = 56
GROUPS = 36
SPARE_ROW = SIDE * 64
HIGH = lax.Precision.HIGH
screen = 0.25
AXES = ("pool", "band", "fft")
VMEM = pl.BlockSpec(memory_space=pltpu.VMEM)
HBM = pl.BlockSpec(memory_space=pltpu.HBM)
SMEM = pl.BlockSpec(memory_space=pltpu.SMEM)


def trig(rows, columns, length):
    angles = 2.0 * np.pi / length * (np.outer(rows, columns) % length)
    return np.cos(angles).astype(np.float32), np.sin(angles).astype(np.float32)


def exchange_groups():
    ranks = np.arange(256).reshape(16, 8, 2)
    return ranks.transpose(0, 2, 1).reshape(16, 16).tolist()


def reduce_groups():
    ranks = np.arange(256).reshape(2, 4, 2, 8, 2)
    across = ranks.transpose(3, 2, 4, 0, 1).reshape(16, 16)
    along = ranks.transpose(0, 1, 4, 2, 3).reshape(16, 16)
    return across.tolist(), along.tolist()


def halves(values):
    high = values.astype(jnp.bfloat16)
    return high, (values - high.astype(jnp.float32)).astype(jnp.bfloat16)


def table_halves(values):
    high = lax.reduce_precision(values, 8, 7)
    return high.astype(jnp.bfloat16), (values - high).astype(jnp.bfloat16)


def np_halves(values):
    high = values.astype(jnp.bfloat16)
    return high, (values - high.astype(np.float32)).astype(jnp.bfloat16)


def mm(left, right):
    return jnp.dot(left, right, preferred_element_type=jnp.float32)


def z_table():
    both = np.zeros((2, NZ, LANES), np.float32)
    both[:, :, :ZSPAN] = trig(np.arange(NZ), np.arange(ZSPAN) - NZ // 4, NZ)
    return np.concatenate(np_halves(both.reshape(2 * NZ, LANES)), 1)


def inverse_y_tables():
    cosine, sine = trig(np.arange(SIDE) - HALF, np.arange(96), 96)
    both = np.zeros((SIDE, 256), np.float32)
    both[:, :96], both[:, 128:224] = cosine, sine
    high, low = np_halves(both)
    table = np.zeros((2, 256, 256), high.dtype)
    for half in range(2):
        for part in range(2):
            table[half, 64 * part : 64 * part + SIDE] = high
        table[half, 128 + 64 * half : 128 + 64 * half + SIDE] = low
    return table


def inverse_x_table():
    cosine, sine = trig(np.arange(SIDE), np.arange(SIDE) - HALF, 96)
    both = np.zeros((2 * FOLD, 64), np.float32)
    both[:SIDE, :SIDE], both[FOLD : FOLD + SIDE, :SIDE] = cosine, sine
    high, low = np_halves(both)
    return np.concatenate([high, high, low], 1)


def forward_y_tables():
    cosine, sine = trig(np.arange(96), np.arange(SIDE), 96)
    both = np.zeros((128, 128), np.float32)
    both[:96, :SIDE], both[:96, 64 : 64 + SIDE] = cosine, sine
    high, low = np_halves(both)
    return np.concatenate([high, high], 0), low


def forward_x_tables():
    cosine, sine = trig(np.arange(50), np.arange(SIDE), 96)
    cosine[SIDE:], sine[SIDE:] = 0.0, 0.0
    cosine[:, 0], cosine[:, 48] = cosine[:, 0] / 2, cosine[:, 48] / 2
    result = []
    for core in range(2):
        both = np.zeros((128, 2 * FOLD), np.float32)
        for index, rows in enumerate((core, 1 - core)):
            both[64 * index : 64 * index + SLOTS, :SIDE] = cosine[rows::2]
            both[64 * index + 32 : 64 * index + 32 + SLOTS, FOLD : FOLD + SIDE] = sine[rows::2]
        high, low = np_halves(both)
        result.append(np.concatenate([high, high, low], 1))
    return np.stack(result)


def mm_t(left, right):
    return lax.dot_general(
        left, right, (((1,), (1,)), ((), ())), preferred_element_type=jnp.float32
    )


def small(flags):
    return flags.astype(jnp.float32).astype(jnp.bfloat16)


def pieces(held, dest, tile):
    found = []
    for row in range(tile * 8, tile * 8 + 8, 4):
        start = (row // 48) * 192 + dest * PLANES + row % 12
        found.append(held[(row % 48) // 12, start : start + 4, :])
    return jnp.concatenate(found, 0)


def send_kernel(
    cells, coefs, z_waves, out, place, raw, table, held, natural, rows, packed, loads, stores
):
    copies = [
        pltpu.make_async_copy(coefs.at[0, band], raw.at[band], loads.at[band]) for band in range(4)
    ]
    copies.append(pltpu.make_async_copy(z_waves, table, loads.at[4]))
    where = pltpu.make_async_copy(cells, place, loads.at[5])
    where.start()
    for copy in copies:
        copy.start()
    where.wait()
    for copy in copies:
        copy.wait()
    stick = jnp.concatenate([place[...], jnp.full((1, 112), 48 * NY, jnp.int32)], 1)
    stick = jnp.broadcast_to(stick, (8, 256))
    column = stick // NY
    freq_x = jnp.where(column < 48, column, column - NX)
    freq_y = stick - column * NY
    freq_y = jnp.where(freq_y < 48, freq_y, freq_y - NY)
    reach = freq_x * freq_x + freq_y * freq_y
    chosen = reach <= HALF * HALF
    earlier = lax.broadcasted_iota(jnp.int32, (256, 256), 0)
    earlier = earlier < lax.broadcasted_iota(jnp.int32, (256, 256), 1)
    rank = mm(chosen.astype(jnp.float32).astype(jnp.bfloat16), small(earlier))
    order = lax.broadcasted_iota(jnp.int32, (LANES, 256), 0).astype(jnp.float32)
    pick = small((rank[0:1] == order) & chosen[0:1])
    line = lax.broadcasted_iota(jnp.int32, (8, 256), 0)
    facts = jnp.where(line == 0, (freq_x + HALF) * 64, jnp.where(line == 1, freq_y + HALF, 1))
    facts = mm_t(facts.astype(jnp.float32).astype(jnp.bfloat16), pick)
    ids = facts[0:1] + facts[1:2] + SPARE_ROW * (1.0 - facts[2:3])
    coarse = reach // 16 * 16
    spread = [jnp.broadcast_to(part[0:1], (LANES, 256)) for part in (coarse, reach - coarse)]
    level = sum(mm_t(pick, part.astype(jnp.float32).astype(jnp.bfloat16)) for part in spread)
    slot = lax.broadcasted_iota(jnp.int32, (LANES, LANES), 1)
    freq_z = (slot - NZ // 4).astype(jnp.float32)
    inside = (16.0 * level + 4.0 * freq_z * freq_z <= NX * NX) & (slot < ZSPAN)
    inside = jnp.concatenate([inside, inside], 1)
    high_table = table[:, :LANES]
    wide_table = jnp.concatenate([high_table, high_table], 1)
    low_table = table[:, LANES:]
    lane = lax.broadcasted_iota(jnp.int32, (40, LANES), 1)
    filler = jnp.zeros((112, 256), jnp.bfloat16)
    for band in range(4):
        highs, lows = [], []
        for chunk in range(3 * GROUPS):
            piece = raw[band, :, chunk * LANES : (chunk + 1) * LANES]
            for part in range(2):
                start = part * 40 + chunk // 3
                rows[band, chunk % 3, start : start + 1, :] = piece[part : part + 1]
        for part in range(2):
            span = slice(part * 40, part * 40 + 40)
            first, second, third = rows[band, 0, span, :], rows[band, 1, span, :], rows[band, 2, span, :]
            quarters = [
                first,
                jnp.where(lane < 32, pltpu.roll(first, 32, 1), pltpu.roll(second, 32, 1)),
                jnp.where(lane < 64, pltpu.roll(second, 64, 1), pltpu.roll(third, 64, 1)),
                pltpu.roll(third, 96, 1),
            ]
            for index in range(4):
                natural[band, pl.ds(part * 144 + index, GROUPS, stride=4), :] = quarters[index][:GROUPS]
            values = natural[band, part * 144 : part * 144 + 144, :]
            both = jnp.concatenate(halves(values), 1)
            taken = mm(pick, jnp.concatenate([both, filler], 0))
            taken = jnp.where(inside, taken, 0.0).astype(jnp.bfloat16)
            highs.append(taken[:, :128])
            lows.append(taken[:, 128:])
        high = jnp.concatenate(highs, 0)
        spread = jnp.concatenate([high, jnp.concatenate(lows, 0)], 1)
        waves = mm_t(wide_table, spread) + mm_t(low_table, high)
        cosine, sine = waves[:192], waves[192:]
        held[band, :192] = cosine[:, :128] - sine[:, 128:]
        held[band, 192:] = sine[:, :128] + cosine[:, 128:]
    lane = lax.broadcasted_iota(jnp.int32, (8, LANES), 1)
    row = lax.broadcasted_iota(jnp.int32, (8, LANES), 0)
    marks = jnp.zeros((8, LANES), jnp.float32)
    spots = jnp.broadcast_to(ids, (8, LANES))
    for index in range(8):
        marks = jnp.where(row == index, pltpu.roll(spots, STICK_LIMIT - SPARE * index, 1), marks)
    sent = []
    for dest in range(16):
        tail = pieces(held, dest, 11)
        for tile in range(11):
            main = pieces(held, dest, tile)
            if tile < 8:
                extra = pltpu.roll(tail, STICK_LIMIT - SPARE * tile, 1)
            else:
                extra = marks
            packed[dest, tile * 8 : tile * 8 + 8, :] = jnp.where(lane < STICK_LIMIT, main, extra)
        copy = pltpu.make_async_copy(packed.at[dest], out.at[dest], stores.at[dest])
        copy.start()
        sent.append(copy)
    for copy in sent:
        copy.wait()


def density_kernel(
    factors,
    recv,
    inv_y,
    inv_x,
    fwd_y1,
    fwd_y2,
    fwd_x,
    own,
    other,
    columns,
    grid,
    held_re,
    held_im,
    density,
    ids_vector,
    ids,
    arrival,
):
    lane = lax.broadcasted_iota(jnp.int32, (16, LANES), 1)
    marks = jnp.zeros((16, LANES), jnp.float32)
    for index in range(8):
        rolled = pltpu.roll(recv[pl.ds(64 + index, 16, stride=ROWS), :], 15 + SPARE * index, 1)
        marks = jnp.where(lane // SPARE == index, rolled, marks)
    ids_vector[...] = marks.astype(jnp.int32)
    to_scalars = pltpu.make_async_copy(ids_vector, ids, arrival)
    to_scalars.start()
    lane = lane[:8]
    pad = jnp.zeros((32, LANES), jnp.float32)
    for source in range(16):
        first = source * ROWS
        tail = jnp.zeros((8, LANES), jnp.float32)
        for tile in range(8):
            piece = recv[first + tile * 8 : first + tile * 8 + 8, :]
            tail = jnp.where(lane // SPARE == tile, pltpu.roll(piece, 15 + SPARE * tile, 1), tail)
        columns[source] = jnp.concatenate([recv[first : first + ROWS, :], tail, pad], 0).T
    blank = jnp.zeros((48, 128), jnp.float32)
    for row in range(50, 64):
        held_re[pl.ds(row, 48, stride=HELD), :] = blank
        held_im[pl.ds(row, 48, stride=HELD), :] = blank
    grid[...] = jnp.zeros_like(grid)
    to_scalars.wait()

    def put(source, _):
        for stick in range(STICK_LIMIT):
            grid[pl.ds(ids[source, stick], 1), :] = columns[source, stick : stick + 1, :]
        return 0

    lax.fori_loop(0, 16, put, 0, unroll=16)
    lower = lax.broadcasted_iota(jnp.int32, (96, 128), 1) < 64

    def place(pair, _):
        rows = grid[pl.ds(pl.multiple_of(pair * 128, 128), 128), :].T[:96]
        high = rows.astype(jnp.bfloat16).astype(jnp.float32)
        low = pltpu.roll(rows - high, 64, 1)
        for half in range(2):
            mixed = jnp.where(lower, low, high) if half else jnp.where(lower, high, low)
            both = jnp.concatenate([mixed, high], 1).astype(jnp.bfloat16)
            out = mm(both, inv_y[half])
            rows_to = pl.ds(pair * 2 + half, 48, stride=HELD)
            held_re[rows_to, :] = out[:48, :128] - out[48:, 128:]
            held_im[rows_to, :] = out[48:, :128] + out[:48, 128:]
        return 0

    lax.fori_loop(0, 25, place, 0, unroll=25)
    clear = jnp.zeros((2 * SLOTS, 128), jnp.float32)
    for row in range(PLANES, 16):
        own[pl.ds(row, 2 * SLOTS, stride=16), :] = clear
        other[pl.ds(row, 2 * SLOTS, stride=16), :] = clear

    def waves(plane, _):
        even = jnp.zeros((FOLD, 128), jnp.float32)
        odd = jnp.zeros((FOLD, 128), jnp.float32)
        for band in range(4):
            start = pl.multiple_of((band * PLANES + plane) * HELD, HELD)
            rows = pl.ds(start, 64)
            high, low = halves(jnp.concatenate([held_re[rows, :], held_im[rows, :]], 1))
            out = mm(inv_x[...], jnp.concatenate([high, low, high], 0))
            cos_re, cos_im = out[:FOLD, :128], out[:FOLD, 128:]
            sin_re, sin_im = out[FOLD:, :128], out[FOLD:, 128:]
            sums = cos_re * cos_re + cos_im * cos_im + (sin_re * sin_re + sin_im * sin_im)
            even = even + (2.0 * factors[band]) * sums
            odd = odd + (4.0 * factors[band]) * (cos_im * sin_re - cos_re * sin_im)
        start = pl.multiple_of(plane * 2 * FOLD, 2 * FOLD)
        density[pl.ds(start, 2 * FOLD), :] = jnp.concatenate([even, odd], 0)
        return 0

    lax.fori_loop(0, PLANES, waves, 0, unroll=12)

    def forward(group, _):
        start = pl.multiple_of(group * 8 * FOLD, 8 * FOLD)
        high, low = halves(density[pl.ds(start, 8 * FOLD), :])
        rows = mm(jnp.concatenate([high, low], 1), fwd_y1[...]) + mm(high, fwd_y2[...])
        high, low = halves(rows)
        for pair in range(2):
            middle = (4 * pair + 2) * FOLD
            first, second = slice(middle - 2 * FOLD, middle), slice(middle, middle + 2 * FOLD)
            wide_high = jnp.concatenate([high[first], high[second]], 1)
            wide_low = jnp.concatenate([low[first], low[second]], 1)
            out = mm(fwd_x[...], jnp.concatenate([wide_high, wide_low, wide_high], 0))
            for member in range(2):
                plane = group * 4 + pair * 2 + member
                lanes = slice(member * 128, member * 128 + 128)
                cosine = pl.ds(plane, SLOTS, stride=16)
                sine = pl.ds(plane + SIDE_ROWS, SLOTS, stride=16)
                own[cosine, :] = out[0:SLOTS, lanes]
                own[sine, :] = out[32 : 32 + SLOTS, lanes]
                other[cosine, :] = out[64 : 64 + SLOTS, lanes]
                other[sine, :] = out[96 : 96 + SLOTS, lanes]
        return 0

    lax.fori_loop(0, 3, forward, 0, unroll=3)


def force_kernel(
    gx2, own, arrived, base, wave_z, atom_z, near_z, last_z, x_all, y_cos, y_sin, strength, out, acc, turn
):
    acc[...] = jnp.zeros_like(acc)
    turn[...] = x_all[...]

    def step(slot, reach, phases):
        start = pl.multiple_of(slot * 16, 16)
        first, second = pl.ds(start, 16), pl.ds(start + SIDE_ROWS, 16)
        pair = [own[first, :] + arrived[first, :], own[second, :] + arrived[second, :]]
        high, low = halves(jnp.concatenate(pair, 1))
        waves = wave_z[...]
        if reach < ZSPAN:
            waves = jnp.concatenate([waves[:reach], waves[ZSPAN : ZSPAN + reach]], 0)
        raw = mm(waves, jnp.concatenate([high, low, high], 0))
        weight = 1.0 / (base[:reach] + gx2[slot])
        weight = jnp.concatenate([weight, weight], 1)
        weight = jnp.concatenate([weight, weight], 0)
        high, low = halves(raw * weight)
        both = mm(phases[...], jnp.concatenate([high, low, high], 0))
        table = turn[...]
        xc_c, xc_s = table[:, 0:1], table[:, 32:33]
        xs_c, xs_s = table[:, 64:65], table[:, 96:97]
        plain_c, plain_s = both[:128, :128], both[:128, 128:]
        acc[0] += xs_c * plain_c + xs_s * plain_s
        acc[1] += xc_c * plain_c + xc_s * plain_s
        acc[2] += xc_c * both[128:, :128] + xc_s * both[128:, 128:]
        turn[...] = pltpu.roll(table, 127, 1)
        return 0

    lax.fori_loop(0, 14, lambda slot, _: step(slot, ZSPAN, atom_z), 0, unroll=14)
    lax.fori_loop(14, 23, lambda slot, _: step(slot, NEAR, near_z), 0, unroll=9)
    lax.fori_loop(23, SLOTS, lambda slot, _: step(slot, LAST, last_z), 0, unroll=2)
    parts = [acc[0] * y_cos[...], acc[1] * y_sin[...], acc[2] * y_cos[...]]
    rows = [-strength[...] * jnp.sum(part.T, axis=0, keepdims=True) for part in parts]
    block = jnp.concatenate(rows, 0)
    for index in range(16):
        out[index] = block


def shards(
    coefficients, occupation, kpoint_weight, stick_cell, species, positions, amplitude, core_width
):
    payload = pl.pallas_call(
        send_kernel,
        out_shape=jax.ShapeDtypeStruct((16, ROWS, LANES), jnp.float32),
        in_specs=[HBM] * 3,
        out_specs=HBM,
        scratch_shapes=[
            pltpu.VMEM((1, 144), jnp.int32),
            pltpu.VMEM((4, 2, 13824), jnp.float32),
            pltpu.VMEM((384, 256), jnp.bfloat16),
            pltpu.VMEM((4, 384, LANES), jnp.float32),
            pltpu.VMEM((4, 288, LANES), jnp.float32),
            pltpu.VMEM((4, 3, 80, LANES), jnp.float32),
            pltpu.VMEM((16, ROWS, LANES), jnp.float32),
            pltpu.SemaphoreType.DMA((6,)),
            pltpu.SemaphoreType.DMA((16,)),
        ],
        compiler_params=pltpu.CompilerParams(vmem_limit_bytes=60 * 1024 * 1024),
        name="sticks",
    )(stick_cell[None], coefficients, z_table())
    received = lax.all_to_all(payload, AXES, 0, 0, axis_index_groups=exchange_groups(), tiled=True)
    received = received.reshape(16 * ROWS, LANES)

    core = lax.axis_index("band") % 2
    pool_weight = lax.dynamic_index_in_dim(
        kpoint_weight, lax.axis_index("pool"), keepdims=False
    ).astype(jnp.float32) / jnp.sum(kpoint_weight).astype(jnp.float32)
    factors = pool_weight * occupation[0] * (16.0 / NGRID / 32.0 / NGRID)
    fwd_y1, fwd_y2 = forward_y_tables()
    fwd_x = lax.dynamic_index_in_dim(jnp.asarray(forward_x_tables()), core, keepdims=False)
    halves_shape = jax.ShapeDtypeStruct((2 * SIDE_ROWS, 128), jnp.float32)
    own, other = pl.pallas_call(
        density_kernel,
        out_shape=(halves_shape, halves_shape),
        in_specs=[SMEM] + [VMEM] * 6,
        out_specs=(VMEM, VMEM),
        scratch_shapes=[
            pltpu.VMEM((16, LANES, LANES), jnp.float32),
            pltpu.VMEM((50 * 64, LANES), jnp.float32),
            pltpu.VMEM((48 * HELD, LANES), jnp.float32),
            pltpu.VMEM((48 * HELD, LANES), jnp.float32),
            pltpu.VMEM((PLANES * 2 * FOLD, LANES), jnp.float32),
            pltpu.VMEM((16, LANES), jnp.int32),
            pltpu.SMEM((16, LANES), jnp.int32),
            pltpu.SemaphoreType.DMA,
        ],
        compiler_params=pltpu.CompilerParams(vmem_limit_bytes=40 * 1024 * 1024),
        name="density",
    )(factors, received, inverse_y_tables(), inverse_x_table(), fwd_y1, fwd_y2, fwd_x)
    swap = [(index, index ^ 1) for index in range(8)]
    arrived = lax.ppermute(other, "band", swap)

    rank_z, rank_y = lax.axis_index("fft") // 2, lax.axis_index("fft") % 2
    start = (rank_y * 8 + rank_z) * PLANES
    steps = (jnp.arange(ZSPAN)[:, None] * (start + jnp.arange(PLANES))[None, :]) % NZ
    angles = 2.0 * math.pi / NZ * steps.astype(jnp.float32)
    turned = jnp.pad(jnp.concatenate([jnp.cos(angles), jnp.sin(angles)], 0), ((0, 0), (0, 4)))
    high, low = table_halves(turned)
    wave_z = jnp.concatenate([high, high, low], 1)
    kinds = species[None, :] == jnp.arange(3, dtype=jnp.int32)[:, None]
    width = jnp.sum(jnp.where(kinds, core_width[:, None], 0.0), axis=0)
    strength = jnp.sum(jnp.where(kinds, amplitude[:, None], 0.0), axis=0)

    def tables(where, order, unit, counts):
        waves = unit * order
        turns = where[:, None] * order[None, :]
        phase = 2.0 * math.pi * (turns - jnp.round(turns))
        scale = counts[None, :] * jnp.exp(-0.5 * (width * width)[:, None] * (waves * waves)[None])
        cosine, sine = scale * jnp.cos(phase), scale * jnp.sin(phase)
        slope = waves[None, :]
        return cosine, sine, slope * sine, -slope * cosine

    hx = 2.0 * jnp.arange(32, dtype=jnp.float32) + core.astype(jnp.float32)
    unit = 2.0 * math.pi / 96
    count_x = jnp.where(hx > 48.0, 0.0, jnp.where((hx == 0.0) | (hx == 48.0), 1.0, 2.0))
    x_all = jnp.concatenate(tables(positions[0], hx, unit, count_x), 1)
    hy = jnp.arange(64, dtype=jnp.float32)
    count_y = jnp.where(hy > 48.0, 0.0, jnp.where((hy == 0.0) | (hy == 48.0), 1.0, 2.0))
    y_parts = tables(positions[1], hy, unit, count_y)
    y_cos = jnp.concatenate(y_parts[:2], 1)
    y_sin = jnp.concatenate(y_parts[2:], 1)
    hz = jnp.arange(ZSPAN, dtype=jnp.float32)
    z_parts = tables(positions[2], hz, 2.0 * math.pi / NZ, jnp.where(hz == 0.0, 1.0, 2.0))

    def atom_table(reach):
        plain = jnp.concatenate([part[:, :reach] for part in z_parts[:2]], 1)
        sloped = jnp.concatenate([part[:, :reach] for part in z_parts[2:]], 1)
        high, low = table_halves(jnp.concatenate([plain, sloped], 0))
        return jnp.concatenate([high, high, low], 1)

    gy = np.tile(2.0 * np.pi / 96 * np.arange(64), 2)
    gz = 2.0 * np.pi / NZ * np.arange(ZSPAN)
    base = (gy[None, :] ** 2 + gz[:, None] ** 2 + screen).astype(np.float32)
    gx2 = (unit * hx) * (unit * hx)
    spread = pl.pallas_call(
        force_kernel,
        out_shape=jax.ShapeDtypeStruct((16, 3, LANES), jnp.float32),
        in_specs=[SMEM] + [VMEM] * 11,
        out_specs=VMEM,
        scratch_shapes=[
            pltpu.VMEM((3, 128, 128), jnp.float32),
            pltpu.VMEM((128, 128), jnp.float32),
        ],
        compiler_params=pltpu.CompilerParams(vmem_limit_bytes=40 * 1024 * 1024),
        name="force",
    )(
        gx2,
        own,
        arrived,
        base,
        wave_z,
        atom_table(ZSPAN),
        atom_table(NEAR),
        atom_table(LAST),
        x_all,
        y_cos,
        y_sin,
        strength[None],
    )
    along, across = reduce_groups()
    total = jnp.sum(lax.all_to_all(spread, AXES, 0, 0, axis_index_groups=across, tiled=True), axis=0)
    spread = jnp.broadcast_to(total[None], (16, 3, LANES))
    return jnp.sum(lax.all_to_all(spread, AXES, 0, 0, axis_index_groups=along, tiled=True), axis=0)


def solution(mesh):
    placed = (P("pool", "band", None, "fft"), P("pool", "band"), P(), P("fft"), P(), P(), P(), P())
    return jax.shard_map(shards, mesh=mesh, in_specs=placed, out_specs=P(), check_vma=False)
```

```python
import math

import jax
import jax.numpy as jnp
import numpy as np
from jax import lax
from jax.experimental import pallas as pl
from jax.experimental.pallas import tpu as pltpu
from jax.sharding import PartitionSpec as P

NX = 96
NY = 96
NZ = 192
ZSPAN = 96
NGRID = 1769472
HALF = 24
SIDE = 49
LANES = 128
PLANES = 12
SLOTS = 25
SIDE_ROWS = SLOTS * 12
STICK_LIMIT = 113
SPARE = 15
ROWS = 88
NEAR = 80
HELD = 72
FOLD = 56
GROUPS = 36
SPARE_ROW = SIDE * 64
HIGH = lax.Precision.HIGH
screen = 0.25
AXES = ("pool", "band", "fft")
VMEM = pl.BlockSpec(memory_space=pltpu.VMEM)
HBM = pl.BlockSpec(memory_space=pltpu.HBM)
SMEM = pl.BlockSpec(memory_space=pltpu.SMEM)


def trig(rows, columns, length):
    angles = 2.0 * np.pi / length * (np.outer(rows, columns) % length)
    return np.cos(angles).astype(np.float32), np.sin(angles).astype(np.float32)


def exchange_groups():
    ranks = np.arange(256).reshape(16, 8, 2)
    return ranks.transpose(0, 2, 1).reshape(16, 16).tolist()


def reduce_groups():
    ranks = np.arange(256).reshape(2, 4, 2, 8, 2)
    across = ranks.transpose(3, 2, 4, 0, 1).reshape(16, 16)
    along = ranks.transpose(0, 1, 4, 2, 3).reshape(16, 16)
    return across.tolist(), along.tolist()


def halves(values):
    high = values.astype(jnp.bfloat16)
    return high, (values - high.astype(jnp.float32)).astype(jnp.bfloat16)


def table_halves(values):
    high = lax.reduce_precision(values, 8, 7)
    return high.astype(jnp.bfloat16), (values - high).astype(jnp.bfloat16)


def np_halves(values):
    high = values.astype(jnp.bfloat16)
    return high, (values - high.astype(np.float32)).astype(jnp.bfloat16)


def mm(left, right):
    return jnp.dot(left, right, preferred_element_type=jnp.float32)


def z_table():
    both = np.zeros((2, NZ, LANES), np.float32)
    both[:, :, :ZSPAN] = trig(np.arange(NZ), np.arange(ZSPAN) - NZ // 4, NZ)
    return np.concatenate(np_halves(both.reshape(2 * NZ, LANES)), 1)


def inverse_y_tables():
    cosine, sine = trig(np.arange(SIDE) - HALF, np.arange(96), 96)
    both = np.zeros((SIDE, 256), np.float32)
    both[:, :96], both[:, 128:224] = cosine, sine
    high, low = np_halves(both)
    table = np.zeros((2, 256, 256), high.dtype)
    for half in range(2):
        for part in range(2):
            table[half, 64 * part : 64 * part + SIDE] = high
        table[half, 128 + 64 * half : 128 + 64 * half + SIDE] = low
    return table


def inverse_x_table():
    cosine, sine = trig(np.arange(SIDE), np.arange(SIDE) - HALF, 96)
    both = np.zeros((2 * FOLD, 64), np.float32)
    both[:SIDE, :SIDE], both[FOLD : FOLD + SIDE, :SIDE] = cosine, sine
    high, low = np_halves(both)
    return np.concatenate([high, high, low], 1)


def forward_y_tables():
    cosine, sine = trig(np.arange(96), np.arange(SIDE), 96)
    both = np.zeros((128, 128), np.float32)
    both[:96, :SIDE], both[:96, 64 : 64 + SIDE] = cosine, sine
    high, low = np_halves(both)
    return np.concatenate([high, high], 0), low


def forward_x_tables():
    cosine, sine = trig(np.arange(50), np.arange(SIDE), 96)
    cosine[SIDE:], sine[SIDE:] = 0.0, 0.0
    cosine[:, 0], cosine[:, 48] = cosine[:, 0] / 2, cosine[:, 48] / 2
    result = []
    for core in range(2):
        both = np.zeros((128, 2 * FOLD), np.float32)
        for index, rows in enumerate((core, 1 - core)):
            both[64 * index : 64 * index + SLOTS, :SIDE] = cosine[rows::2]
            both[64 * index + 32 : 64 * index + 32 + SLOTS, FOLD : FOLD + SIDE] = sine[rows::2]
        high, low = np_halves(both)
        result.append(np.concatenate([high, high, low], 1))
    return np.stack(result)


def mm_t(left, right):
    return lax.dot_general(
        left, right, (((1,), (1,)), ((), ())), preferred_element_type=jnp.float32
    )


def small(flags):
    return flags.astype(jnp.float32).astype(jnp.bfloat16)


def pieces(held, dest, tile):
    found = []
    for row in range(tile * 8, tile * 8 + 8, 4):
        start = (row // 48) * 192 + dest * PLANES + row % 12
        found.append(held[(row % 48) // 12, start : start + 4, :])
    return jnp.concatenate(found, 0)


def send_kernel(
    cells, coefs, z_waves, out, place, raw, table, held, natural, rows, packed, loads, stores
):
    copies = [
        pltpu.make_async_copy(coefs.at[0, band], raw.at[band], loads.at[band]) for band in range(4)
    ]
    copies.append(pltpu.make_async_copy(z_waves, table, loads.at[4]))
    where = pltpu.make_async_copy(cells, place, loads.at[5])
    where.start()
    for copy in copies:
        copy.start()
    where.wait()
    for copy in copies:
        copy.wait()
    stick = jnp.concatenate([place[...], jnp.full((1, 112), 48 * NY, jnp.int32)], 1)
    stick = jnp.broadcast_to(stick, (8, 256))
    column = stick // NY
    freq_x = jnp.where(column < 48, column, column - NX)
    freq_y = stick - column * NY
    freq_y = jnp.where(freq_y < 48, freq_y, freq_y - NY)
    reach = freq_x * freq_x + freq_y * freq_y
    chosen = reach <= HALF * HALF
    earlier = lax.broadcasted_iota(jnp.int32, (256, 256), 0)
    earlier = earlier < lax.broadcasted_iota(jnp.int32, (256, 256), 1)
    rank = mm(chosen.astype(jnp.float32).astype(jnp.bfloat16), small(earlier))
    order = lax.broadcasted_iota(jnp.int32, (LANES, 256), 0).astype(jnp.float32)
    pick = small((rank[0:1] == order) & chosen[0:1])
    line = lax.broadcasted_iota(jnp.int32, (8, 256), 0)
    facts = jnp.where(line == 0, (freq_x + HALF) * 64, jnp.where(line == 1, freq_y + HALF, 1))
    facts = mm_t(facts.astype(jnp.float32).astype(jnp.bfloat16), pick)
    ids = facts[0:1] + facts[1:2] + SPARE_ROW * (1.0 - facts[2:3])
    coarse = reach // 16 * 16
    spread = [jnp.broadcast_to(part[0:1], (LANES, 256)) for part in (coarse, reach - coarse)]
    level = sum(mm_t(pick, part.astype(jnp.float32).astype(jnp.bfloat16)) for part in spread)
    slot = lax.broadcasted_iota(jnp.int32, (LANES, LANES), 1)
    freq_z = (slot - NZ // 4).astype(jnp.float32)
    inside = (16.0 * level + 4.0 * freq_z * freq_z <= NX * NX) & (slot < ZSPAN)
    inside = jnp.concatenate([inside, inside], 1)
    high_table = table[:, :LANES]
    wide_table = jnp.concatenate([high_table, high_table], 1)
    low_table = table[:, LANES:]
    lane = lax.broadcasted_iota(jnp.int32, (40, LANES), 1)
    filler = jnp.zeros((112, 256), jnp.bfloat16)
    for band in range(4):
        highs, lows = [], []
        for chunk in range(3 * GROUPS):
            piece = raw[band, :, chunk * LANES : (chunk + 1) * LANES]
            for part in range(2):
                start = part * 40 + chunk // 3
                rows[band, chunk % 3, start : start + 1, :] = piece[part : part + 1]
        for part in range(2):
            span = slice(part * 40, part * 40 + 40)
            first, second, third = rows[band, 0, span, :], rows[band, 1, span, :], rows[band, 2, span, :]
            quarters = [
                first,
                jnp.where(lane < 32, pltpu.roll(first, 32, 1), pltpu.roll(second, 32, 1)),
                jnp.where(lane < 64, pltpu.roll(second, 64, 1), pltpu.roll(third, 64, 1)),
                pltpu.roll(third, 96, 1),
            ]
            for index in range(4):
                natural[band, pl.ds(part * 144 + index, GROUPS, stride=4), :] = quarters[index][:GROUPS]
            values = natural[band, part * 144 : part * 144 + 144, :]
            both = jnp.concatenate(halves(values), 1)
            taken = mm(pick, jnp.concatenate([both, filler], 0))
            taken = jnp.where(inside, taken, 0.0).astype(jnp.bfloat16)
            highs.append(taken[:, :128])
            lows.append(taken[:, 128:])
        high = jnp.concatenate(highs, 0)
        spread = jnp.concatenate([high, jnp.concatenate(lows, 0)], 1)
        waves = mm_t(wide_table, spread) + mm_t(low_table, high)
        cosine, sine = waves[:192], waves[192:]
        held[band, :192] = cosine[:, :128] - sine[:, 128:]
        held[band, 192:] = sine[:, :128] + cosine[:, 128:]
    lane = lax.broadcasted_iota(jnp.int32, (8, LANES), 1)
    row = lax.broadcasted_iota(jnp.int32, (8, LANES), 0)
    marks = jnp.zeros((8, LANES), jnp.float32)
    spots = jnp.broadcast_to(ids, (8, LANES))
    for index in range(8):
        marks = jnp.where(row == index, pltpu.roll(spots, STICK_LIMIT - SPARE * index, 1), marks)
    sent = []
    for dest in range(16):
        tail = pieces(held, dest, 11)
        for tile in range(11):
            main = pieces(held, dest, tile)
            if tile < 8:
                extra = pltpu.roll(tail, STICK_LIMIT - SPARE * tile, 1)
            else:
                extra = marks
            packed[dest, tile * 8 : tile * 8 + 8, :] = jnp.where(lane < STICK_LIMIT, main, extra)
        copy = pltpu.make_async_copy(packed.at[dest], out.at[dest], stores.at[dest])
        copy.start()
        sent.append(copy)
    for copy in sent:
        copy.wait()


def density_kernel(
    factors,
    recv,
    inv_y,
    inv_x,
    fwd_y1,
    fwd_y2,
    fwd_x,
    own,
    other,
    columns,
    grid,
    held_re,
    held_im,
    density,
    ids_vector,
    ids,
    arrival,
):
    lane = lax.broadcasted_iota(jnp.int32, (16, LANES), 1)
    marks = jnp.zeros((16, LANES), jnp.float32)
    for index in range(8):
        rolled = pltpu.roll(recv[pl.ds(64 + index, 16, stride=ROWS), :], 15 + SPARE * index, 1)
        marks = jnp.where(lane // SPARE == index, rolled, marks)
    ids_vector[...] = marks.astype(jnp.int32)
    to_scalars = pltpu.make_async_copy(ids_vector, ids, arrival)
    to_scalars.start()
    lane = lane[:8]
    pad = jnp.zeros((32, LANES), jnp.float32)
    for source in range(16):
        first = source * ROWS
        tail = jnp.zeros((8, LANES), jnp.float32)
        for tile in range(8):
            piece = recv[first + tile * 8 : first + tile * 8 + 8, :]
            tail = jnp.where(lane // SPARE == tile, pltpu.roll(piece, 15 + SPARE * tile, 1), tail)
        columns[source] = jnp.concatenate([recv[first : first + ROWS, :], tail, pad], 0).T
    blank = jnp.zeros((48, 128), jnp.float32)
    for row in range(50, 64):
        held_re[pl.ds(row, 48, stride=HELD), :] = blank
        held_im[pl.ds(row, 48, stride=HELD), :] = blank
    grid[...] = jnp.zeros_like(grid)
    to_scalars.wait()

    def put(source, _):
        for stick in range(STICK_LIMIT):
            grid[pl.ds(ids[source, stick], 1), :] = columns[source, stick : stick + 1, :]
        return 0

    lax.fori_loop(0, 16, put, 0, unroll=16)
    lower = lax.broadcasted_iota(jnp.int32, (96, 128), 1) < 64

    def place(pair, _):
        rows = grid[pl.ds(pl.multiple_of(pair * 128, 128), 128), :].T[:96]
        high = rows.astype(jnp.bfloat16).astype(jnp.float32)
        low = pltpu.roll(rows - high, 64, 1)
        for half in range(2):
            mixed = jnp.where(lower, low, high) if half else jnp.where(lower, high, low)
            both = jnp.concatenate([mixed, high], 1).astype(jnp.bfloat16)
            out = mm(both, inv_y[half])
            rows_to = pl.ds(pair * 2 + half, 48, stride=HELD)
            held_re[rows_to, :] = out[:48, :128] - out[48:, 128:]
            held_im[rows_to, :] = out[48:, :128] + out[:48, 128:]
        return 0

    lax.fori_loop(0, 25, place, 0, unroll=25)
    def waves(plane, _):
        even = jnp.zeros((FOLD, 128), jnp.float32)
        odd = jnp.zeros((FOLD, 128), jnp.float32)
        for band in range(4):
            start = pl.multiple_of((band * PLANES + plane) * HELD, HELD)
            rows = pl.ds(start, 64)
            high, low = halves(jnp.concatenate([held_re[rows, :], held_im[rows, :]], 1))
            out = mm(inv_x[...], jnp.concatenate([high, low, high], 0))
            cos_re, cos_im = out[:FOLD, :128], out[:FOLD, 128:]
            sin_re, sin_im = out[FOLD:, :128], out[FOLD:, 128:]
            sums = cos_re * cos_re + cos_im * cos_im + (sin_re * sin_re + sin_im * sin_im)
            even = even + (2.0 * factors[band]) * sums
            odd = odd + (4.0 * factors[band]) * (cos_im * sin_re - cos_re * sin_im)
        start = pl.multiple_of(plane * 2 * FOLD, 2 * FOLD)
        density[pl.ds(start, 2 * FOLD), :] = jnp.concatenate([even, odd], 0)
        return 0

    lax.fori_loop(0, PLANES, waves, 0, unroll=12)

    def forward(group, _):
        start = pl.multiple_of(group * 8 * FOLD, 8 * FOLD)
        high, low = halves(density[pl.ds(start, 8 * FOLD), :])
        rows = mm(jnp.concatenate([high, low], 1), fwd_y1[...]) + mm(high, fwd_y2[...])
        high, low = halves(rows)
        for pair in range(2):
            middle = (4 * pair + 2) * FOLD
            first, second = slice(middle - 2 * FOLD, middle), slice(middle, middle + 2 * FOLD)
            wide_high = jnp.concatenate([high[first], high[second]], 1)
            wide_low = jnp.concatenate([low[first], low[second]], 1)
            out = mm(fwd_x[...], jnp.concatenate([wide_high, wide_low, wide_high], 0))
            for member in range(2):
                plane = group * 4 + pair * 2 + member
                lanes = slice(member * 128, member * 128 + 128)
                cosine = pl.ds(plane, SLOTS, stride=12)
                sine = pl.ds(plane + SIDE_ROWS, SLOTS, stride=12)
                own[cosine, :] = out[0:SLOTS, lanes]
                own[sine, :] = out[32 : 32 + SLOTS, lanes]
                other[cosine, :] = out[64 : 64 + SLOTS, lanes]
                other[sine, :] = out[96 : 96 + SLOTS, lanes]
        return 0

    lax.fori_loop(0, 3, forward, 0, unroll=3)


def force_kernel(
    gx2, own, arrived, base, wave_z, atom_z, near_z, x_all, y_cos, y_sin, strength, out, acc, turn
):
    acc[...] = jnp.zeros_like(acc)
    turn[...] = x_all[...]

    def step(slot, reach, phases):
        first = slice(slot * PLANES, slot * PLANES + PLANES)
        second = slice(SIDE_ROWS + slot * PLANES, SIDE_ROWS + slot * PLANES + PLANES)
        pair = [own[first, :] + arrived[first, :], own[second, :] + arrived[second, :]]
        pair = jnp.concatenate([jnp.concatenate(pair, 1), jnp.zeros((4, 256), jnp.float32)], 0)
        high, low = halves(pair)
        waves = wave_z[...]
        if reach < ZSPAN:
            waves = jnp.concatenate([waves[:reach], waves[ZSPAN : ZSPAN + reach]], 0)
        raw = mm(waves, jnp.concatenate([high, low, high], 0))
        weight = 1.0 / (base[:reach] + gx2[slot])
        weight = jnp.concatenate([weight, weight], 1)
        weight = jnp.concatenate([weight, weight], 0)
        high, low = halves(raw * weight)
        both = mm(phases[...], jnp.concatenate([high, low, high], 0))
        table = turn[...]
        xc_c, xc_s = table[:, 0:1], table[:, 32:33]
        xs_c, xs_s = table[:, 64:65], table[:, 96:97]
        plain_c, plain_s = both[:128, :128], both[:128, 128:]
        acc[0] += xs_c * plain_c + xs_s * plain_s
        acc[1] += xc_c * plain_c + xc_s * plain_s
        acc[2] += xc_c * both[128:, :128] + xc_s * both[128:, 128:]
        turn[...] = pltpu.roll(table, 127, 1)
        return 0

    for slot in range(SLOTS):
        step(slot, *((ZSPAN, atom_z) if slot < 14 else (NEAR, near_z)))
    parts = [acc[0] * y_cos[...], acc[1] * y_sin[...], acc[2] * y_cos[...]]
    rows = [-strength[...] * jnp.sum(part.T, axis=0, keepdims=True) for part in parts]
    block = jnp.concatenate(rows, 0)
    for index in range(16):
        out[index] = block


def shards(
    coefficients, occupation, kpoint_weight, stick_cell, species, positions, amplitude, core_width
):
    payload = pl.pallas_call(
        send_kernel,
        out_shape=jax.ShapeDtypeStruct((16, ROWS, LANES), jnp.float32),
        in_specs=[HBM] * 3,
        out_specs=HBM,
        scratch_shapes=[
            pltpu.VMEM((1, 144), jnp.int32),
            pltpu.VMEM((4, 2, 13824), jnp.float32),
            pltpu.VMEM((384, 256), jnp.bfloat16),
            pltpu.VMEM((4, 384, LANES), jnp.float32),
            pltpu.VMEM((4, 288, LANES), jnp.float32),
            pltpu.VMEM((4, 3, 80, LANES), jnp.float32),
            pltpu.VMEM((16, ROWS, LANES), jnp.float32),
            pltpu.SemaphoreType.DMA((6,)),
            pltpu.SemaphoreType.DMA((16,)),
        ],
        compiler_params=pltpu.CompilerParams(vmem_limit_bytes=60 * 1024 * 1024),
        name="sticks",
    )(stick_cell[None], coefficients, z_table())
    received = lax.all_to_all(payload, AXES, 0, 0, axis_index_groups=exchange_groups(), tiled=True)
    received = received.reshape(16 * ROWS, LANES)

    core = lax.axis_index("band") % 2
    pool_weight = lax.dynamic_index_in_dim(
        kpoint_weight, lax.axis_index("pool"), keepdims=False
    ).astype(jnp.float32) / jnp.sum(kpoint_weight).astype(jnp.float32)
    factors = pool_weight * occupation[0] * (16.0 / NGRID / 32.0 / NGRID)
    fwd_y1, fwd_y2 = forward_y_tables()
    fwd_x = lax.dynamic_index_in_dim(jnp.asarray(forward_x_tables()), core, keepdims=False)
    halves_shape = jax.ShapeDtypeStruct((2 * SIDE_ROWS, 128), jnp.float32)
    own, other = pl.pallas_call(
        density_kernel,
        out_shape=(halves_shape, halves_shape),
        in_specs=[SMEM] + [VMEM] * 6,
        out_specs=(VMEM, VMEM),
        scratch_shapes=[
            pltpu.VMEM((16, LANES, LANES), jnp.float32),
            pltpu.VMEM((50 * 64, LANES), jnp.float32),
            pltpu.VMEM((48 * HELD, LANES), jnp.float32),
            pltpu.VMEM((48 * HELD, LANES), jnp.float32),
            pltpu.VMEM((PLANES * 2 * FOLD, LANES), jnp.float32),
            pltpu.VMEM((16, LANES), jnp.int32),
            pltpu.SMEM((16, LANES), jnp.int32),
            pltpu.SemaphoreType.DMA,
        ],
        compiler_params=pltpu.CompilerParams(vmem_limit_bytes=40 * 1024 * 1024),
        name="density",
    )(factors, received, inverse_y_tables(), inverse_x_table(), fwd_y1, fwd_y2, fwd_x)
    swap = [(index, index ^ 1) for index in range(8)]
    arrived = lax.ppermute(other, "band", swap)

    rank_z, rank_y = lax.axis_index("fft") // 2, lax.axis_index("fft") % 2
    start = (rank_y * 8 + rank_z) * PLANES
    steps = (jnp.arange(ZSPAN)[:, None] * (start + jnp.arange(PLANES))[None, :]) % NZ
    angles = 2.0 * math.pi / NZ * steps.astype(jnp.float32)
    turned = jnp.pad(jnp.concatenate([jnp.cos(angles), jnp.sin(angles)], 0), ((0, 0), (0, 4)))
    high, low = table_halves(turned)
    wave_z = jnp.concatenate([high, high, low], 1)
    kinds = species[None, :] == jnp.arange(3, dtype=jnp.int32)[:, None]
    width = jnp.sum(jnp.where(kinds, core_width[:, None], 0.0), axis=0)
    strength = jnp.sum(jnp.where(kinds, amplitude[:, None], 0.0), axis=0)

    def tables(where, order, unit, counts):
        waves = unit * order
        turns = where[:, None] * order[None, :]
        phase = 2.0 * math.pi * (turns - jnp.round(turns))
        scale = counts[None, :] * jnp.exp(-0.5 * (width * width)[:, None] * (waves * waves)[None])
        cosine, sine = scale * jnp.cos(phase), scale * jnp.sin(phase)
        slope = waves[None, :]
        return cosine, sine, slope * sine, -slope * cosine

    hx = 2.0 * jnp.arange(32, dtype=jnp.float32) + core.astype(jnp.float32)
    unit = 2.0 * math.pi / 96
    count_x = jnp.where(hx > 48.0, 0.0, jnp.where((hx == 0.0) | (hx == 48.0), 1.0, 2.0))
    x_all = jnp.concatenate(tables(positions[0], hx, unit, count_x), 1)
    hy = jnp.arange(64, dtype=jnp.float32)
    count_y = jnp.where(hy > 48.0, 0.0, jnp.where((hy == 0.0) | (hy == 48.0), 1.0, 2.0))
    y_parts = tables(positions[1], hy, unit, count_y)
    y_cos = jnp.concatenate(y_parts[:2], 1)
    y_sin = jnp.concatenate(y_parts[2:], 1)
    hz = jnp.arange(ZSPAN, dtype=jnp.float32)
    z_parts = tables(positions[2], hz, 2.0 * math.pi / NZ, jnp.where(hz == 0.0, 1.0, 2.0))

    def atom_table(reach):
        plain = jnp.concatenate([part[:, :reach] for part in z_parts[:2]], 1)
        sloped = jnp.concatenate([part[:, :reach] for part in z_parts[2:]], 1)
        high, low = table_halves(jnp.concatenate([plain, sloped], 0))
        return jnp.concatenate([high, high, low], 1)

    gy = np.tile(2.0 * np.pi / 96 * np.arange(64), 2)
    gz = 2.0 * np.pi / NZ * np.arange(ZSPAN)
    base = (gy[None, :] ** 2 + gz[:, None] ** 2 + screen).astype(np.float32)
    gx2 = (unit * hx) * (unit * hx)
    spread = pl.pallas_call(
        force_kernel,
        out_shape=jax.ShapeDtypeStruct((16, 3, LANES), jnp.float32),
        in_specs=[SMEM] + [VMEM] * 10,
        out_specs=VMEM,
        scratch_shapes=[
            pltpu.VMEM((3, 128, 128), jnp.float32),
            pltpu.VMEM((128, 128), jnp.float32),
        ],
        compiler_params=pltpu.CompilerParams(vmem_limit_bytes=40 * 1024 * 1024),
        name="force",
    )(
        gx2,
        own,
        arrived,
        base,
        wave_z,
        atom_table(ZSPAN),
        atom_table(NEAR),
        x_all,
        y_cos,
        y_sin,
        strength[None],
    )
    along, across = reduce_groups()
    total = jnp.sum(lax.all_to_all(spread, AXES, 0, 0, axis_index_groups=across, tiled=True), axis=0)
    spread = jnp.broadcast_to(total[None], (16, 3, LANES))
    return jnp.sum(lax.all_to_all(spread, AXES, 0, 0, axis_index_groups=along, tiled=True), axis=0)


def solution(mesh):
    placed = (P("pool", "band", None, "fft"), P("pool", "band"), P(), P("fft"), P(), P(), P(), P())
    return jax.shard_map(shards, mesh=mesh, in_specs=placed, out_specs=P(), check_vma=False)
```
